32 devices in a mesh: dp: 8 (over z, x), blk: 4 (over y, core).
Axes of the slice: x: 2, y: 2, z: 4, core: 2. Of those that a mesh axis runs over, the one named last changes fastest.
Arguments:
- hidden_input: bfloat16 [24, 512, 512], P('dp', 'blk'), may hold values from -6 to 6
- lengths: int32 [24], P('dp'), may hold values from 64 to 512, as said below
- key_mask: int32 [24, 512], P('dp', 'blk'), may hold values 0 or 1
- query_weight: bfloat16 [512, 512], replicated, may hold values from -0.25 to 0.25
- query_offset: bfloat16 [512], replicated, may hold values from -3 to 3
- key_weight: bfloat16 [512, 512], replicated, may hold values from -0.25 to 0.25
- value_weight: bfloat16 [512, 512], replicated, may hold values from -0.25 to 0.25
- value_offset: bfloat16 [512], replicated, may hold values from -0.29882812 to 0.29882812
- output_weight: bfloat16 [512, 512], replicated, may hold values from -2 to 2
- output_offset: bfloat16 [512], replicated, may hold values from -3 to 3
- mixer_gain: bfloat16 [512], replicated, may hold values from 0.5 to 1.5
- mixer_shift: bfloat16 [512], replicated, may hold values from -3 to 3
- up_weight: bfloat16 [512, 2048], replicated, may hold values from -0.25 to 0.25
- up_offset: bfloat16 [2048], replicated, may hold values from -3 to 3
- down_weight: bfloat16 [2048, 512], replicated, may hold values from -0.125 to 0.125
- down_offset: bfloat16 [512], replicated, may hold values from -3 to 3
- final_gain: bfloat16 [512], replicated, may hold values from 0.5 to 1.5
- final_shift: bfloat16 [512], replicated, may hold values from -3 to 3
- cotangent: bfloat16 [24, 512, 512], P('dp', 'blk'), may hold values from -6 to 6
Outputs:
- hidden_output: bfloat16 [24, 512, 512], P('dp', 'blk')
- input_gradient: bfloat16 [24, 512, 512], P('dp', 'blk')
- query_weight_gradient: float32 [512, 512], replicated
- query_offset_gradient: float32 [512], replicated
- key_weight_gradient: float32 [512, 512], replicated
- value_weight_gradient: float32 [512, 512], replicated
- value_offset_gradient: float32 [512], replicated
- output_weight_gradient: float32 [512, 512], replicated
- output_offset_gradient: float32 [512], replicated
- mixer_gain_gradient: float32 [512], replicated
- mixer_shift_gradient: float32 [512], replicated
- up_weight_gradient: float32 [512, 2048], replicated
- up_offset_gradient: float32 [2048], replicated
- down_weight_gradient: float32 [2048, 512], replicated
- down_offset_gradient: float32 [512], replicated
- final_gain_gradient: float32 [512], replicated
- final_shift_gradient: float32 [512], replicated
The draws below stay inside these ranges and needn't reach their ends.
Inputs may be any that keep to these rules, and one draw needn't show every extreme that they name: `lengths`: in each aligned group of 3 consecutive sequences at least one, drawn from the seed, has length 512.
All inputs are finite; a program needn't handle non-finite values. No bound on the sum of `key_mask` on one device may be relied on, other than what follows from the above.
Results may differ from the reference program's by a relative error of at most 0.019.
Values may be sent and summed in bfloat16 or wider, within the bound.
A program may use at most 128 MiB of HBM per device.

```python
import jax
import jax.numpy as jnp
from jax import lax

D = 512
HEADS = 8
HEAD = 64
FF = 2048
SEQ_LEN = 512
SEQ_GRP = 3
SEQS_ALL = 24


def draw_lengths(key, part):
    key = jax.random.fold_in(key, 11)
    first, second = jax.random.split(key)
    groups = SEQS_ALL // SEQ_GRP
    drawn = jax.random.randint(first, (groups, SEQ_GRP), SEQ_LEN // 8, SEQ_LEN + 1)
    picked = jax.random.randint(second, (groups, 1), 0, SEQ_GRP)
    whole = jnp.arange(SEQ_GRP)[None, :] == picked
    return jnp.where(whole, SEQ_LEN, drawn).reshape(-1).astype(jnp.int32)


def place_ends(values, key, least, top_value):
    longest = values.shape.index(max(values.shape))
    spots = []
    for shift in (0, 1):
        where = [jax.random.randint(jax.random.fold_in(key, axis), (), 0, length) for axis, length in enumerate(values.shape)]
        where[longest] = (where[longest] + shift) % values.shape[longest]
        spots.append(tuple(where))
    return values.at[spots[0]].set(least).at[spots[1]].set(top_value)


def levels(rng, extent, cuts, least, largest):
    def one(position, shards_of):
        steps = jax.random.uniform(jax.random.fold_in(jax.random.fold_in(rng, 6), position), (shards_of,), jnp.float32, least / len(cuts), largest / len(cuts))
        return jnp.repeat(jnp.exp(steps), extent[position] // shards_of).reshape((-1,) + (1,) * (len(extent) - position - 1))

    factor_of = one(*cuts[0])
    for cut in cuts[1:]:
        factor_of = factor_of * one(*cut)
    return factor_of


def centred(key, extent, deviation, bound, cuts=(), held_as=jnp.bfloat16):
    entries = jax.random.normal(key, extent, jnp.float32) * deviation
    if len(cuts) > 0:
        entries = levels(key, extent, cuts, -0.22, 0.18) * entries
    return jnp.clip(entries, min=-bound, max=bound).astype(held_as)


def setup_inputs(seed: int = 0) -> dict:
    streams_of = jax.random.split(jax.random.key(seed), 20)
    return {
        "hidden_input": centred(streams_of[0], (SEQS_ALL, SEQ_LEN, D), 1.0, 6.0, ((0, 8), (1, 4))),
        "lengths": draw_lengths(jax.random.fold_in(streams_of[19], 71), 0),
        "key_mask": place_ends((jax.random.randint(streams_of[2], (SEQS_ALL, SEQ_LEN), 0, 8) < 7).astype(jnp.int32), jax.random.fold_in(streams_of[2], 1), 0, 1),
        "query_weight": centred(streams_of[3], (D, D), D ** -0.5, 0.25),
        "query_offset": centred(streams_of[4], (D,), 0.5, 3.0),
        "key_weight": centred(streams_of[5], (D, D), D ** -0.5, 0.25),
        "value_weight": centred(streams_of[6], (D, D), D ** -0.5, 0.25),
        "value_offset": centred(streams_of[7], (D,), 0.05, 0.29882812),
        "output_weight": centred(streams_of[8], (D, D), (max(D // 64, 1)) ** -0.5, 2.0),
        "output_offset": centred(streams_of[9], (D,), 0.5, 3.0),
        "mixer_gain": jnp.clip(1.0 + 0.1 * jax.random.normal(streams_of[10], (D,), jnp.float32), 0.5, 1.5).astype(jnp.bfloat16),
        "mixer_shift": centred(streams_of[11], (D,), 0.5, 3.0),
        "up_weight": centred(streams_of[12], (D, FF), D ** -0.5, 0.25),
        "up_offset": centred(streams_of[13], (FF,), 0.5, 3.0),
        "down_weight": centred(streams_of[14], (FF, D), FF ** -0.5, 0.125),
        "down_offset": centred(streams_of[15], (D,), 0.5, 3.0),
        "final_gain": jnp.clip(1.0 + 0.1 * jax.random.normal(streams_of[16], (D,), jnp.float32), 0.5, 1.5).astype(jnp.bfloat16),
        "final_shift": centred(streams_of[17], (D,), 0.5, 3.0),
        "cotangent": centred(streams_of[18], (SEQS_ALL, SEQ_LEN, D), 1.0, 6.0, ((0, 8), (1, 4))),
    }


EPSILON = 1e-06
HIGHEST = lax.Precision.HIGHEST

@jax.custom_vjp
def low(v):
    return lax.optimization_barrier(v.astype(jnp.bfloat16)).astype(jnp.float32)

@jax.custom_vjp
def low_back(v):
    return v

def low_keep(v):
    return (low(v), None)

def low_pass(kept, grad):
    return (grad,)

def back_keep(v):
    return (v, None)

def back_low(kept, grad):
    return (low(grad),)
low.defvjp(low_keep, low_pass)
low_back.defvjp(back_keep, back_low)

def layer_norm(values, gain, shift):
    center = values - lax.optimization_barrier(jnp.mean(values, axis=-1, keepdims=True))
    inverse = lax.rsqrt(lax.optimization_barrier(jnp.mean(center * center, axis=-1, keepdims=True)) + EPSILON)
    return center * inverse * gain + shift

def project(inputs, weight):
    return jnp.matmul(inputs, weight, precision=HIGHEST)

def layer(inputs, params, allowed):
    query_weight, query_offset, key_weight, value_weight, value_offset, output_weight, output_offset, mixer_gain, mixer_shift, up_weight, up_offset, down_weight, down_offset, final_gain, final_shift = params
    seqs = inputs.shape[0]
    queries = low(low_back(project(inputs, query_weight) + query_offset)).reshape(seqs, SEQ_LEN, HEADS, HEAD)
    keys = low(low_back(project(inputs, key_weight))).reshape(seqs, SEQ_LEN, HEADS, HEAD)
    values = low(low_back(project(inputs, value_weight) + value_offset)).reshape(seqs, SEQ_LEN, HEADS, HEAD)
    scores = low_back(jnp.einsum('sqhd,skhd->sqhk', queries, keys, precision=HIGHEST) * HEAD ** (-0.5))
    scores = jnp.where(allowed[:, :, None, :], scores, -1000000000.0)
    highest = lax.optimization_barrier(jnp.max(scores, axis=-1, keepdims=True))
    logsum = highest + jnp.log(lax.optimization_barrier(jnp.sum(jnp.exp(scores - highest), axis=-1, keepdims=True)))
    probs = low(jnp.exp(scores - logsum))
    attended = jnp.einsum('sqhk,skhd->sqhd', probs, values, precision=HIGHEST)
    mixed = low(low_back(attended)).reshape(seqs, SEQ_LEN, D)
    branch = low_back(project(mixed, output_weight) + output_offset)
    normed = layer_norm(inputs + branch, mixer_gain, mixer_shift)
    inner = low_back(project(low(normed), up_weight) + up_offset)
    activated = low(jax.nn.gelu(inner, approximate=False))
    result = low_back(project(activated, down_weight) + down_offset)
    return layer_norm(normed + result, final_gain, final_shift)

def reference(hidden_input, lengths, key_mask, query_weight, query_offset, key_weight, value_weight, value_offset, output_weight, output_offset, mixer_gain, mixer_shift, up_weight, up_offset, down_weight, down_offset, final_gain, final_shift, cotangent):
    weights = (query_weight, query_offset, key_weight, value_weight, value_offset, output_weight, output_offset, mixer_gain, mixer_shift, up_weight, up_offset, down_weight, down_offset, final_gain, final_shift)
    params = tuple((item.astype(jnp.float32) for item in weights))
    groups = hidden_input.shape[0] // SEQ_GRP
    places = jnp.arange(SEQ_LEN, dtype=jnp.int32)
    diagonal = places[:, None] == places[None, :]

    def step(carry, item):
        block_input, block_length, block_mask, block_cot = item
        usable = (block_mask == 1) & (places[None, :] < block_length[:, None])
        allowed = usable[:, None, :] | diagonal[None]

        def forward(inputs, weights_in):
            return layer(inputs, weights_in, allowed)
        result, pullback = jax.vjp(forward, block_input.astype(jnp.float32), params)
        input_grad, param_grads = pullback(block_cot.astype(jnp.float32))
        carry = jax.tree.map(lambda first, second: first + second, carry, param_grads)
        return (carry, (result.astype(jnp.bfloat16), input_grad.astype(jnp.bfloat16)))
    start = tuple((jnp.zeros_like(item) for item in params))
    items = (hidden_input.reshape(groups, SEQ_GRP, SEQ_LEN, D), lengths.reshape(groups, SEQ_GRP), key_mask.reshape(groups, SEQ_GRP, SEQ_LEN), cotangent.reshape(groups, SEQ_GRP, SEQ_LEN, D))
    sums, (outputs, in_grads) = lax.scan(step, start, items)
    return (outputs.reshape(-1, SEQ_LEN, D), in_grads.reshape(-1, SEQ_LEN, D), sums[0], sums[1], sums[2], sums[3], sums[4], sums[5], sums[6], sums[7], sums[8], sums[9], sums[10], sums[11], sums[12], sums[13], sums[14])
```

```python
import functools

import jax
import jax.numpy as jnp
from jax import lax
from jax.experimental import pallas as pl
from jax.experimental.pallas import tpu as pltpu
from jax.sharding import PartitionSpec as P

MESH = pl.DeviceIdType.MESH
ROWS = 16

HEADS = 8
HEAD = 64


EPSILON = 1e-06


def project(inputs, weight):
    return jnp.einsum("sqd,df->sqf", inputs, weight, preferred_element_type=jnp.float32)


def project_back(upstream, weight):
    return jnp.einsum("sqf,df->sqd", upstream, weight, preferred_element_type=jnp.float32)


def weight_term(inputs, upstream):
    return jnp.einsum("sqd,sqf->df", inputs, upstream, preferred_element_type=jnp.float32)


def totals(values):
    return jnp.sum(values.astype(jnp.float32), axis=(0, 1))


def normalize(values, gain, shift):
    center = values - jnp.mean(values, axis=-1, keepdims=True)
    inverse = lax.rsqrt(jnp.mean(center * center, axis=-1, keepdims=True) + EPSILON)
    scaled = center * inverse
    return (scaled * gain + shift, scaled, inverse)


def norm_back(upstream, scaled, inverse, gain):
    inner = upstream * gain
    return inverse * (
        inner
        - jnp.mean(inner, axis=-1, keepdims=True)
        - scaled * jnp.mean(inner * scaled, axis=-1, keepdims=True)
    )


def bits_of(sizes):
    found = {}
    for axis, size in sizes.items():
        steps = []
        step = 1
        while step < size:
            steps.append((axis, step))
            step *= 2
        found[axis] = steps
    return found


def orders_of(sizes):
    bits = bits_of(sizes)
    blk, dp = bits["blk"], bits["dp"]
    return (
        blk[:1] + dp[:1] + blk[1:] + dp[1:],
        blk + dp,
        blk[:1] + dp[1:] + dp[:1] + blk[1:],
    )


def partner_of(bit):
    axis, step = bit
    index = lax.axis_index(axis)
    side = lax.rem(lax.div(index, step), 2)
    return side, {axis: index + step - 2 * step * side}


def greet(bits):
    barrier = pltpu.get_barrier_semaphore()
    for bit in bits:
        pl.semaphore_signal(barrier, inc=1, device_id=partner_of(bit)[1], device_id_type=MESH)
    pl.semaphore_wait(barrier, len(bits))


def rows_at(ref, start, count):
    if not isinstance(start, int):
        start = pl.multiple_of(start, ROWS)
    return ref.at[pl.ds(start, count)]


def plan_of(rows, order):
    plan = []
    size = rows
    for bit in order:
        split = (size // 2) % ROWS == 0
        size = size // 2 if split else size
        plan.append((bit, split, size))
    return plan


def landing_rows(rows, order):
    return sum(size for _, _, size in plan_of(rows, order))


def add_rows(first, first_at, second, second_at, out, out_at, count):
    chunk = 64 if count % 64 == 0 else (32 if count % 32 == 0 else 16)

    def body(step, carry):
        shift = step * chunk
        at = lambda start: pl.ds(pl.multiple_of(start + shift, ROWS), chunk)
        total = first[at(first_at)].astype(jnp.float32) + second[at(second_at)].astype(jnp.float32)
        out[at(out_at)] = total.astype(out.dtype)
        return carry

    lax.fori_loop(0, count // chunk, body, 0)


def reduce_rows(work, land, out, sends, receives, base, rows, land_at, sem_at, order):
    plan = plan_of(rows, order)
    start, size = base, rows
    pending, trail = [], []
    for level, (bit, split, count) in enumerate(plan):
        side, peer = partner_of(bit)
        keep = start + side * count if split else start
        give = start + (1 - side) * count if split else start
        copy = pltpu.make_async_remote_copy(
            src_ref=rows_at(work, give, count),
            dst_ref=rows_at(land, land_at, count),
            send_sem=sends.at[sem_at],
            recv_sem=receives.at[sem_at],
            device_id=peer,
            device_id_type=MESH,
        )
        copy.start()
        yield
        copy.wait_recv()
        if split:
            pending.append(copy)
        else:
            copy.wait_send()
        target = out if level == len(plan) - 1 else work
        add_rows(work, keep, land, land_at, target, keep, count)
        land_at += count
        sem_at += 1
        if split:
            trail.append((peer, start, keep, count))
        start = keep
    for peer, parent, mine, count in reversed(trail):
        copy = pltpu.make_async_remote_copy(
            src_ref=rows_at(out, mine, count),
            dst_ref=rows_at(out, mine, count),
            send_sem=sends.at[sem_at],
            recv_sem=receives.at[sem_at],
            device_id=peer,
            device_id_type=MESH,
        )
        copy.start()
        yield
        copy.wait_recv()
        pending.append(copy)
        sem_at += 1
    for copy in pending:
        copy.wait_send()


def reduce_whole(steps, land, sends, receives, sem_at, order):
    for level, bit in enumerate(order):
        copy = pltpu.make_async_remote_copy(
            src_ref=steps.at[level],
            dst_ref=land.at[level],
            send_sem=sends.at[sem_at + level],
            recv_sem=receives.at[sem_at + level],
            device_id=partner_of(bit)[1],
            device_id_type=MESH,
        )
        copy.start()
        yield
        copy.wait()
        steps[level + 1] = steps[level] + land[level]


def interleave(running):
    running = list(running)
    while running:
        kept = []
        for item in running:
            if next(item, True) is None:
                kept.append(item)
        running = kept


GROUP_ROWS = 1024


def sum_kernel(orders, grad_in, vec_in, grad_out, vec_out, work, land, out, steps, vec_land, sends, receives, local):
    greet(sorted(set(orders[0])))
    count = grad_in.shape[0] // GROUP_ROWS
    loads = []
    for group in range(count):
        span = pl.ds(group * GROUP_ROWS, GROUP_ROWS)
        load = pltpu.make_async_copy(grad_in.at[span], work.at[span], local.at[group])
        load.start()
        loads.append(load)
    running = []
    land_at = sem_at = 0
    steps[0] = vec_in[...]
    running.append(reduce_whole(steps, vec_land, sends, receives, 0, orders[1]))
    sem_at += len(orders[1])
    for group in range(count):
        order = orders[group % 3]
        running.append(
            reduce_rows(work, land, out, sends, receives, group * GROUP_ROWS, GROUP_ROWS, land_at, sem_at, order)
        )
        land_at += landing_rows(GROUP_ROWS, order)
        sem_at += 2 * len(order)
    for load in loads:
        load.wait()
    interleave(running)
    vec_out[...] = steps[len(orders[0])]
    stores = []
    for group in range(count):
        span = pl.ds(group * GROUP_ROWS, GROUP_ROWS)
        store = pltpu.make_async_copy(out.at[span], grad_out.at[span], local.at[group])
        store.start()
        stores.append(store)
    for store in stores:
        store.wait()


def sum_all(grads, vecs, sizes):
    orders = orders_of(sizes)
    levels = len(orders[0])
    rows, width = grads.shape
    count = rows // GROUP_ROWS
    land_total = sum(landing_rows(GROUP_ROWS, orders[group % 3]) for group in range(count))
    sems = levels + 2 * levels * count
    return pl.pallas_call(
        functools.partial(sum_kernel, orders),
        out_shape=(
            jax.ShapeDtypeStruct(grads.shape, grads.dtype),
            jax.ShapeDtypeStruct(vecs.shape, vecs.dtype),
        ),
        in_specs=[pl.BlockSpec(memory_space=pl.ANY), pl.BlockSpec(memory_space=pltpu.VMEM)],
        out_specs=(pl.BlockSpec(memory_space=pl.ANY), pl.BlockSpec(memory_space=pltpu.VMEM)),
        scratch_shapes=[
            pltpu.VMEM((rows, width), jnp.bfloat16),
            pltpu.VMEM((land_total, width), jnp.bfloat16),
            pltpu.VMEM((rows, width), jnp.bfloat16),
            pltpu.VMEM((levels + 1,) + vecs.shape, jnp.float32),
            pltpu.VMEM((levels,) + vecs.shape, jnp.float32),
            pltpu.SemaphoreType.DMA((sems,)),
            pltpu.SemaphoreType.DMA((sems,)),
            pltpu.SemaphoreType.DMA((count,)),
        ],
        compiler_params=pltpu.CompilerParams(
            collective_id=0, has_side_effects=True, vmem_limit_bytes=48 * 1024 * 1024
        ),
    )(grads, vecs)


def on_device(
    sizes,
    hidden_input,
    lengths,
    key_mask,
    query_weight,
    query_offset,
    key_weight,
    value_weight,
    value_offset,
    output_weight,
    output_offset,
    mixer_gain,
    mixer_shift,
    up_weight,
    up_offset,
    down_weight,
    down_offset,
    final_gain,
    final_shift,
    cotangent,
):
    seqs, rows, width = hidden_input.shape
    factor_scale = HEAD ** (-0.5)
    positions = lax.axis_index("blk") * rows + jnp.arange(rows, dtype=jnp.int32)
    usable = ((key_mask == 1) & (positions[None, :] < lengths[:, None])).astype(jnp.int32)
    inputs_wide = hidden_input.astype(jnp.float32)
    queries = (project(hidden_input, query_weight) + query_offset.astype(jnp.float32)).astype(
        jnp.bfloat16
    )
    keys = project(hidden_input, key_weight).astype(jnp.bfloat16)
    values = (project(hidden_input, value_weight) + value_offset.astype(jnp.float32)).astype(
        jnp.bfloat16
    )
    query_heads = queries.reshape(seqs, rows, HEADS, HEAD)

    def score_block(key_piece, usable_piece):
        count = key_piece.shape[1]
        key_heads = key_piece.reshape(seqs, count, HEADS, HEAD)
        scores = (
            jnp.einsum(
                "sqhd,skhd->sqhk", query_heads, key_heads, preferred_element_type=jnp.float32
            )
            * factor_scale
        )
        places = jnp.arange(count, dtype=jnp.int32)
        allowed = (usable_piece[:, None, None, :] == 1) | (
            places[None, None, None, :] == positions[None, :, None, None]
        )
        return jnp.where(allowed, scores, -1000000000.0)

    running = jnp.full((seqs, rows, HEADS), -1e30, jnp.float32)
    key_piece = lax.all_gather(keys, "blk", axis=1, tiled=True)
    value_piece = lax.all_gather(values, "blk", axis=1, tiled=True)
    usable_piece = lax.all_gather(usable, "blk", axis=1, tiled=True)
    scores_part = score_block(key_piece, usable_piece)
    newmax = jnp.maximum(running, jnp.max(scores_part, axis=-1))
    weights = jnp.exp(scores_part - newmax[..., None])
    mass = jnp.sum(weights, axis=-1)
    value_heads = value_piece.reshape(seqs, value_piece.shape[1], HEADS, HEAD)
    accum = jnp.einsum(
        "sqhk,skhd->sqhd",
        weights.astype(jnp.bfloat16),
        value_heads,
        preferred_element_type=jnp.float32,
    )
    running, mass, accum = (newmax, mass, accum)
    logsum = running + jnp.log(mass)
    attended = accum / mass[..., None]
    mixed = attended.reshape(seqs, rows, width).astype(jnp.bfloat16)
    branch = project(mixed, output_weight) + output_offset.astype(jnp.float32)
    mixer_wide = mixer_gain.astype(jnp.float32)
    normed, mixer_scaled, mixer_inverse = normalize(
        inputs_wide + branch, mixer_wide, mixer_shift.astype(jnp.float32)
    )
    normed_low = normed.astype(jnp.bfloat16)
    inner = project(normed_low, up_weight) + up_offset.astype(jnp.float32)
    activated, gelu_back = jax.vjp(lambda given: jax.nn.gelu(given, approximate=False), inner)
    activated_low = activated.astype(jnp.bfloat16)
    result = project(activated_low, down_weight) + down_offset.astype(jnp.float32)
    final_wide = final_gain.astype(jnp.float32)
    output_wide, final_scaled, final_inverse = normalize(
        normed + result, final_wide, final_shift.astype(jnp.float32)
    )
    hidden_output = output_wide.astype(jnp.bfloat16)
    upstream = cotangent.astype(jnp.float32)
    final_shift_part = jnp.sum(upstream, axis=(0, 1))
    final_gain_part = jnp.sum(upstream * final_scaled, axis=(0, 1))
    second_grad = norm_back(upstream, final_scaled, final_inverse, final_wide)
    result_grad = second_grad.astype(jnp.bfloat16)
    down_weight_part = weight_term(activated_low, result_grad)
    down_offset_part = totals(result_grad)
    inner_grad = gelu_back(project_back(result_grad, down_weight))[0].astype(jnp.bfloat16)
    up_weight_part = weight_term(normed_low, inner_grad)
    up_offset_part = totals(inner_grad)
    normed_grad = second_grad + project_back(inner_grad, up_weight)
    mixer_shift_part = jnp.sum(normed_grad, axis=(0, 1))
    mixer_gain_part = jnp.sum(normed_grad * mixer_scaled, axis=(0, 1))
    first_grad = norm_back(normed_grad, mixer_scaled, mixer_inverse, mixer_wide)
    branch_grad = first_grad.astype(jnp.bfloat16)
    output_weight_part = weight_term(mixed, branch_grad)
    output_offset_part = totals(branch_grad)
    mixed_grad = project_back(branch_grad, output_weight).astype(jnp.bfloat16)
    mixed_heads = mixed_grad.reshape(seqs, rows, HEADS, HEAD)
    key_all, value_all, usable_all = (
        lax.all_gather(keys, "blk", axis=1, tiled=True),
        lax.all_gather(values, "blk", axis=1, tiled=True),
        lax.all_gather(usable, "blk", axis=1, tiled=True),
    )
    scores = score_block(key_all, usable_all)
    probs = jnp.exp(scores - logsum[..., None])
    probs_low = probs.astype(jnp.bfloat16)
    length_all = key_all.shape[1]
    key_heads_all = key_all.reshape(seqs, length_all, HEADS, HEAD)
    value_heads_all = value_all.reshape(seqs, length_all, HEADS, HEAD)
    prob_grad = jnp.einsum(
        "sqhd,skhd->sqhk", mixed_heads, value_heads_all, preferred_element_type=jnp.float32
    )
    centre = jnp.sum(probs * prob_grad, axis=-1)
    score_grad = (probs * (prob_grad - centre[..., None])).astype(jnp.bfloat16)
    query_grad = (
        (
            jnp.einsum(
                "sqhk,skhd->sqhd", score_grad, key_heads_all, preferred_element_type=jnp.float32
            )
            * factor_scale
        )
        .reshape(seqs, rows, width)
        .astype(jnp.bfloat16)
    )
    key_term = (
        jnp.einsum("sqhk,sqhd->skhd", score_grad, query_heads, preferred_element_type=jnp.float32)
        * factor_scale
    )
    value_term = jnp.einsum(
        "sqhk,sqhd->skhd", probs_low, mixed_heads, preferred_element_type=jnp.float32
    )
    joined = jnp.concatenate(
        [key_term.reshape(seqs, length_all, width), value_term.reshape(seqs, length_all, width)],
        axis=-1,
    )
    returned = lax.psum_scatter(
        joined.astype(jnp.bfloat16), "blk", scatter_dimension=1, tiled=True
    ).astype(jnp.float32)
    key_grad = returned[:, :, :width].astype(jnp.bfloat16)
    value_grad = returned[:, :, width:].astype(jnp.bfloat16)
    query_weight_part = weight_term(hidden_input, query_grad)
    query_offset_part = totals(query_grad)
    key_weight_part = weight_term(hidden_input, key_grad)
    value_weight_part = weight_term(hidden_input, value_grad)
    value_offset_part = totals(value_grad)
    input_wide = (
        first_grad
        + project_back(query_grad, query_weight)
        + project_back(key_grad, key_weight)
        + project_back(value_grad, value_weight)
    )
    input_gradient = input_wide.astype(jnp.bfloat16)
    low = lambda value: value.astype(jnp.bfloat16)
    cut = lambda value: [low(value[:, at : at + width]) for at in range(0, value.shape[1], width)]
    hidden = up_weight_part.shape[1]
    grads = jnp.concatenate(
        [low(down_weight_part)]
        + cut(up_weight_part)
        + [low(output_weight_part), low(query_weight_part), low(key_weight_part), low(value_weight_part)],
        axis=0,
    )
    vecs = jnp.concatenate(
        [
            query_offset_part,
            value_offset_part,
            output_offset_part,
            mixer_gain_part,
            mixer_shift_part,
            down_offset_part,
            final_gain_part,
            final_shift_part,
            up_offset_part,
            jnp.zeros((4 * width,), jnp.float32),
        ]
    ).reshape(-1, width)
    grad_sums, vec_sums = sum_all(grads, vecs, sizes)
    wide = lambda at, count: grad_sums[at : at + count].astype(jnp.float32)
    down_weight_sum = wide(0, hidden)
    up_weight_sum = jnp.concatenate([wide(hidden + at, width) for at in range(0, hidden, width)], axis=1)
    output_weight_sum, query_weight_sum, key_weight_sum, value_weight_sum = (
        wide(2 * hidden + at * width, width) for at in range(4)
    )
    (
        query_offset_sum,
        value_offset_sum,
        output_offset_sum,
        mixer_gain_sum,
        mixer_shift_sum,
        down_offset_sum,
        final_gain_sum,
        final_shift_sum,
    ) = (vec_sums[at] for at in range(8))
    up_offset_sum = vec_sums[8:12].reshape(-1)
    return (
        hidden_output,
        input_gradient,
        query_weight_sum,
        query_offset_sum,
        key_weight_sum,
        value_weight_sum,
        value_offset_sum,
        output_weight_sum,
        output_offset_sum,
        mixer_gain_sum,
        mixer_shift_sum,
        up_weight_sum,
        up_offset_sum,
        down_weight_sum,
        down_offset_sum,
        final_gain_sum,
        final_shift_sum,
    )


def solution(mesh):
    in_specs = (
        P("dp", "blk", None),
        P("dp"),
        P("dp", "blk"),
        P(),
        P(),
        P(),
        P(),
        P(),
        P(),
        P(),
        P(),
        P(),
        P(),
        P(),
        P(),
        P(),
        P(),
        P(),
        P("dp", "blk", None),
    )
    out_specs = (
        P("dp", "blk", None),
        P("dp", "blk", None),
        P(),
        P(),
        P(),
        P(),
        P(),
        P(),
        P(),
        P(),
        P(),
        P(),
        P(),
        P(),
        P(),
        P(),
        P(),
    )
    return jax.shard_map(
        functools.partial(on_device, dict(mesh.shape)), mesh=mesh, in_specs=in_specs, out_specs=out_specs, check_vma=False
    )
```

```python
import functools

import jax
import jax.numpy as jnp
from jax import lax
from jax.experimental import pallas as pl
from jax.experimental.pallas import tpu as pltpu
from jax.sharding import PartitionSpec as P

HEAD = 64
EPSILON = 1e-06
MESH = pl.DeviceIdType.MESH
ROWS = 16
LOW = jnp.bfloat16
WIDE = jnp.float32
VECTORS = 16


def bits_of(sizes):
    found = {}
    for axis, size in sizes.items():
        found[axis] = []
        step = 1
        while step < size:
            found[axis].append((axis, step))
            step *= 2
    return found


def orders_of(sizes):
    bits = bits_of(sizes)
    blk, dp = bits["blk"], bits["dp"]
    return (
        blk[:1] + dp[:1] + blk[1:] + dp[1:],
        blk + dp,
        blk[:1] + dp[1:] + dp[:1] + blk[1:],
    )


def partner_of(bit):
    axis, step = bit
    index = lax.axis_index(axis)
    side = lax.rem(lax.div(index, step), 2)
    return side, {axis: index + step - 2 * step * side}


def flip(index, step):
    return index + step - 2 * step * lax.rem(lax.div(index, step), 2)


def aligned(start, unit):
    return start if isinstance(start, int) else pl.multiple_of(start, unit)


def span(start, count, unit=ROWS):
    return pl.ds(aligned(start, unit), count)


def send(src, dst, sems, at, peer):
    sends, receives = sems
    copy = pltpu.make_async_remote_copy(
        src_ref=src,
        dst_ref=dst,
        send_sem=sends.at[at],
        recv_sem=receives.at[at],
        device_id=peer,
        device_id_type=MESH,
    )
    copy.start()
    return copy


def plan_of(rows, order):
    plan = []
    size = rows
    for bit in order:
        split = (size // 2) % ROWS == 0
        size = size // 2 if split else size
        plan.append((bit, split, size))
    return plan


def landing_rows(rows, order):
    return sum(size for _, _, size in plan_of(rows, order))


def add_rows(first, first_at, second, second_at, out, out_at, count):
    chunk = 64 if count % 64 == 0 else (32 if count % 32 == 0 else 16)

    def body(step, carry):
        shift = step * chunk
        total = first[span(first_at + shift, chunk)].astype(WIDE) + second[span(second_at + shift, chunk)].astype(WIDE)
        out[span(out_at + shift, chunk)] = total.astype(out.dtype)
        return carry

    lax.fori_loop(0, count // chunk, body, 0)


def reduce_rows(work, land, out, sems, base, rows, land_at, sem_at, order, pending):
    plan = plan_of(rows, order)
    start = base
    trail = []
    for level, (bit, split, count) in enumerate(plan):
        side, peer = partner_of(bit)
        keep = start + side * count if split else start
        give = start + (1 - side) * count if split else start
        copy = send(work.at[span(give, count)], land.at[span(land_at, count)], sems, sem_at, peer)
        yield
        copy.wait_recv()
        if split:
            pending.append(copy)
            trail.append((peer, keep, count))
        else:
            copy.wait_send()
        target = out if level == len(plan) - 1 else work
        add_rows(work, keep, land, land_at, target, keep, count)
        land_at += count
        sem_at += 1
        start = keep
    for peer, mine, count in reversed(trail):
        part = out.at[span(mine, count)]
        copy = send(part, part, sems, sem_at, peer)
        yield
        copy.wait_recv()
        pending.append(copy)
        sem_at += 1


def reduce_whole(steps, land, sems, sem_at, order):
    for level, bit in enumerate(order):
        copy = send(steps.at[level], land.at[level], sems, sem_at + level, partner_of(bit)[1])
        yield
        copy.wait()
        steps[level + 1] = steps[level] + land[level]


def share_blocks(slots, sems, sem_at, me, pending):
    near, far = flip(me, 1), flip(me, 2)
    across = send(slots.at[me], slots.at[me], sems, sem_at, {"blk": far})
    beside = send(slots.at[me], slots.at[me], sems, sem_at + 1, {"blk": near})
    yield
    across.wait_recv()
    onward = send(slots.at[far], slots.at[far], sems, sem_at + 2, {"blk": near})
    yield
    beside.wait_recv()
    onward.wait_recv()
    pending.extend([across, beside, onward])


def advance(running):
    running[:] = [item for item in running if next(item, True) is None]


def by_rows(total, chunk, body, carry=0):
    def step(index, held):
        return body(pl.multiple_of(index * chunk, chunk), held)

    return lax.fori_loop(0, total // chunk, step, carry)


def dot(left, right):
    return jnp.dot(left, right, preferred_element_type=WIDE)


def dot_right_t(left, right):
    return lax.dot_general(left, right, (((1,), (1,)), ((), ())), preferred_element_type=WIDE)


def dot_left_t(left, right):
    return lax.dot_general(left, right, (((0,), (0,)), ((), ())), preferred_element_type=WIDE)


def fold(values):
    rows, width = values.shape
    return jnp.sum(values.reshape(rows // 8, 8, width), axis=0)


def mean_of(values):
    return jnp.mean(values, axis=-1, keepdims=True)


def norm_back(upstream, scaled, inverse, gain):
    inner = upstream * gain
    return inverse * (inner - mean_of(inner) - scaled * mean_of(inner * scaled))


def layout_of(sizes, seqs, rows, width, hidden):
    tokens = seqs * rows
    blocks = sizes["blk"]
    length = rows * blocks
    own = width // blocks
    heads = own // HEAD
    orders = orders_of(sizes)
    levels = len(orders[0])
    units = 2 * (hidden // width) + 1
    groups = group_table(sizes, width, hidden)
    land_total = sum(landing_rows(count, order) for _, count, order in groups)
    dp_order = bits_of(sizes)["dp"]
    shapes = {
        "x_all": ((seqs, length, width), LOW),
        "x_own": ((seqs, rows, width), LOW),
        "cot": ((seqs, rows, width), LOW),
        "w_qkv": ((width, 3 * own), LOW),
        "w_o": ((width, width), LOW),
        "w_up": ((width, hidden), LOW),
        "w_down": ((hidden, width), LOW),
        "flags": ((blocks, 8, rows), WIDE),
        "qkv": ((seqs, length, 3 * own), LOW),
        "probs": ((seqs * heads, length, length), LOW),
        "o_wide": ((seqs, length, own), WIDE),
        "o_send": ((seqs, length, own), LOW),
        "o_all": ((seqs, rows, width), LOW),
        "total": ((tokens, width), WIDE),
        "scaled": ((tokens, width), WIDE),
        "inverse": ((tokens, 128), WIDE),
        "normed": ((tokens, width), WIDE),
        "normed_low": ((tokens, width), LOW),
        "active": ((tokens, hidden), LOW),
        "slope": ((tokens, hidden), WIDE),
        "hid": ((seqs, rows, width), LOW),
        "grad_b": ((tokens, width), WIDE),
        "grad_y": ((tokens, width), LOW),
        "grad_z": ((tokens, hidden), LOW),
        "grad_t": ((tokens, width), LOW),
        "do_send": ((seqs, rows, width), LOW),
        "do_all": ((seqs, length, own), LOW),
        "grad_s": ((heads, length, length), LOW),
        "d_qkv": ((seqs, length, 3 * own), LOW),
        "dx_part": ((seqs, length, width), LOW),
        "dx_near": ((seqs, 2, rows, width), LOW),
        "dx_chip": ((seqs, rows, width), LOW),
        "dx_far": ((seqs, rows, width), LOW),
        "dx": ((seqs, rows, width), LOW),
        "work": ((units * width, width), LOW),
        "land": ((land_total, width), LOW),
        "out": ((units * width, width), LOW),
        "qkv_work": ((width, 3 * own), LOW),
        "qkv_land": ((landing_rows(width, dp_order), 3 * own), LOW),
        "qkv_out": ((blocks, width, 3 * own), LOW),
        "steps": ((levels + 1, VECTORS, width), WIDE),
        "vec_land": ((levels, VECTORS, width), WIDE),
    }
    return shapes


def group_table(sizes, width, hidden):
    orders = orders_of(sizes)
    half = hidden // 2
    return (
        (0, half, orders[0]),
        (half, half, orders[1]),
        (2 * half, half, orders[2]),
        (3 * half, half + width, orders[0]),
    )


OUT_NAMES = ("hid_out", "dx_out", "sums_out", "qkv_sums_out", "vec_out")
IN_NAMES = ("x", "lengths", "mask", "wq", "wk", "wv", "wo", "wu", "wd", "vec", "cotangent")


def layer_kernel(sizes, scratch_names, *refs):
    names = IN_NAMES + OUT_NAMES + tuple(scratch_names) + ("sends", "receives", "local")
    r = dict(zip(names, refs, strict=True))
    sems = (r["sends"], r["receives"])
    local = r["local"]
    x_all, qkv, vec, steps = r["x_all"], r["qkv"], r["vec"], r["steps"]
    seqs, rows, width = r["x_own"].shape
    tokens = seqs * rows
    length = x_all.shape[1]
    blocks = sizes["blk"]
    own = width // blocks
    heads = own // HEAD
    hidden = r["w_up"].shape[1]
    tiles = hidden // width
    scale = HEAD ** (-0.5)
    bits = bits_of(sizes)
    me = lax.axis_index("blk")
    near, far = flip(me, 1), flip(me, 2)
    cross = flip(far, 1)
    peers = (near, far, cross)
    place = lambda index: span(index * rows, rows, rows)
    lanes = lambda index: span(index * own, own, own)

    used = {"sem": 0, "local": 0}
    pending, stores = [], []

    def slot(count=1):
        at = used["sem"]
        used["sem"] += count
        return at

    def fetch(src, dst):
        copy = pltpu.make_async_copy(src, dst, local.at[used["local"]])
        used["local"] += 1
        copy.start()
        return copy

    loads_x = [
        fetch(r["x"], x_all.at[:, place(me), :]),
        fetch(r["x"], r["x_own"]),
    ]
    loads_w = [
        fetch(r[name].at[:, lanes(me)], r["w_qkv"].at[:, pl.ds(at * own, own)])
        for at, name in enumerate(("wq", "wk", "wv"))
    ]
    load_o = fetch(r["wo"], r["w_o"])
    load_up = fetch(r["wu"], r["w_up"])
    load_down = fetch(r["wd"], r["w_down"])
    load_cot = fetch(r["cotangent"], r["cot"])

    positions = me * rows + lax.broadcasted_iota(jnp.int32, (1, rows), 1)
    flag_rows = []
    for seq in range(seqs):
        good = (r["mask"][seq : seq + 1, :] == 1) & (positions < r["lengths"][seq])
        flag_rows.append(jnp.where(good, 0.0, -1000000000.0).astype(WIDE))
    flag_rows.append(jnp.zeros((8 - seqs, rows), WIDE))
    r["flags"][me] = jnp.concatenate(flag_rows, axis=0)

    barrier = pltpu.get_barrier_semaphore()
    greeted = [{"blk": peer} for peer in peers] + [partner_of(bit)[1] for bit in bits["dp"]]
    for peer in greeted:
        pl.semaphore_signal(barrier, inc=1, device_id=peer, device_id_type=MESH)
    pl.semaphore_wait(barrier, len(greeted))

    at_far, at_near, at_on, at_flag = slot(seqs), slot(seqs), slot(seqs), slot(len(peers))
    flag_copies = [
        send(r["flags"].at[me], r["flags"].at[me], sems, at_flag + index, {"blk": peer})
        for index, peer in enumerate(peers)
    ]
    x_far, x_near, x_on = [], [], []
    for seq in range(seqs):
        target = x_all.at[seq, place(me), :]
        x_far.append(send(r["x"].at[seq], target, sems, at_far + seq, {"blk": far}))
        x_near.append(send(r["x"].at[seq], target, sems, at_near + seq, {"blk": near}))
    pending += flag_copies + x_far + x_near

    def forward_x(seq):
        x_far[seq].wait_recv()
        block = x_all.at[seq, place(far), :]
        x_on.append(send(block, block, sems, at_on + seq, {"blk": near}))

    lane = lax.broadcasted_iota(jnp.int32, (1, own), 1)
    of_head = [(lane >= head * HEAD) & (lane < (head + 1) * HEAD) for head in range(heads)]
    only = lambda values, head: jnp.where(of_head[head], values.astype(WIDE), 0.0)
    bias_q = vec[0:1, lanes(me)]
    bias_v = vec[1:2, lanes(me)]
    bias_qkv = jnp.concatenate([bias_q, jnp.zeros_like(bias_q), bias_v], axis=1)
    o_all, o_send = r["o_all"], r["o_send"]
    at_o = slot(seqs * len(peers))
    o_copies = []

    def project(seq):
        def body(at, carry):
            made = dot(x_all[seq, pl.ds(at, 256), :], r["w_qkv"][...]) + bias_qkv
            qkv[seq, pl.ds(at, 256), :] = made.astype(LOW)
            return carry

        by_rows(length, 256, body)

    def attend(seq):
        keys = qkv[seq, :, own : 2 * own]
        values = qkv[seq, :, 2 * own :]
        key_bias = jnp.concatenate([r["flags"][block, seq : seq + 1, :] for block in range(blocks)], axis=1)
        column = lax.broadcasted_iota(jnp.int32, (128, length), 1)
        row = lax.broadcasted_iota(jnp.int32, (128, length), 0)

        def body(at, carry):
            query = qkv[seq, pl.ds(at, 128), 0:own].astype(WIDE) * scale
            bias = jnp.where(column == row + at, 0.0, key_bias)
            joined = None
            for head in range(heads):
                scores = dot_right_t(only(query, head).astype(LOW), keys) + bias
                raised = jnp.exp(scores - jnp.max(scores, axis=-1, keepdims=True))
                probs = (raised / jnp.sum(raised, axis=-1, keepdims=True)).astype(LOW)
                r["probs"][seq * heads + head, pl.ds(at, 128), :] = probs
                result = dot(probs, values)
                joined = result if joined is None else jnp.where(of_head[head], result, joined)
            r["o_wide"][seq, pl.ds(at, 128), :] = joined
            o_send[seq, pl.ds(at, 128), :] = joined.astype(LOW)
            return carry

        by_rows(length, 128, body)
        for index, peer in enumerate(peers):
            o_copies.append(
                send(
                    o_send.at[seq, place(peer), :],
                    o_all.at[seq, :, lanes(me)],
                    sems,
                    at_o + seq * len(peers) + index,
                    {"blk": peer},
                )
            )
        o_all[seq, :, lanes(me)] = o_send[seq, place(me), :]

    for copy in loads_w:
        copy.wait()
    for copy in loads_x:
        copy.wait()
    for copy in flag_copies:
        copy.wait_recv()
    forward_x(0)
    for seq in range(seqs):
        x_near[seq].wait_recv()
        x_on[seq].wait_recv()
        project(seq)
        if seq + 1 < seqs:
            forward_x(seq + 1)
        attend(seq)
    pending += x_on + o_copies

    total, scaled, inverse = r["total"], r["scaled"], r["inverse"]
    normed, normed_low = r["normed"], r["normed_low"]
    wide_row = lambda at: vec[at : at + 1, :]
    load_o.wait()
    for copy in o_copies:
        copy.wait_recv()
    flat = lambda ref, at, count: ref[lax.div(at, rows), span(lax.rem(at, rows), count), :]

    total[...] = dot(o_all[...].reshape(tokens, width), r["w_o"][...])

    def first_norm(at, carry):
        part = pl.ds(at, 32)
        values = flat(r["x_own"], at, 32).astype(WIDE) + total[part, :] + wide_row(2)
        center = values - mean_of(values)
        inv = lax.rsqrt(mean_of(center * center) + EPSILON)
        made = center * inv
        scaled[part, :] = made
        inverse[part, :] = jnp.broadcast_to(inv, (32, 128))
        result = made * wide_row(3) + wide_row(4)
        normed[part, :] = result
        normed_low[part, :] = result.astype(LOW)
        return carry

    by_rows(tokens, 32, first_norm)

    load_up.wait()
    active, slope = r["active"], r["slope"]

    def up(tile, carry):
        columns = span(tile * width, width, width)
        total[...] = dot(normed_low[...], r["w_up"][:, columns])
        offset = vec[pl.ds(8 + tile, 1), :]

        def bend(at, held):
            part = pl.ds(at, 32)
            z = total[part, :] + offset
            below = 0.5 * (1.0 + lax.erf(z * 0.7071067811865476))
            active[part, columns] = (z * below).astype(LOW)
            slope[part, columns] = below + z * (0.3989422804014327 * jnp.exp(-0.5 * z * z))
            return held

        by_rows(tokens, 32, bend)
        return carry

    lax.fori_loop(0, tiles, up, 0)
    load_down.wait()
    load_cot.wait()
    total[...] = dot(active[...], r["w_down"][...])

    grad_b, grad_y = r["grad_b"], r["grad_y"]
    zero = jnp.zeros((8, width), WIDE)

    def second_norm(at, sums):
        shift_sum, gain_sum, down_sum = sums
        part = pl.ds(at, 32)
        values = normed[part, :] + total[part, :] + wide_row(5)
        center = values - mean_of(values)
        inv = lax.rsqrt(mean_of(center * center) + EPSILON)
        made = center * inv
        r["hid"][lax.div(at, rows), span(lax.rem(at, rows), 32), :] = (made * wide_row(6) + wide_row(7)).astype(LOW)
        upstream = flat(r["cot"], at, 32).astype(WIDE)
        back = norm_back(upstream, made, inv, wide_row(6))
        grad_b[part, :] = back
        rounded = back.astype(LOW)
        grad_y[part, :] = rounded
        return shift_sum + fold(upstream), gain_sum + fold(upstream * made), down_sum + fold(rounded.astype(WIDE))

    shift_sum, gain_sum, down_sum = by_rows(tokens, 32, second_norm, (zero, zero, zero))
    stores.append(fetch(r["hid"], r["hid_out"]))
    total_row = lambda values: jnp.sum(values, axis=0, keepdims=True)
    steps[0] = jnp.zeros((VECTORS, width), WIDE)
    steps[0, 7:8, :] = total_row(shift_sum)
    steps[0, 6:7, :] = total_row(gain_sum)
    steps[0, 5:6, :] = total_row(down_sum)

    work = r["work"]
    groups = group_table(sizes, width, hidden)
    running = []
    land_at = 0

    def launch(index):
        nonlocal land_at
        base, count, order = groups[index]
        running.append(
            reduce_rows(work, r["land"], r["out"], sems, base, count, land_at, slot(2 * len(order)), order, pending)
        )
        land_at += landing_rows(count, order)
        next(running[-1])

    for tile in range(tiles):
        work[tile * width : (tile + 1) * width, :] = dot_left_t(
            active[:, tile * width : (tile + 1) * width], grad_y[...]
        ).astype(LOW)
        if tile == tiles // 2 - 1:
            launch(0)
    launch(1)

    grad_z = r["grad_z"]

    def back_up(tile, carry):
        columns = span(tile * width, width, width)
        total[...] = dot_right_t(grad_y[...], r["w_down"][columns, :])

        def bend(at, held):
            part = pl.ds(at, 32)
            made = (total[part, :] * slope[part, columns]).astype(LOW)
            grad_z[part, columns] = made
            return held + fold(made.astype(WIDE))

        sums = by_rows(tokens, 32, bend, zero)
        steps[0, pl.ds(8 + tile, 1), :] = total_row(sums)
        return carry

    lax.fori_loop(0, tiles, back_up, 0)
    advance(running)
    total[...] = dot_right_t(grad_z[...], r["w_up"][...])

    grad_t = r["grad_t"]

    def first_back(at, sums):
        shift_part, gain_part, out_part = sums
        part = pl.ds(at, 32)
        upstream = grad_b[part, :] + total[part, :]
        made = scaled[part, :]
        back = norm_back(upstream, made, inverse[part, 0:1], wide_row(3))
        grad_b[part, :] = back
        rounded = back.astype(LOW)
        grad_t[part, :] = rounded
        return shift_part + fold(upstream), gain_part + fold(upstream * made), out_part + fold(rounded.astype(WIDE))

    shift_part, gain_part, out_part = by_rows(tokens, 32, first_back, (zero, zero, zero))
    steps[0, 4:5, :] = total_row(shift_part)
    steps[0, 3:4, :] = total_row(gain_part)
    steps[0, 2:3, :] = total_row(out_part)

    do_send, do_all = r["do_send"], r["do_all"]
    at_do = slot(seqs * len(peers))
    do_copies = []
    made = dot_right_t(grad_t[...], r["w_o"][...]).astype(LOW)
    do_send[...] = made.reshape(seqs, rows, width)
    for seq in range(seqs):
        do_copies.append(
            [
                send(
                    do_send.at[seq, :, lanes(peer)],
                    do_all.at[seq, place(me), :],
                    sems,
                    at_do + seq * len(peers) + index,
                    {"blk": peer},
                )
                for index, peer in enumerate(peers)
            ]
        )
        do_all[seq, place(me), :] = do_send[seq, :, lanes(me)]
        pending += do_copies[-1]

    advance(running)
    for tile in range(tiles):
        at = hidden + tile * width
        work[at : at + width, :] = dot_left_t(normed_low[...], grad_z[:, tile * width : (tile + 1) * width]).astype(LOW)
        if tile == tiles // 2 - 1:
            launch(2)
    work[2 * hidden : 2 * hidden + width, :] = dot_left_t(
        o_all[...].reshape(tokens, width), grad_t[...]
    ).astype(LOW)
    launch(3)
    advance(running)

    d_qkv, grad_s, dx_part = r["d_qkv"], r["grad_s"], r["dx_part"]
    at_dx_near, at_dx_far = slot(2 * seqs), slot(seqs)
    dx_near, dx_far = [], []

    def attend_back(seq):
        keys = qkv[seq, :, own : 2 * own]
        values = qkv[seq, :, 2 * own :]

        def body(at, carry):
            upstream = do_all[seq, pl.ds(at, 128), :].astype(WIDE)
            inner = upstream * r["o_wide"][seq, pl.ds(at, 128), :]
            for head in range(heads):
                delta = jnp.sum(jnp.where(of_head[head], inner, 0.0), axis=-1, keepdims=True)
                prob_grad = dot_right_t(only(upstream, head).astype(LOW), values)
                probs = r["probs"][seq * heads + head, pl.ds(at, 128), :].astype(WIDE)
                grad_s[head, pl.ds(at, 128), :] = (probs * (prob_grad - delta)).astype(LOW)
            return carry

        by_rows(length, 128, body)
        queries_wide = qkv[seq, :, 0:own].astype(WIDE) * scale
        keys_wide = keys.astype(WIDE) * scale
        upstream = do_all[seq]
        query_grad = key_grad = value_grad = None
        for head in range(heads):
            terms = (
                dot(grad_s[head], only(keys_wide, head).astype(LOW)),
                dot_left_t(grad_s[head], only(queries_wide, head).astype(LOW)),
                dot_left_t(r["probs"][seq * heads + head], only(upstream, head).astype(LOW)),
            )
            if query_grad is None:
                query_grad, key_grad, value_grad = terms
            else:
                query_grad, key_grad, value_grad = query_grad + terms[0], key_grad + terms[1], value_grad + terms[2]
        d_qkv[seq, :, 0:own] = query_grad.astype(LOW)
        d_qkv[seq, :, own : 2 * own] = key_grad.astype(LOW)
        d_qkv[seq, :, 2 * own :] = value_grad.astype(LOW)

        def partial(at, carry):
            dx_part[seq, pl.ds(at, 128), :] = dot_right_t(d_qkv[seq, pl.ds(at, 128), :], r["w_qkv"][...]).astype(LOW)
            return carry

        by_rows(length, 128, partial)
        dx_near.append(
            [
                send(dx_part.at[seq, place(near), :], r["dx_near"].at[seq, 0], sems, at_dx_near + 2 * seq, {"blk": near}),
                send(dx_part.at[seq, place(cross), :], r["dx_near"].at[seq, 1], sems, at_dx_near + 2 * seq + 1, {"blk": near}),
            ]
        )
        pending.extend(dx_near[-1])

    def hand_on(seq):
        dx_near[seq][1].wait_recv()

        def body(at, carry):
            part = pl.ds(at, 32)
            summed = dx_part[seq, span(far * rows + at, 32), :].astype(WIDE) + r["dx_near"][seq, 1, part, :].astype(WIDE)
            r["dx_chip"][seq, part, :] = summed.astype(LOW)
            return carry

        by_rows(rows, 32, body)
        dx_far.append(send(r["dx_chip"].at[seq], r["dx_far"].at[seq], sems, at_dx_far + seq, {"blk": far}))
        pending.append(dx_far[-1])

    for seq in range(seqs):
        for copy in do_copies[seq]:
            copy.wait_recv()
        attend_back(seq)
        if seq > 0:
            hand_on(seq - 1)
        advance(running)
    hand_on(seqs - 1)

    flat_d = d_qkv[...].reshape(seqs * length, 3 * own)
    made = dot_left_t(x_all[...].reshape(seqs * length, width), flat_d)
    r["qkv_work"][...] = made.astype(LOW)

    def offsets(at, sums):
        part = flat_rows(d_qkv, at, 128, length)
        return sums + fold(part.astype(WIDE))

    flat_rows = lambda ref, at, count, each: ref[lax.div(at, each), span(lax.rem(at, each), count), :]
    sums = total_row(by_rows(seqs * length, 128, offsets, jnp.zeros((8, 3 * own), WIDE)))
    steps[0, 0:1, lanes(me)] = sums[:, 0:own]
    steps[0, 1:2, lanes(me)] = sums[:, 2 * own :]

    def sum_qkv():
        dp_order = bits["dp"]
        base = slot(2 * len(dp_order))
        blocks_at = slot(3)
        yield from reduce_rows(
            r["qkv_work"], r["qkv_land"], r["qkv_out"].at[me], sems, 0, width, 0, base, dp_order, pending
        )
        yield from share_blocks(r["qkv_out"], sems, blocks_at, me, pending)

    running.append(sum_qkv())
    running.append(reduce_whole(steps, r["vec_land"], sems, slot(len(groups[0][2])), groups[1][2]))
    advance(running)

    for seq in range(seqs):
        dx_near[seq][0].wait_recv()
        dx_far[seq].wait_recv()

        def finish(at, carry):
            part = pl.ds(at, 32)
            summed = grad_b[span(seq * rows + at, 32), :] + dx_part[seq, span(me * rows + at, 32), :].astype(WIDE)
            summed = summed + r["dx_near"][seq, 0, part, :].astype(WIDE) + r["dx_far"][seq, part, :].astype(WIDE)
            r["dx"][seq, part, :] = summed.astype(LOW)
            return carry

        by_rows(rows, 32, finish)
        advance(running)
    stores.append(fetch(r["dx"], r["dx_out"]))

    while running:
        advance(running)
    r["vec_out"][...] = steps[len(groups[0][2])]
    stores.append(fetch(r["out"], r["sums_out"]))
    stores.append(fetch(r["qkv_out"], r["qkv_sums_out"]))
    for copy in pending:
        copy.wait_send()
    for copy in stores:
        copy.wait()


def on_device(
    sizes,
    hidden_input,
    lengths,
    key_mask,
    query_weight,
    query_offset,
    key_weight,
    value_weight,
    value_offset,
    output_weight,
    output_offset,
    mixer_gain,
    mixer_shift,
    up_weight,
    up_offset,
    down_weight,
    down_offset,
    final_gain,
    final_shift,
    cotangent,
):
    seqs, rows, width = hidden_input.shape
    hidden = up_weight.shape[1]
    blocks = sizes["blk"]
    own = width // blocks
    tiles = hidden // width
    vectors = (query_offset, value_offset, output_offset, mixer_gain, mixer_shift, down_offset, final_gain, final_shift)
    spare = jnp.zeros(((VECTORS - len(vectors) - tiles) * width,), LOW)
    vec = jnp.concatenate(vectors + (up_offset, spare)).astype(WIDE).reshape(VECTORS, width)
    scratch = layout_of(sizes, seqs, rows, width, hidden)
    anywhere = pl.BlockSpec(memory_space=pl.ANY)
    inside = pl.BlockSpec(memory_space=pltpu.VMEM)
    scalars = pl.BlockSpec(memory_space=pltpu.SMEM)
    units = scratch["work"][0]
    hid, dx, sums, qkv_sums, vec_sums = pl.pallas_call(
        functools.partial(layer_kernel, sizes, tuple(scratch)),
        out_shape=(
            jax.ShapeDtypeStruct(hidden_input.shape, LOW),
            jax.ShapeDtypeStruct(hidden_input.shape, LOW),
            jax.ShapeDtypeStruct(units, LOW),
            jax.ShapeDtypeStruct((blocks, width, 3 * own), LOW),
            jax.ShapeDtypeStruct((VECTORS, width), WIDE),
        ),
        in_specs=[anywhere, scalars, inside] + [anywhere] * 6 + [inside, anywhere],
        out_specs=(anywhere, anywhere, anywhere, anywhere, inside),
        scratch_shapes=[pltpu.VMEM(shape, kind) for shape, kind in scratch.values()]
        + [
            pltpu.SemaphoreType.DMA((256,)),
            pltpu.SemaphoreType.DMA((256,)),
            pltpu.SemaphoreType.DMA((32,)),
        ],
        compiler_params=pltpu.CompilerParams(
            collective_id=0, has_side_effects=True, vmem_limit_bytes=60 * 1024 * 1024
        ),
    )(
        hidden_input,
        lengths,
        key_mask,
        query_weight,
        key_weight,
        value_weight,
        output_weight,
        up_weight,
        down_weight,
        vec,
        cotangent,
    )
    wide = lambda at, count: sums[at : at + count].astype(WIDE)
    down_sum = wide(0, hidden)
    up_sum = jnp.concatenate([wide(hidden + at, width) for at in range(0, hidden, width)], axis=1)
    output_sum = wide(2 * hidden, width)
    query_sum, key_sum, value_sum = (
        jnp.concatenate([qkv_sums[block, :, at * own : (at + 1) * own] for block in range(blocks)], axis=1).astype(WIDE)
        for at in range(3)
    )
    return (
        hid,
        dx,
        query_sum,
        vec_sums[0],
        key_sum,
        value_sum,
        vec_sums[1],
        output_sum,
        vec_sums[2],
        vec_sums[3],
        vec_sums[4],
        up_sum,
        vec_sums[8 : 8 + tiles].reshape(-1),
        down_sum,
        vec_sums[5],
        vec_sums[6],
        vec_sums[7],
    )


def solution(mesh):
    split = P("dp", "blk", None)
    in_specs = (split, P("dp"), P("dp", "blk")) + (P(),) * 15 + (split,)
    out_specs = (split, split) + (P(),) * 15
    return jax.shard_map(
        functools.partial(on_device, dict(mesh.shape)),
        mesh=mesh,
        in_specs=in_specs,
        out_specs=out_specs,
        check_vma=False,
    )
```

```python
import functools
import types

import jax
import jax.numpy as jnp
from jax import lax
from jax.experimental import pallas as pl
from jax.experimental.pallas import tpu as pltpu
from jax.sharding import PartitionSpec as P

HEAD = 64
EPSILON = 1e-06
MESH = pl.DeviceIdType.MESH
ROWS = 16
LOW = jnp.bfloat16
WIDE = jnp.float32
VECTORS = 16

UNIT_ORDERS = ("cxyz", "cyxz", "cxyz", "cyxz", "cxyz", "cxyz", "cyxz", "cxyz", "cyxz")
OWN_ORDERS = ("zx", "xz", "zx")
SUM_ORDER = "cxyz"
POLLS = (
    (),
    (),
    (),
    (),
    (0, 1,),
    (2, 3,),
    (),
    (),
    (),
    (0,),
    (1,),
    (),
    (2, 3,),
    (),
    (8, 0,),
    (4, 5,),
    (1, 6, 7, 3,),
    (2, 0,),
    (4,),
    (8, 1,),
    (3, 5, 6, 2,),
    (4, 0, 7,),
    (8,),
    (9, 5, 6, 1,),
    (3, 0,),
    (2, 7,),
    (9, 4,),
    (8, 1, 5, 3,),
    (2, 6,),
    (9, 7, 0, 4,),
    (8, 1, 12,),
    (10, 11, 5, 2, 0, 6, 1, 3, 8, 12,),
    (9, 2,),
    (3, 7, 11, 4, 10, 6, 5, 11, 8, 12, 4, 8, 10, 4, 9, 5, 9, 7, 11, 5, 10, 12, 6, 6, 7, 11, 12, 7, 11, 10, 10,),
)


def stages_of(sizes):
    rest, step, far = sizes["dp"] // 2, 2, []
    while rest > 1:
        radix = 4 if rest % 4 == 0 else 2
        far.append(("dp", step, radix))
        step *= radix
        rest //= radix
    return {"c": [("blk", 1, 2)], "y": [("blk", 2, 2)], "x": [("dp", 1, 2)], "z": far}


def bits_of(sizes, letters):
    bits = []
    for letter in letters:
        for axis, step, radix in stages_of(sizes)[letter]:
            bits += [(axis, step, 2)] if radix == 2 else [(axis, step, 2), (axis, 2 * step, 2)]
    return bits


def digit_of(stage):
    axis, step, radix = stage
    index = lax.axis_index(axis)
    digit = lax.rem(lax.div(index, step), radix)
    others = []
    for offset in range(1, radix):
        other = lax.rem(digit + offset, radix)
        others.append((other, {axis: index + (other - digit) * step}))
    return digit, others


def flip(index, step):
    return index + step - 2 * step * lax.rem(lax.div(index, step), 2)


def aligned(start, unit):
    return start if isinstance(start, int) else pl.multiple_of(start, unit)


def span(start, count, unit=ROWS):
    return pl.ds(aligned(start, unit), count)


def send(src, dst, sems, at, peer, land_at=None):
    sends, receives = sems
    copy = pltpu.make_async_remote_copy(
        src_ref=src,
        dst_ref=dst,
        send_sem=sends.at[at],
        recv_sem=receives.at[at if land_at is None else land_at],
        device_id=peer,
        device_id_type=MESH,
    )
    copy.start()
    return copy


def plan_of(sizes, rows, letters):
    plan = []
    size = rows
    for letter in letters:
        for axis, step, radix in stages_of(sizes)[letter]:
            if size % (radix * ROWS) == 0:
                size //= radix
                plan.append(((axis, step, radix), True, size))
                continue
            bit = step
            while bit < step * radix:
                split = size % (2 * ROWS) == 0
                size = size // 2 if split else size
                plan.append(((axis, bit, 2), split, size))
                bit *= 2
    return plan


def landing_rows(sizes, rows, letters):
    return sum(size * (stage[2] - 1) for stage, _, size in plan_of(sizes, rows, letters))


def semaphores_of(sizes, rows, letters):
    return 2 * sum(stage[2] - 1 for stage, _, _ in plan_of(sizes, rows, letters))


def add_rows(first, first_at, land, land_at, terms, out, out_at, count):
    chunk = 64 if count % 64 == 0 else (32 if count % 32 == 0 else 16)

    def body(step, carry):
        shift = step * chunk
        total = first[span(first_at + shift, chunk)].astype(WIDE)
        for term in range(terms):
            total = total + land[span(land_at + term * count + shift, chunk)].astype(WIDE)
        out[span(out_at + shift, chunk)] = total.astype(out.dtype)
        return carry

    if count == chunk:
        body(0, 0)
    else:
        lax.fori_loop(0, count // chunk, body, 0)


def reduce_rows(sizes, work, land, out, sems, base, rows, land_at, sem_at, letters, pending):
    plan = plan_of(sizes, rows, letters)
    start = base
    trail = []
    for level, (stage, split, count) in enumerate(plan):
        digit, others = digit_of(stage)
        keep = start + digit * count if split else start
        copies = []
        for offset, (other, peer) in enumerate(others):
            give = start + other * count if split else start
            slot = len(others) - 1 - offset
            copies.append(
                send(
                    work.at[span(give, count)],
                    land.at[span(land_at + slot * count, count)],
                    sems,
                    sem_at + offset,
                    peer,
                    sem_at + slot,
                )
            )
        yield
        for copy in copies:
            copy.wait_recv()
        if split:
            pending.extend(copies)
            trail.append((others, keep, count))
        else:
            for copy in copies:
                copy.wait_send()
        target = out if level == len(plan) - 1 else work
        add_rows(work, keep, land, land_at, len(others), target, keep, count)
        land_at += count * len(others)
        sem_at += len(others)
        start = keep
    for others, mine, count in reversed(trail):
        part = out.at[span(mine, count)]
        copies = [
            send(part, part, sems, sem_at + offset, peer, sem_at + len(others) - 1 - offset)
            for offset, (_, peer) in enumerate(others)
        ]
        yield
        for copy in copies:
            copy.wait_recv()
        pending.extend(copies)
        sem_at += len(others)


def reduce_whole(steps, land, sems, sem_at, bits):
    for level, bit in enumerate(bits):
        copy = send(steps.at[level], land.at[level], sems, sem_at + level, digit_of(bit)[1][0][1])
        yield
        copy.wait()
        steps[level + 1] = steps[level] + land[level]


def share_blocks(slots, sems, sem_at, me, pending):
    near, far = flip(me, 1), flip(me, 2)
    across = send(slots.at[me], slots.at[me], sems, sem_at, {"blk": far})
    beside = send(slots.at[me], slots.at[me], sems, sem_at + 1, {"blk": near})
    yield
    across.wait_recv()
    onward = send(slots.at[far], slots.at[far], sems, sem_at + 2, {"blk": near})
    yield
    beside.wait_recv()
    onward.wait_recv()
    pending.extend([across, beside, onward])


def by_rows(total, chunk, body, carry=0):
    def step(index, held):
        return body(pl.multiple_of(index * chunk, chunk), held)

    return lax.fori_loop(0, total // chunk, step, carry)


def dot(left, right):
    return jnp.dot(left, right, preferred_element_type=WIDE)


def dot_right_t(left, right):
    return lax.dot_general(left, right, (((1,), (1,)), ((), ())), preferred_element_type=WIDE)


def dot_left_t(left, right):
    return lax.dot_general(left, right, (((0,), (0,)), ((), ())), preferred_element_type=WIDE)


def fold(values):
    rows, width = values.shape
    return jnp.sum(values.reshape(rows // 8, 8, width), axis=0)


def mean_of(values):
    return jnp.mean(values, axis=-1, keepdims=True)


def norm_back(upstream, scaled, inverse, gain):
    inner = upstream * gain
    return inverse * (inner - mean_of(inner) - scaled * mean_of(inner * scaled))


def layout_of(sizes, seqs, rows, width, hidden):
    tokens = seqs * rows
    blocks = sizes["blk"]
    length = rows * blocks
    own = width // blocks
    heads = own // HEAD
    levels = len(bits_of(sizes, SUM_ORDER))
    units = 2 * (hidden // width) + 1
    land_total = sum(landing_rows(sizes, width, UNIT_ORDERS[at]) for at in range(units))
    own_land = max(landing_rows(sizes, width, order) for order in OWN_ORDERS)
    return dict(
        x_all=((seqs, length, width), LOW),
        x_own=((seqs, rows, width), LOW),
        cot=((seqs, rows, width), LOW),
        w_qkv=((width, 3 * own), LOW),
        w_o=((width, width), LOW),
        w_up=((width, hidden), LOW),
        w_down=((hidden, width), LOW),
        vec_low=((VECTORS * width,), LOW),
        vec=((VECTORS, width), WIDE),
        flags=((blocks, 8, rows), WIDE),
        qkv=((seqs, length, 3 * own), LOW),
        probs=((seqs * heads, length, length), LOW),
        o_wide=((seqs, length, own), WIDE),
        o_send=((seqs, length, own), LOW),
        o_all=((seqs, rows, width), LOW),
        total=((tokens, width), WIDE),
        scaled=((tokens, width), WIDE),
        inverse=((tokens, 128), WIDE),
        normed=((tokens, width), WIDE),
        normed_low=((tokens, width), LOW),
        active=((tokens, hidden), LOW),
        slope=((tokens, hidden), WIDE),
        hid=((seqs, rows, width), LOW),
        grad_b=((tokens, width), WIDE),
        grad_y=((tokens, width), LOW),
        grad_z=((tokens, hidden), LOW),
        grad_t=((tokens, width), LOW),
        do_send=((seqs, rows, width), LOW),
        do_all=((seqs, length, own), LOW),
        grad_s=((heads, length, length), LOW),
        d_qkv=((seqs, length, 3 * own), LOW),
        dx_part=((seqs, length, width), LOW),
        dx_near=((seqs, 2, rows, width), LOW),
        dx_chip=((seqs, rows, width), LOW),
        dx_far=((seqs, rows, width), LOW),
        dx=((seqs, rows, width), LOW),
        work=((units * width, width), LOW),
        land=((land_total, width), LOW),
        out=((units * width, width), LOW),
        own_work=((3, width, own), LOW),
        own_land=((3, own_land, own), LOW),
        own_out=((3, blocks, width, own), LOW),
        steps=((levels + 1, VECTORS, width), WIDE),
        vec_land=((levels, VECTORS, width), WIDE),
    )


def layer_kernel(sizes, names, *refs):
    x, lengths, mask, wq, wk, wv, wo, wu, wd, cotangent = refs[:10]
    vectors_in = refs[10:19]
    hid_out, dx_out, sums_out, own_sums_out, vec_out = refs[19:24]
    r = types.SimpleNamespace(**dict(zip(names, refs[24:-3], strict=True)))
    sems = refs[-3:-1]
    local = refs[-1]
    x_all, qkv, vec, steps = r.x_all, r.qkv, r.vec, r.steps
    seqs, rows, width = r.x_own.shape
    tokens = seqs * rows
    length = x_all.shape[1]
    blocks = sizes["blk"]
    own = width // blocks
    heads = own // HEAD
    hidden = r.w_up.shape[1]
    tiles = hidden // width
    scale = HEAD ** (-0.5)
    me = lax.axis_index("blk")
    near, far = flip(me, 1), flip(me, 2)
    cross = flip(far, 1)
    peers = (near, far, cross)
    place = lambda index: span(index * rows, rows, rows)
    lanes = lambda index: span(index * own, own, own)

    used = {"sem": 0, "local": 0}
    pending, stores = [], []

    def slot(count=1):
        at = used["sem"]
        used["sem"] += count
        return at

    def fetch(src, dst):
        copy = pltpu.make_async_copy(src, dst, local.at[used["local"]])
        used["local"] += 1
        copy.start()
        return copy

    loads_x = [
        fetch(x, x_all.at[:, place(me), :]),
        fetch(x, r.x_own),
    ]
    loads_w = [
        fetch(weight.at[:, lanes(me)], r.w_qkv.at[:, pl.ds(at * own, own)])
        for at, weight in enumerate((wq, wk, wv))
    ]
    load_vectors = []
    at = 0
    for vector in vectors_in:
        count = vector.shape[0]
        load_vectors.append(fetch(vector, r.vec_low.at[pl.ds(at, count)]))
        at += count
    load_o = fetch(wo, r.w_o)
    load_up = fetch(wu, r.w_up)
    load_down = fetch(wd, r.w_down)
    load_cot = fetch(cotangent, r.cot)

    positions = me * rows + lax.broadcasted_iota(jnp.int32, (1, rows), 1)
    flag_rows = []
    for seq in range(seqs):
        good = (mask[seq : seq + 1, :] == 1) & (positions < lengths[seq])
        flag_rows.append(jnp.where(good, 0.0, -1000000000.0).astype(WIDE))
    flag_rows.append(jnp.zeros((8 - seqs, rows), WIDE))
    r.flags[me] = jnp.concatenate(flag_rows, axis=0)

    barrier = pltpu.get_barrier_semaphore()
    greeted = [{"blk": peer} for peer in peers] + [
        peer for letter in "xz" for stage in stages_of(sizes)[letter] for _, peer in digit_of(stage)[1]
    ]
    for peer in greeted:
        pl.semaphore_signal(barrier, inc=1, device_id=peer, device_id_type=MESH)
    pl.semaphore_wait(barrier, len(greeted))

    at_far, at_near, at_on, at_flag = slot(seqs), slot(seqs), slot(seqs), slot(len(peers))
    flag_copies = [
        send(r.flags.at[me], r.flags.at[me], sems, at_flag + index, {"blk": peer})
        for index, peer in enumerate(peers)
    ]
    x_far, x_near, x_on = [], [], []
    for seq in range(seqs):
        target = x_all.at[seq, place(me), :]
        x_far.append(send(x.at[seq], target, sems, at_far + seq, {"blk": far}))
        x_near.append(send(x.at[seq], target, sems, at_near + seq, {"blk": near}))
    pending += flag_copies + x_far + x_near

    def forward_x(seq):
        x_far[seq].wait_recv()
        block = x_all.at[seq, place(far), :]
        x_on.append(send(block, block, sems, at_on + seq, {"blk": near}))

    lane = lax.broadcasted_iota(jnp.int32, (1, own), 1)
    of_head = [(lane >= head * HEAD) & (lane < (head + 1) * HEAD) for head in range(heads)]
    only = lambda values, head: jnp.where(of_head[head], values.astype(WIDE), 0.0)
    for copy in load_vectors:
        copy.wait()
    for at in range(8 + tiles):
        vec[at : at + 1, :] = r.vec_low[at * width : (at + 1) * width].astype(WIDE).reshape(1, width)
    bias_q = vec[0:1, lanes(me)]
    bias_v = vec[1:2, lanes(me)]
    bias_qkv = jnp.concatenate([bias_q, jnp.zeros_like(bias_q), bias_v], axis=1)
    o_all, o_send = r.o_all, r.o_send
    at_o = slot(seqs * len(peers))
    o_copies = []

    def project(seq):
        def body(at, carry):
            made = dot(x_all[seq, pl.ds(at, 256), :], r.w_qkv[...]) + bias_qkv
            qkv[seq, pl.ds(at, 256), :] = made.astype(LOW)
            return carry

        by_rows(length, 256, body)

    def attend(seq):
        keys = qkv[seq, :, own : 2 * own]
        values = qkv[seq, :, 2 * own :]
        key_bias = jnp.concatenate([r.flags[block, seq : seq + 1, :] for block in range(blocks)], axis=1)
        column = lax.broadcasted_iota(jnp.int32, (128, length), 1)
        row = lax.broadcasted_iota(jnp.int32, (128, length), 0)

        def body(at, carry):
            query = qkv[seq, pl.ds(at, 128), 0:own].astype(WIDE) * scale
            bias = jnp.where(column == row + at, 0.0, key_bias)
            joined = None
            for head in range(heads):
                scores = dot_right_t(only(query, head).astype(LOW), keys) + bias
                raised = jnp.exp(scores - jnp.max(scores, axis=-1, keepdims=True))
                probs = (raised / jnp.sum(raised, axis=-1, keepdims=True)).astype(LOW)
                r.probs[seq * heads + head, pl.ds(at, 128), :] = probs
                result = dot(probs, values)
                joined = result if joined is None else jnp.where(of_head[head], result, joined)
            r.o_wide[seq, pl.ds(at, 128), :] = joined
            o_send[seq, pl.ds(at, 128), :] = joined.astype(LOW)
            return carry

        by_rows(length, 128, body)
        for index, peer in enumerate(peers):
            o_copies.append(
                send(
                    o_send.at[seq, place(peer), :],
                    o_all.at[seq, :, lanes(me)],
                    sems,
                    at_o + seq * len(peers) + index,
                    {"blk": peer},
                )
            )
        o_all[seq, :, lanes(me)] = o_send[seq, place(me), :]

    for copy in loads_w:
        copy.wait()
    for copy in loads_x:
        copy.wait()
    for copy in flag_copies:
        copy.wait_recv()
    forward_x(0)
    for seq in range(seqs):
        x_near[seq].wait_recv()
        x_on[seq].wait_recv()
        project(seq)
        if seq + 1 < seqs:
            forward_x(seq + 1)
        attend(seq)
    pending += x_on + o_copies

    total, scaled, inverse = r.total, r.scaled, r.inverse
    normed, normed_low = r.normed, r.normed_low
    wide_row = lambda at: vec[at : at + 1, :]
    load_o.wait()
    for copy in o_copies:
        copy.wait_recv()
    flat = lambda ref, at, count: ref[lax.div(at, rows), span(lax.rem(at, rows), count), :]

    total[...] = dot(o_all[...].reshape(tokens, width), r.w_o[...])

    def first_norm(at, carry):
        part = pl.ds(at, 32)
        values = flat(r.x_own, at, 32).astype(WIDE) + total[part, :] + wide_row(2)
        center = values - mean_of(values)
        inv = lax.rsqrt(mean_of(center * center) + EPSILON)
        made = center * inv
        scaled[part, :] = made
        inverse[part, :] = jnp.broadcast_to(inv, (32, 128))
        result = made * wide_row(3) + wide_row(4)
        normed[part, :] = result
        normed_low[part, :] = result.astype(LOW)
        return carry

    by_rows(tokens, 32, first_norm)

    load_up.wait()
    active, slope = r.active, r.slope

    def up(tile, carry):
        columns = span(tile * width, width, width)
        total[...] = dot(normed_low[...], r.w_up[:, columns])
        offset = vec[pl.ds(8 + tile, 1), :]

        def bend(at, held):
            part = pl.ds(at, 32)
            z = total[part, :] + offset
            below = 0.5 * (1.0 + lax.erf(z * 0.7071067811865476))
            active[part, columns] = (z * below).astype(LOW)
            slope[part, columns] = below + z * (0.3989422804014327 * jnp.exp(-0.5 * z * z))
            return held

        by_rows(tokens, 32, bend)
        return carry

    lax.fori_loop(0, tiles, up, 0)
    load_down.wait()
    load_cot.wait()
    total[...] = dot(active[...], r.w_down[...])

    grad_b, grad_y = r.grad_b, r.grad_y
    zero = jnp.zeros((8, width), WIDE)

    def second_norm(at, sums):
        shift_sum, gain_sum, down_sum = sums
        part = pl.ds(at, 32)
        values = normed[part, :] + total[part, :] + wide_row(5)
        center = values - mean_of(values)
        inv = lax.rsqrt(mean_of(center * center) + EPSILON)
        made = center * inv
        r.hid[lax.div(at, rows), span(lax.rem(at, rows), 32), :] = (made * wide_row(6) + wide_row(7)).astype(LOW)
        upstream = flat(r.cot, at, 32).astype(WIDE)
        back = norm_back(upstream, made, inv, wide_row(6))
        grad_b[part, :] = back
        rounded = back.astype(LOW)
        grad_y[part, :] = rounded
        return shift_sum + fold(upstream), gain_sum + fold(upstream * made), down_sum + fold(rounded.astype(WIDE))

    shift_sum, gain_sum, down_sum = by_rows(tokens, 32, second_norm, (zero, zero, zero))
    stores.append(fetch(r.hid, hid_out))
    total_row = lambda values: jnp.sum(values, axis=0, keepdims=True)
    steps[0] = jnp.zeros((VECTORS, width), WIDE)
    steps[0, 7:8, :] = total_row(shift_sum)
    steps[0, 6:7, :] = total_row(gain_sum)
    steps[0, 5:6, :] = total_row(down_sum)

    work = r.work
    running = {}
    place_of = {"land": 0, "poll": 0}

    def launch(name, item):
        running[name] = item
        advance(name)

    def advance(name):
        if name in running and next(running[name], True) is not None:
            del running[name]

    def launch_unit(unit):
        letters = UNIT_ORDERS[unit]
        at = slot(semaphores_of(sizes, width, letters))
        land_at = place_of["land"]
        place_of["land"] += landing_rows(sizes, width, letters)
        launch(
            unit,
            reduce_rows(sizes, work, r.land, r.out, sems, unit * width, width, land_at, at, letters, pending),
        )

    def launch_own(kind):
        letters = OWN_ORDERS[kind]
        at = slot(semaphores_of(sizes, width, letters))
        blocks_at = slot(3)
        slots = r.own_out.at[kind]

        def item():
            parts = r.own_work.at[kind], r.own_land.at[kind], slots.at[me]
            yield from reduce_rows(sizes, *parts, sems, 0, width, 0, at, letters, pending)
            yield from share_blocks(slots, sems, blocks_at, me, pending)

        launch(2 * tiles + 1 + kind, item())

    def poll():
        at = place_of["poll"]
        place_of["poll"] += 1
        for name in POLLS[at] if at < len(POLLS) else ():
            advance(name)

    cut = lambda tile: slice(tile * width, (tile + 1) * width)
    for tile in range(tiles):
        work[cut(tile), :] = dot_left_t(active[:, cut(tile)], grad_y[...]).astype(LOW)
        launch_unit(tile)
        poll()

    grad_z = r.grad_z

    for tile in range(tiles):
        total[...] = dot_right_t(grad_y[...], r.w_down[cut(tile), :])

        def bend(at, held):
            part = pl.ds(at, 32)
            made = (total[part, :] * slope[part, cut(tile)]).astype(LOW)
            grad_z[part, cut(tile)] = made
            return held + fold(made.astype(WIDE))

        steps[0, 8 + tile : 9 + tile, :] = total_row(by_rows(tokens, 32, bend, zero))
        poll()
    total[...] = dot_right_t(grad_z[...], r.w_up[...])
    poll()

    grad_t = r.grad_t

    def first_back(at, sums):
        shift_part, gain_part, out_part = sums
        part = pl.ds(at, 32)
        upstream = grad_b[part, :] + total[part, :]
        made = scaled[part, :]
        back = norm_back(upstream, made, inverse[part, 0:1], wide_row(3))
        grad_b[part, :] = back
        rounded = back.astype(LOW)
        grad_t[part, :] = rounded
        return shift_part + fold(upstream), gain_part + fold(upstream * made), out_part + fold(rounded.astype(WIDE))

    shift_part, gain_part, out_part = by_rows(tokens, 32, first_back, (zero, zero, zero))
    steps[0, 4:5, :] = total_row(shift_part)
    steps[0, 3:4, :] = total_row(gain_part)
    steps[0, 2:3, :] = total_row(out_part)
    poll()

    do_send, do_all = r.do_send, r.do_all
    at_do = slot(seqs * len(peers))
    do_copies = []
    made = dot_right_t(grad_t[...], r.w_o[...]).astype(LOW)
    do_send[...] = made.reshape(seqs, rows, width)
    for seq in range(seqs):
        do_copies.append(
            [
                send(
                    do_send.at[seq, :, lanes(peer)],
                    do_all.at[seq, place(me), :],
                    sems,
                    at_do + seq * len(peers) + index,
                    {"blk": peer},
                )
                for index, peer in enumerate(peers)
            ]
        )
        do_all[seq, place(me), :] = do_send[seq, :, lanes(me)]
        pending += do_copies[-1]

    poll()
    work[2 * hidden :, :] = dot_left_t(o_all[...].reshape(tokens, width), grad_t[...]).astype(LOW)
    launch_unit(2 * tiles)
    poll()
    for tile in range(tiles):
        work[cut(tiles + tile), :] = dot_left_t(normed_low[...], grad_z[:, cut(tile)]).astype(LOW)
        launch_unit(tiles + tile)
        poll()

    d_qkv, grad_s, dx_part = r.d_qkv, r.grad_s, r.dx_part
    at_dx_near, at_dx_far = slot(2 * seqs), slot(seqs)
    dx_near, dx_far = [], []

    def value_back(seq):
        upstream = do_all[seq].astype(WIDE)
        grads = [
            dot_left_t(r.probs[seq * heads + head], only(upstream, head).astype(LOW)) for head in range(heads)
        ]
        d_qkv[seq, :, 2 * own :] = functools.reduce(jnp.add, grads).astype(LOW)

    def score_back(seq):
        values = qkv[seq, :, 2 * own :]

        def body(at, carry):
            upstream = do_all[seq, pl.ds(at, 128), :].astype(WIDE)
            inner = upstream * r.o_wide[seq, pl.ds(at, 128), :]
            for head in range(heads):
                delta = jnp.sum(jnp.where(of_head[head], inner, 0.0), axis=-1, keepdims=True)
                prob_grad = dot_right_t(only(upstream, head).astype(LOW), values)
                probs = r.probs[seq * heads + head, pl.ds(at, 128), :].astype(WIDE)
                grad_s[head, pl.ds(at, 128), :] = (probs * (prob_grad - delta)).astype(LOW)
            return carry

        by_rows(length, 128, body)

    def query_key_back(seq):
        queries_wide = qkv[seq, :, 0:own].astype(WIDE) * scale
        keys_wide = qkv[seq, :, own : 2 * own].astype(WIDE) * scale
        query_grads, key_grads = [], []
        for head in range(heads):
            query_grads.append(dot(grad_s[head], only(keys_wide, head).astype(LOW)))
            key_grads.append(dot_left_t(grad_s[head], only(queries_wide, head).astype(LOW)))
        d_qkv[seq, :, 0:own] = functools.reduce(jnp.add, query_grads).astype(LOW)
        d_qkv[seq, :, own : 2 * own] = functools.reduce(jnp.add, key_grads).astype(LOW)

    def input_back(seq):
        def partial(at, carry):
            dx_part[seq, pl.ds(at, 128), :] = dot_right_t(d_qkv[seq, pl.ds(at, 128), :], r.w_qkv[...]).astype(LOW)
            return carry

        by_rows(length, 128, partial)
        dx_near.append(
            [
                send(dx_part.at[seq, place(block), :], r.dx_near.at[seq, at], sems, at_dx_near + 2 * seq + at, {"blk": near})
                for at, block in enumerate((near, cross))
            ]
        )
        pending.extend(dx_near[-1])

    def own_grad(columns):
        tokens_in = x_all[...].reshape(seqs * length, width)
        return dot_left_t(tokens_in, d_qkv[:, :, columns].reshape(seqs * length, -1)).astype(LOW)

    def hand_on(seq):
        dx_near[seq][1].wait_recv()

        def body(at, carry):
            part = pl.ds(at, 32)
            summed = dx_part[seq, span(far * rows + at, 32), :].astype(WIDE) + r.dx_near[seq, 1, part, :].astype(WIDE)
            r.dx_chip[seq, part, :] = summed.astype(LOW)
            return carry

        by_rows(rows, 32, body)
        dx_far.append(send(r.dx_chip.at[seq], r.dx_far.at[seq], sems, at_dx_far + seq, {"blk": far}))
        pending.append(dx_far[-1])

    for seq in range(seqs):
        for copy in do_copies[seq]:
            copy.wait_recv()
        value_back(seq)
        poll()
    r.own_work[0] = own_grad(slice(2 * own, None))
    launch_own(0)
    poll()
    for seq in range(seqs):
        score_back(seq)
        poll()
        query_key_back(seq)
        poll()
        input_back(seq)
        poll()
        if seq > 0:
            hand_on(seq - 1)
    made = own_grad(slice(0, 2 * own))
    r.own_work[1] = made[:, :own]
    launch_own(1)
    r.own_work[2] = made[:, own:]
    launch_own(2)
    hand_on(seqs - 1)

    def offsets(at, sums):
        part = d_qkv[lax.div(at, length), span(lax.rem(at, length), 128), :]
        return sums + fold(part.astype(WIDE))

    sums = total_row(by_rows(seqs * length, 128, offsets, jnp.zeros((8, 3 * own), WIDE)))
    steps[0, 0:1, lanes(me)] = sums[:, 0:own]
    steps[0, 1:2, lanes(me)] = sums[:, 2 * own :]
    sum_bits = bits_of(sizes, SUM_ORDER)
    launch(2 * tiles + 4, reduce_whole(steps, r.vec_land, sems, slot(len(sum_bits)), sum_bits))
    poll()

    for seq in range(seqs):
        dx_near[seq][0].wait_recv()
        dx_far[seq].wait_recv()

        def finish(at, carry):
            part = pl.ds(at, 32)
            summed = grad_b[span(seq * rows + at, 32), :] + dx_part[seq, span(me * rows + at, 32), :].astype(WIDE)
            summed = summed + r.dx_near[seq, 0, part, :].astype(WIDE) + r.dx_far[seq, part, :].astype(WIDE)
            r.dx[seq, part, :] = summed.astype(LOW)
            return carry

        by_rows(rows, 32, finish)
        poll()
    stores.append(fetch(r.dx, dx_out))

    for name in sum(POLLS[place_of["poll"] :], ()):
        advance(name)
    while running:
        for name in list(running):
            advance(name)
    vec_out[...] = steps[len(sum_bits)]
    stores.append(fetch(r.out, sums_out))
    stores.append(fetch(r.own_out, own_sums_out))
    for copy in pending:
        copy.wait_send()
    for copy in stores:
        copy.wait()


def widen_kernel(blocks, hid, dx, sums, shared, vec, *refs):
    hid_out, dx_out, wq, wk, wv, wo, wu, wd = refs[:8]
    rows_out, bu = refs[8:16], refs[16]
    low, shared_low, wide, shared_wide, hid_low, dx_low, sems = refs[17:]
    width = wq.shape[0]
    own = width // blocks
    units = low.shape[0] // width
    tiles = (units - 1) // 2
    used = [0]

    def copy(src, dst):
        made = pltpu.make_async_copy(src, dst, sems.at[used[0]])
        used[0] += 1
        made.start()
        return made

    unit = lambda ref, at: ref.at[pl.ds(at * width, width)]
    loads = [copy(unit(sums, at), unit(low, at)) for at in range(units)]
    load_shared = copy(shared, shared_low)
    token_loads = [copy(hid, hid_low), copy(dx, dx_low)]
    stores = []
    targets = (
        [unit(wd, at) for at in range(tiles)] + [wu.at[:, pl.ds(at * width, width)] for at in range(tiles)] + [wo]
    )
    for at, row in enumerate(rows_out):
        row[...] = vec[at, :]
    for at in range(tiles):
        bu[at * width : (at + 1) * width] = vec[len(rows_out) + at, :]
    for at in range(units):
        loads[at].wait()

        def body(step, carry):
            part = span(at * width + step * 64, 64)
            wide[part, :] = low[part, :].astype(WIDE)
            return carry

        lax.fori_loop(0, width // 64, body, 0)
        stores.append(copy(unit(wide, at), targets[at]))
    for load in token_loads:
        load.wait()
    stores += [copy(hid_low, hid_out), copy(dx_low, dx_out)]
    load_shared.wait()
    for kind, target in enumerate((wv, wq, wk)):

        def body(step, carry):
            part = span(step * 64, 64)
            for block in range(blocks):
                shared_wide[kind, part, block * own : (block + 1) * own] = shared_low[kind, block, part, :].astype(WIDE)
            return carry

        lax.fori_loop(0, width // 64, body, 0)
        stores.append(copy(shared_wide.at[kind], target))
    for made in stores:
        made.wait()


def on_device(
    sizes,
    hidden_input,
    lengths,
    key_mask,
    query_weight,
    query_offset,
    key_weight,
    value_weight,
    value_offset,
    output_weight,
    output_offset,
    mixer_gain,
    mixer_shift,
    up_weight,
    up_offset,
    down_weight,
    down_offset,
    final_gain,
    final_shift,
    cotangent,
):
    seqs, rows, width = hidden_input.shape
    hidden = up_weight.shape[1]
    blocks = sizes["blk"]
    own = width // blocks
    scratch = layout_of(sizes, seqs, rows, width, hidden)
    anywhere = pl.BlockSpec(memory_space=pl.ANY)
    inside = pl.BlockSpec(memory_space=pltpu.VMEM)
    scalars = pl.BlockSpec(memory_space=pltpu.SMEM)
    scratch_shape = types.SimpleNamespace(**{name: shape for name, (shape, _) in scratch.items()})
    units = scratch_shape.work
    shared = scratch_shape.own_out
    hid, dx, sums, own_sums, vec_sums = pl.pallas_call(
        functools.partial(layer_kernel, sizes, tuple(scratch)),
        out_shape=(
            jax.ShapeDtypeStruct(hidden_input.shape, LOW),
            jax.ShapeDtypeStruct(hidden_input.shape, LOW),
            jax.ShapeDtypeStruct(units, LOW),
            jax.ShapeDtypeStruct(shared, LOW),
            jax.ShapeDtypeStruct((VECTORS, width), WIDE),
        ),
        in_specs=[anywhere, scalars, inside] + [anywhere] * 16,
        out_specs=(anywhere, anywhere, anywhere, anywhere, inside),
        scratch_shapes=[pltpu.VMEM(shape, kind) for shape, kind in scratch.values()]
        + [
            pltpu.SemaphoreType.DMA((256,)),
            pltpu.SemaphoreType.DMA((256,)),
            pltpu.SemaphoreType.DMA((32,)),
        ],
        compiler_params=pltpu.CompilerParams(
            collective_id=0, has_side_effects=True, vmem_limit_bytes=60 * 1024 * 1024
        ),
    )(
        hidden_input,
        lengths,
        key_mask,
        query_weight,
        key_weight,
        value_weight,
        output_weight,
        up_weight,
        down_weight,
        cotangent,
        query_offset,
        value_offset,
        output_offset,
        mixer_gain,
        mixer_shift,
        down_offset,
        final_gain,
        final_shift,
        up_offset,
    )
    full = jax.ShapeDtypeStruct((width, width), WIDE)
    row = jax.ShapeDtypeStruct((width,), WIDE)
    flat = jax.ShapeDtypeStruct(hidden_input.shape, LOW)
    final = pl.pallas_call(
        functools.partial(widen_kernel, blocks),
        out_shape=(
            flat,
            flat,
            full,
            full,
            full,
            full,
            jax.ShapeDtypeStruct((width, hidden), WIDE),
            jax.ShapeDtypeStruct((hidden, width), WIDE),
        )
        + (row,) * 8
        + (jax.ShapeDtypeStruct((hidden,), WIDE),),
        in_specs=[anywhere] * 4 + [inside],
        out_specs=(anywhere,) * 8 + (inside,) * 9,
        scratch_shapes=[
            pltpu.VMEM(units, LOW),
            pltpu.VMEM(shared, LOW),
            pltpu.VMEM(units, WIDE),
            pltpu.VMEM((3, width, width), WIDE),
            pltpu.VMEM(hidden_input.shape, LOW),
            pltpu.VMEM(hidden_input.shape, LOW),
            pltpu.SemaphoreType.DMA((2 * units[0] // width + 12,)),
        ],
        compiler_params=pltpu.CompilerParams(vmem_limit_bytes=60 * 1024 * 1024),
    )(hid, dx, sums, own_sums, vec_sums)
    hid, dx, wq, wk, wv, wo, wu, wd, bq, bv, bo, g1, s1, bd, g2, s2, bu = final
    return hid, dx, wq, bq, wk, wv, bv, wo, bo, g1, s1, wu, bu, wd, bd, g2, s2


def solution(mesh):
    split = P("dp", "blk", None)
    in_specs = (split, P("dp"), P("dp", "blk")) + (P(),) * 15 + (split,)
    out_specs = (split, split) + (P(),) * 15
    return jax.shard_map(
        functools.partial(on_device, dict(mesh.shape)),
        mesh=mesh,
        in_specs=in_specs,
        out_specs=out_specs,
        check_vma=False,
    )
```

```python
import functools
import types

import jax
import jax.numpy as jnp
from jax import lax
from jax.experimental import pallas as pl
from jax.experimental.pallas import tpu as pltpu
from jax.sharding import PartitionSpec as P

HEAD = 64
EPSILON = 1e-06
MESH = pl.DeviceIdType.MESH
ROWS = 16
LOW = jnp.bfloat16
WIDE = jnp.float32
VECTORS = 16
LOCALS = 32

UNIT_ORDERS = ("cyxz", "cxyz", "cyxz", "cayxb", "caxby", "cxyab", "caxyb", "czxy", "cxyab")
OWN_ORDERS = ("xab", "xz", "xz")
SUM_ORDER = "cxyab"
POLLS = (
    (),
    (),
    (),
    (),
    (),
    (0,),
    (1, 2,),
    (3,),
    (),
    (),
    (),
    (),
    (),
    (0,),
    (1, 8,),
    (4, 3, 5,),
    (6, 2, 7,),
    (0,),
    (),
    (8, 4,),
    (1,),
    (3, 5,),
    (6,),
    (2,),
    (9, 8,),
    (4,),
    (5, 3,),
    (7, 6, 0,),
    (1,),
    (9, 2, 8, 7,),
    (4, 5, 6, 12,),
    (10, 3, 0, 1,),
    (9, 11, 2, 12, 8,),
    (7, 5, 4, 6, 0, 1, 10, 3, 9, 12, 7, 2, 4, 11, 8, 5, 9, 6, 1, 0, 12, 3, 10, 7, 1, 0, 4, 8, 2, 5, 6, 9, 11, 2, 3, 10, 12, 4, 8, 6, 5, 11, 7, 9, 3, 8, 7, 9, 3, 10, 8, 4, 5, 10, 4, 11, 5, 6, 11, 6,),
)


def stages_of(sizes):
    def split(step, rest):
        found = []
        while rest > 1:
            radix = 4 if rest % 4 == 0 else 2
            found.append(("dp", step, radix))
            step *= radix
            rest //= radix
        return found

    dp = sizes["dp"]
    return dict(
        c=[("blk", 1, 2)], y=[("blk", 2, 2)], x=[("dp", 1, 2)], a=[("dp", 2, 2)], b=split(4, dp // 4), z=split(2, dp // 2)
    )


def bits_of(sizes, letters):
    bits = []
    for letter in letters:
        for axis, step, radix in stages_of(sizes)[letter]:
            bits += [(axis, step, 2)] if radix == 2 else [(axis, step, 2), (axis, 2 * step, 2)]
    return bits


def digit_of(stage):
    axis, step, radix = stage
    index = lax.axis_index(axis)
    digit = lax.rem(lax.div(index, step), radix)
    others = []
    for offset in range(1, radix):
        other = lax.rem(digit + offset, radix)
        others.append((other, {axis: index + (other - digit) * step}))
    return digit, others


def flip(index, step):
    return index + step - 2 * step * lax.rem(lax.div(index, step), 2)


def aligned(start, unit):
    return start if isinstance(start, int) else pl.multiple_of(start, unit)


def span(start, count, unit=ROWS):
    return pl.ds(aligned(start, unit), count)


def send(src, dst, sems, at, peer, land_at=None):
    sends, receives = sems
    copy = pltpu.make_async_remote_copy(
        src_ref=src,
        dst_ref=dst,
        send_sem=sends.at[at],
        recv_sem=receives.at[at if land_at is None else land_at],
        device_id=peer,
        device_id_type=MESH,
    )
    copy.start()
    return copy


def plan_of(sizes, rows, letters):
    plan = []
    size = rows
    for letter in letters:
        for axis, step, radix in stages_of(sizes)[letter]:
            if size % (radix * ROWS) == 0:
                size //= radix
                plan.append(((axis, step, radix), True, size))
                continue
            bit = step
            while bit < step * radix:
                split = size % (2 * ROWS) == 0
                size = size // 2 if split else size
                plan.append(((axis, bit, 2), split, size))
                bit *= 2
    return plan


def landing_rows(sizes, rows, letters):
    return sum(size * (stage[2] - 1) for stage, _, size in plan_of(sizes, rows, letters))


def semaphores_of(sizes, rows, letters):
    peers = [stage[2] - 1 for stage, _, _ in plan_of(sizes, rows, letters)]
    return max(peers), 2 * sum(peers)


def semaphore_counts(sizes, seqs, width):
    sends, receives = 3 + 6 * seqs + 1, 3 + 12 * seqs + len(bits_of(sizes, SUM_ORDER))
    for letters in UNIT_ORDERS:
        sending, receiving = semaphores_of(sizes, width, letters)
        sends, receives = sends + sending, receives + receiving
    for letters in OWN_ORDERS:
        sending, receiving = semaphores_of(sizes, width, letters)
        sends, receives = sends + max(sending, 3), receives + receiving + 3
    return sends, receives


def add_rows(first, first_at, land, land_at, terms, out, out_at, count):
    total = first[span(first_at, count)].astype(WIDE)
    for term in range(terms):
        total = total + land[span(land_at + term * count, count)].astype(WIDE)
    out[span(out_at, count)] = total.astype(out.dtype)


def reduce_rows(sizes, work, land, out, sems, base, rows, land_at, send_at, receive_at, letters, sent):
    plan = plan_of(sizes, rows, letters)
    start = base
    trail = []
    for level, (stage, split, count) in enumerate(plan):
        digit, others = digit_of(stage)
        keep = start + digit * count if split else start
        for copy in sent:
            copy.wait_send()
        sent.clear()
        for offset, (other, peer) in enumerate(others):
            give = start + other * count if split else start
            slot = len(others) - 1 - offset
            sent.append(
                send(
                    work.at[span(give, count)],
                    land.at[span(land_at + slot * count, count)],
                    sems,
                    send_at + offset,
                    peer,
                    receive_at + slot,
                )
            )
        yield
        for copy in sent:
            copy.wait_recv()
        if split:
            trail.append((others, keep, count))
        else:
            for copy in sent:
                copy.wait_send()
            sent.clear()
        target = out if level == len(plan) - 1 else work
        add_rows(work, keep, land, land_at, len(others), target, keep, count)
        land_at += count * len(others)
        receive_at += len(others)
        start = keep
    for others, mine, count in reversed(trail):
        part = out.at[span(mine, count)]
        for copy in sent:
            copy.wait_send()
        sent.clear()
        for offset, (_, peer) in enumerate(others):
            sent.append(send(part, part, sems, send_at + offset, peer, receive_at + len(others) - 1 - offset))
        yield
        for copy in sent:
            copy.wait_recv()
        receive_at += len(others)


def reduce_whole(steps, land, sems, send_at, receive_at, bits):
    for level, bit in enumerate(bits):
        copy = send(steps.at[level], land.at[level], sems, send_at, digit_of(bit)[1][0][1], receive_at + level)
        yield
        copy.wait()
        steps[level + 1] = steps[level] + land[level]


def share_blocks(slots, sems, send_at, receive_at, me, sent):
    near, far = flip(me, 1), flip(me, 2)
    for copy in sent:
        copy.wait_send()
    across = send(slots.at[me], slots.at[me], sems, send_at, {"blk": far}, receive_at)
    beside = send(slots.at[me], slots.at[me], sems, send_at + 1, {"blk": near}, receive_at + 1)
    yield
    across.wait_recv()
    onward = send(slots.at[far], slots.at[far], sems, send_at + 2, {"blk": near}, receive_at + 2)
    yield
    beside.wait_recv()
    onward.wait_recv()
    sent[:] = [across, beside, onward]


def dot(left, right):
    return jnp.dot(left, right, preferred_element_type=WIDE)


def dot_right_t(left, right):
    return lax.dot_general(left, right, (((1,), (1,)), ((), ())), preferred_element_type=WIDE)


def dot_left_t(left, right):
    return lax.dot_general(left, right, (((0,), (0,)), ((), ())), preferred_element_type=WIDE)


def fold(values):
    rows, width = values.shape
    return jnp.sum(values.reshape(rows // 8, 8, width), axis=0)


def mean_of(values):
    return jnp.mean(values, axis=-1, keepdims=True)


def norm_back(upstream, scaled, inverse, gain):
    inner = upstream * gain
    return inverse * (inner - mean_of(inner) - scaled * mean_of(inner * scaled))


def layout_of(sizes, seqs, rows, width, hidden):
    tokens = seqs * rows
    blocks = sizes["blk"]
    length = rows * blocks
    own = width // blocks
    heads = own // HEAD
    levels = len(bits_of(sizes, SUM_ORDER))
    units = 2 * (hidden // width) + 1
    land_total = sum(landing_rows(sizes, width, UNIT_ORDERS[at]) for at in range(units))
    own_land = max(landing_rows(sizes, width, order) for order in OWN_ORDERS)
    return dict(
        x_all=((seqs, length, width), LOW),
        x_own=((seqs, rows, width), LOW),
        cot=((seqs, rows, width), LOW),
        w_qkv=((width, 3 * own), LOW),
        w_o=((width, width), LOW),
        w_up=((width, hidden), LOW),
        w_down=((hidden, width), LOW),
        vec_low=((VECTORS * width,), LOW),
        vec=((VECTORS, width), WIDE),
        flags=((blocks, 8, rows), WIDE),
        qkv=((seqs, length, 3 * own), LOW),
        probs=((seqs * heads, length, length), LOW),
        o_wide=((seqs, length, own), WIDE),
        o_send=((seqs, length, own), LOW),
        o_all=((seqs, rows, width), LOW),
        total=((tokens, width), WIDE),
        scaled=((tokens, width), WIDE),
        inverse=((tokens, 128), WIDE),
        normed=((tokens, width), WIDE),
        normed_low=((tokens, width), LOW),
        active=((tokens, hidden), LOW),
        slope=((tokens, hidden), WIDE),
        grad_b=((tokens, width), WIDE),
        grad_y=((tokens, width), LOW),
        grad_z=((tokens, hidden), LOW),
        grad_t=((tokens, width), LOW),
        do_send=((seqs, rows, width), LOW),
        do_all=((seqs, length, own), LOW),
        grad_s=((heads, length, length), LOW),
        d_qkv=((seqs, length, 3 * own), LOW),
        dx_part=((seqs, length, width), LOW),
        dx_near=((seqs, 2, rows, width), LOW),
        dx_chip=((seqs, rows, width), LOW),
        hid=((seqs, rows, width), LOW),
        dx=((seqs, rows, width), LOW),
        out=((units * width, width), LOW),
        own_out=((3, blocks, width, own), LOW),
        dx_far=((seqs, rows, width), LOW),
        work=((units * width, width), LOW),
        land=((land_total, width), LOW),
        own_work=((3, width, own), LOW),
        own_land=((3, own_land, own), LOW),
        steps=((levels + 1, VECTORS, width), WIDE),
        vec_land=((levels, VECTORS, width), WIDE),
    )


def layer_kernel(sizes, names, *refs):
    x, lengths, mask, wq, wk, wv, wo, wu, wd, cotangent = refs[:10]
    vectors_in = refs[10:19]
    hid_out, dx_out, sums_out, own_sums_out, vec_out = refs[19:24]
    r = types.SimpleNamespace(**dict(zip(names, refs[24:-3], strict=True)))
    sems = refs[-3:-1]
    local = refs[-1]
    x_all, qkv, vec, steps = r.x_all, r.qkv, r.vec, r.steps
    seqs, rows, width = r.x_own.shape
    tokens = seqs * rows
    length = x_all.shape[1]
    blocks = sizes["blk"]
    own = width // blocks
    heads = own // HEAD
    hidden = r.w_up.shape[1]
    tiles = hidden // width
    scale = HEAD ** (-0.5)
    me = lax.axis_index("blk")
    near, far = flip(me, 1), flip(me, 2)
    cross = flip(far, 1)
    peers = (near, far, cross)
    place = lambda index: span(index * rows, rows, rows)
    lanes = lambda index: span(index * own, own, own)

    used = {"send": 0, "receive": 0, "local": 0}
    pending, stores = [], []

    def take(which, count):
        at = used[which]
        used[which] += count
        return at

    def slot(count):
        return take("send", count), take("receive", count)

    def send_in(pair, offset, src, dst, peer):
        return send(src, dst, sems, pair[0] + offset, {"blk": peer}, pair[1] + offset)

    def fetch(src, dst):
        copy = pltpu.make_async_copy(src, dst, local.at[used["local"]])
        used["local"] += 1
        copy.start()
        return copy

    loads_x = [
        fetch(x, x_all.at[:, place(me), :]),
        fetch(x, r.x_own),
    ]
    loads_w = [
        fetch(weight.at[:, lanes(me)], r.w_qkv.at[:, pl.ds(at * own, own)])
        for at, weight in enumerate((wq, wk, wv))
    ]
    load_vectors = []
    at = 0
    for vector in vectors_in:
        count = vector.shape[0]
        load_vectors.append(fetch(vector, r.vec_low.at[pl.ds(at, count)]))
        at += count
    load_o = fetch(wo, r.w_o)
    load_up = fetch(wu, r.w_up)
    load_down = fetch(wd, r.w_down)
    load_cot = fetch(cotangent, r.cot)

    positions = me * rows + lax.broadcasted_iota(jnp.int32, (1, rows), 1)
    flag_rows = []
    for seq in range(seqs):
        good = (mask[seq : seq + 1, :] == 1) & (positions < lengths[seq])
        flag_rows.append(jnp.where(good, 0.0, -1000000000.0).astype(WIDE))
    flag_rows.append(jnp.zeros((8 - seqs, rows), WIDE))
    r.flags[me] = jnp.concatenate(flag_rows, axis=0)

    barrier = pltpu.get_barrier_semaphore()
    greeted = [{"blk": peer} for peer in peers] + [
        peer for letter in "xz" for stage in stages_of(sizes)[letter] for _, peer in digit_of(stage)[1]
    ]
    for peer in greeted:
        pl.semaphore_signal(barrier, inc=1, device_id=peer, device_id_type=MESH)
    pl.semaphore_wait(barrier, len(greeted))

    at_far, at_near, at_on, at_flag = slot(seqs), slot(seqs), slot(seqs), slot(len(peers))
    flag_copies = [
        send_in(at_flag, index, r.flags.at[me], r.flags.at[me], peer)
        for index, peer in enumerate(peers)
    ]
    x_far, x_near, x_on = [], [], []
    for seq in range(seqs):
        target = x_all.at[seq, place(me), :]
        x_far.append(send_in(at_far, seq, x.at[seq], target, far))
        x_near.append(send_in(at_near, seq, x.at[seq], target, near))
    pending += flag_copies

    def forward_x(seq):
        x_far[seq].wait_recv()
        block = x_all.at[seq, place(far), :]
        x_on.append(send_in(at_on, seq, block, block, near))

    lane = lax.broadcasted_iota(jnp.int32, (1, own), 1)
    of_head = [(lane >= head * HEAD) & (lane < (head + 1) * HEAD) for head in range(heads)]
    only = lambda values, head: jnp.where(of_head[head], values.astype(WIDE), 0.0)
    for copy in load_vectors:
        copy.wait()
    for at in range(8 + tiles):
        vec[at : at + 1, :] = r.vec_low[at * width : (at + 1) * width].astype(WIDE).reshape(1, width)
    bias_q = vec[0:1, lanes(me)]
    bias_v = vec[1:2, lanes(me)]
    bias_qkv = jnp.concatenate([bias_q, jnp.zeros_like(bias_q), bias_v], axis=1)
    o_all, o_send = r.o_all, r.o_send
    at_o = slot(seqs * len(peers))
    o_copies = []

    def project(seq):
        qkv[seq] = (dot(x_all[seq], r.w_qkv[...]) + bias_qkv).astype(LOW)

    column = lax.broadcasted_iota(jnp.int32, (length, length), 1)
    row = lax.broadcasted_iota(jnp.int32, (length, length), 0)

    def attend(seq):
        keys = qkv[seq, :, own : 2 * own]
        values = qkv[seq, :, 2 * own :]
        key_bias = jnp.concatenate([r.flags[block, seq : seq + 1, :] for block in range(blocks)], axis=1)
        bias = jnp.where(column == row, 0.0, key_bias)
        query = qkv[seq, :, 0:own].astype(WIDE) * scale
        joined = None
        for head in range(heads):
            scores = dot_right_t(only(query, head).astype(LOW), keys) + bias
            raised = jnp.exp(scores - jnp.max(scores, axis=-1, keepdims=True))
            probs = (raised / jnp.sum(raised, axis=-1, keepdims=True)).astype(LOW)
            r.probs[seq * heads + head] = probs
            result = dot(probs, values)
            joined = result if joined is None else jnp.where(of_head[head], result, joined)
        r.o_wide[seq] = joined
        o_send[seq] = joined.astype(LOW)
        for index, peer in enumerate(peers):
            part = o_send.at[seq, place(peer), :]
            o_copies.append(send_in(at_o, seq * len(peers) + index, part, o_all.at[seq, :, lanes(me)], peer))
        o_all[seq, :, lanes(me)] = o_send[seq, place(me), :]

    for copy in loads_w:
        copy.wait()
    for copy in loads_x:
        copy.wait()
    for copy in flag_copies:
        copy.wait_recv()
    forward_x(0)
    for seq in range(seqs):
        x_near[seq].wait_recv()
        x_on[seq].wait_recv()
        project(seq)
        if seq + 1 < seqs:
            forward_x(seq + 1)
        attend(seq)

    total, scaled, inverse = r.total, r.scaled, r.inverse
    normed, normed_low = r.normed, r.normed_low
    wide_row = lambda at: vec[at : at + 1, :]
    load_o.wait()
    for copy in o_copies:
        copy.wait_recv()
    flat = lambda ref: ref[...].reshape(tokens, width)
    values = flat(r.x_own).astype(WIDE) + dot(flat(o_all), r.w_o[...]) + wide_row(2)
    center = values - mean_of(values)
    inv = lax.rsqrt(mean_of(center * center) + EPSILON)
    made = center * inv
    scaled[...] = made
    inverse[...] = jnp.broadcast_to(inv, inverse.shape)
    result = made * wide_row(3) + wide_row(4)
    normed[...] = result
    normed_low[...] = result.astype(LOW)

    load_up.wait()
    active, slope = r.active, r.slope

    def up(tile, carry):
        columns = span(tile * width, width, width)
        z = dot(normed_low[...], r.w_up[:, columns]) + vec[pl.ds(8 + tile, 1), :]
        below = 0.5 * (1.0 + lax.erf(z * 0.7071067811865476))
        active[:, columns] = (z * below).astype(LOW)
        slope[:, columns] = below + z * (0.3989422804014327 * jnp.exp(-0.5 * z * z))
        return carry

    lax.fori_loop(0, tiles, up, 0)
    load_down.wait()
    load_cot.wait()
    values = normed[...] + dot(active[...], r.w_down[...]) + wide_row(5)

    grad_b, grad_y = r.grad_b, r.grad_y
    center = values - mean_of(values)
    inv = lax.rsqrt(mean_of(center * center) + EPSILON)
    made = center * inv
    r.hid[...] = (made * wide_row(6) + wide_row(7)).astype(LOW).reshape(seqs, rows, width)
    upstream = flat(r.cot).astype(WIDE)
    back = norm_back(upstream, made, inv, wide_row(6))
    grad_b[...] = back
    rounded = back.astype(LOW)
    grad_y[...] = rounded
    total_row = lambda values: jnp.sum(fold(values), axis=0, keepdims=True)
    steps[0] = jnp.zeros((VECTORS, width), WIDE)
    steps[0, 7:8, :] = total_row(upstream)
    steps[0, 6:7, :] = total_row(upstream * made)
    steps[0, 5:6, :] = total_row(rounded.astype(WIDE))

    stores.append(fetch(r.hid, hid_out))

    work = r.work
    running = {}
    last = []
    place_of = {"land": 0, "poll": 0}

    def launch(name, item):
        running[name] = item
        advance(name)

    def advance(name):
        if name in running and next(running[name], True) is not None:
            del running[name]

    def launch_unit(unit):
        letters = UNIT_ORDERS[unit]
        sending, receiving = semaphores_of(sizes, width, letters)
        ats = take("send", sending), take("receive", receiving)
        land_at = place_of["land"]
        place_of["land"] += landing_rows(sizes, width, letters)
        sent = []
        last.append(sent)
        def item():
            yield from reduce_rows(sizes, work, r.land, r.out, sems, unit * width, width, land_at, *ats, letters, sent)
            stores.append(fetch(r.out.at[cut(unit)], sums_out.at[cut(unit)]))

        launch(unit, item())

    def launch_own(kind):
        letters = OWN_ORDERS[kind]
        sending, receiving = semaphores_of(sizes, width, letters)
        ats = take("send", max(sending, 3)), take("receive", receiving)
        blocks_at = take("receive", 3)
        slots = r.own_out.at[kind]
        sent = []
        last.append(sent)

        def item():
            parts = r.own_work.at[kind], r.own_land.at[kind], slots.at[me]
            yield from reduce_rows(sizes, *parts, sems, 0, width, 0, *ats, letters, sent)
            yield from share_blocks(slots, sems, ats[0], blocks_at, me, sent)
            stores.append(fetch(slots, own_sums_out.at[kind]))

        launch(2 * tiles + 1 + kind, item())

    def poll():
        at = place_of["poll"]
        place_of["poll"] += 1
        for name in POLLS[at] if at < len(POLLS) else ():
            advance(name)

    cut = lambda tile: slice(tile * width, (tile + 1) * width)
    for tile in range(tiles):
        work[cut(tile), :] = dot_left_t(active[:, cut(tile)], grad_y[...]).astype(LOW)
        launch_unit(tile)
        poll()

    grad_z = r.grad_z

    for tile in range(tiles):
        made = (dot_right_t(grad_y[...], r.w_down[cut(tile), :]) * slope[:, cut(tile)]).astype(LOW)
        grad_z[:, cut(tile)] = made
        steps[0, 8 + tile : 9 + tile, :] = total_row(made.astype(WIDE))
        poll()
    upstream = grad_b[...] + dot_right_t(grad_z[...], r.w_up[...])
    total[...] = upstream
    poll()
    upstream = total[...]

    grad_t = r.grad_t
    made = scaled[...]
    back = norm_back(upstream, made, inverse[:, 0:1], wide_row(3))
    grad_b[...] = back
    rounded = back.astype(LOW)
    grad_t[...] = rounded
    steps[0, 4:5, :] = total_row(upstream)
    steps[0, 3:4, :] = total_row(upstream * made)
    steps[0, 2:3, :] = total_row(rounded.astype(WIDE))
    poll()

    do_send, do_all = r.do_send, r.do_all
    for copy in x_far + x_near + x_on:
        copy.wait_send()
    at_do = at_far[0], take("receive", seqs * len(peers))
    do_copies = []
    made = dot_right_t(grad_t[...], r.w_o[...]).astype(LOW)
    do_send[...] = made.reshape(seqs, rows, width)
    for seq in range(seqs):
        do_copies.append(
            [
                send_in(
                    at_do,
                    seq * len(peers) + index,
                    do_send.at[seq, :, lanes(peer)],
                    do_all.at[seq, place(me), :],
                    peer,
                )
                for index, peer in enumerate(peers)
            ]
        )
        do_all[seq, place(me), :] = do_send[seq, :, lanes(me)]
        pending += do_copies[-1]

    poll()
    work[2 * hidden :, :] = dot_left_t(o_all[...].reshape(tokens, width), grad_t[...]).astype(LOW)
    launch_unit(2 * tiles)
    poll()
    for tile in range(tiles):
        work[cut(tiles + tile), :] = dot_left_t(normed_low[...], grad_z[:, cut(tile)]).astype(LOW)
        launch_unit(tiles + tile)
        poll()

    d_qkv, grad_s, dx_part = r.d_qkv, r.grad_s, r.dx_part
    for copy in o_copies:
        copy.wait_send()
    at_dx_near = at_o[0], take("receive", 2 * seqs)
    at_dx_far = at_o[0] + 2 * seqs, take("receive", seqs)
    dx_near, dx_far = [], []

    def value_back(seq):
        upstream = do_all[seq].astype(WIDE)
        grads = [
            dot_left_t(r.probs[seq * heads + head], only(upstream, head).astype(LOW)) for head in range(heads)
        ]
        d_qkv[seq, :, 2 * own :] = functools.reduce(jnp.add, grads).astype(LOW)

    def score_back(seq):
        values = qkv[seq, :, 2 * own :]
        upstream = do_all[seq].astype(WIDE)
        inner = upstream * r.o_wide[seq]
        for head in range(heads):
            delta = jnp.sum(only(inner, head), axis=-1, keepdims=True)
            prob_grad = dot_right_t(only(upstream, head).astype(LOW), values)
            probs = r.probs[seq * heads + head].astype(WIDE)
            grad_s[head] = (probs * (prob_grad - delta)).astype(LOW)

    def query_key_back(seq):
        queries_wide = qkv[seq, :, 0:own].astype(WIDE) * scale
        keys_wide = qkv[seq, :, own : 2 * own].astype(WIDE) * scale
        query_grads, key_grads = [], []
        for head in range(heads):
            query_grads.append(dot(grad_s[head], only(keys_wide, head).astype(LOW)))
            key_grads.append(dot_left_t(grad_s[head], only(queries_wide, head).astype(LOW)))
        d_qkv[seq, :, 0:own] = functools.reduce(jnp.add, query_grads).astype(LOW)
        d_qkv[seq, :, own : 2 * own] = functools.reduce(jnp.add, key_grads).astype(LOW)

    def input_back(seq):
        dx_part[seq] = dot_right_t(d_qkv[seq], r.w_qkv[...]).astype(LOW)
        dx_near.append(
            [
                send_in(at_dx_near, 2 * seq + at, dx_part.at[seq, place(block), :], r.dx_near.at[seq, at], near)
                for at, block in enumerate((near, cross))
            ]
        )
        pending.extend(dx_near[-1])

    def own_grad(columns):
        tokens_in = x_all[...].reshape(seqs * length, width)
        return dot_left_t(tokens_in, d_qkv[:, :, columns].reshape(seqs * length, -1)).astype(LOW)

    def hand_on(seq):
        dx_near[seq][1].wait_recv()
        summed = dx_part[seq, place(far), :].astype(WIDE) + r.dx_near[seq, 1].astype(WIDE)
        r.dx_chip[seq] = summed.astype(LOW)
        dx_far.append(send_in(at_dx_far, seq, r.dx_chip.at[seq], r.dx_far.at[seq], far))
        pending.append(dx_far[-1])

    for seq in range(seqs):
        for copy in do_copies[seq]:
            copy.wait_recv()
        value_back(seq)
        poll()
    r.own_work[0] = own_grad(slice(2 * own, None))
    launch_own(0)
    poll()
    for seq in range(seqs):
        score_back(seq)
        poll()
        query_key_back(seq)
        poll()
        input_back(seq)
        poll()
        if seq > 0:
            hand_on(seq - 1)
    made = own_grad(slice(0, 2 * own))
    r.own_work[1] = made[:, :own]
    launch_own(1)
    r.own_work[2] = made[:, own:]
    launch_own(2)
    hand_on(seqs - 1)

    sums = total_row(d_qkv[...].reshape(seqs * length, 3 * own).astype(WIDE))
    steps[0, 0:1, lanes(me)] = sums[:, 0:own]
    steps[0, 1:2, lanes(me)] = sums[:, 2 * own :]
    sum_bits = bits_of(sizes, SUM_ORDER)
    launch(2 * tiles + 4, reduce_whole(steps, r.vec_land, sems, take("send", 1), take("receive", len(sum_bits)), sum_bits))
    poll()

    for seq in range(seqs):
        dx_near[seq][0].wait_recv()
        dx_far[seq].wait_recv()

        summed = grad_b[seq * rows : (seq + 1) * rows, :] + dx_part[seq, place(me), :].astype(WIDE)
        summed = summed + r.dx_near[seq, 0].astype(WIDE) + r.dx_far[seq].astype(WIDE)
        r.dx[seq] = summed.astype(LOW)
        poll()
    stores.append(fetch(r.dx, dx_out))

    for name in sum(POLLS[place_of["poll"] :], ()):
        advance(name)
    while running:
        for name in list(running):
            advance(name)
    vec_out[...] = steps[len(sum_bits)]
    for copy in sum(last, pending):
        copy.wait_send()
    for copy in stores:
        copy.wait()
    assert (used["send"], used["receive"]) == semaphore_counts(sizes, seqs, width) and used["local"] == LOCALS


def widen_kernel(blocks, hid, dx, sums, shared, vec, *refs):
    hid_out, dx_out, wq, wk, wv, wo, wu, wd = refs[:8]
    rows_out, bu = refs[8:16], refs[16]
    low, shared_low, wide, shared_wide, hid_low, dx_low, sems = refs[17:]
    width = wq.shape[0]
    own = width // blocks
    units = sums.shape[0] // width
    tiles = (units - 1) // 2
    used = [0]

    def copy(src, dst):
        made = pltpu.make_async_copy(src, dst, sems.at[used[0]])
        used[0] += 1
        made.start()
        return made

    unit = lambda ref, at: ref.at[pl.ds(at * width, width)]
    loads = [copy(unit(sums, at), unit(low, at)) for at in range(units)]
    shared_loads = [copy(shared.at[kind], shared_low.at[kind]) for kind in range(3)]
    token_loads = [copy(hid, hid_low), copy(dx, dx_low)]
    stores = []
    targets = (
        [unit(wd, at) for at in range(tiles)] + [wu.at[:, pl.ds(at * width, width)] for at in range(tiles)] + [wo]
    )
    for at in range(units):
        loads[at].wait()

        def body(step, carry):
            part = span(at * width + step * 256, 256)
            wide[part, :] = low[part, :].astype(WIDE)
            return carry

        lax.fori_loop(0, width // 256, body, 0)
        stores.append(copy(unit(wide, at), targets[at]))
    for load in token_loads:
        load.wait()
    stores += [copy(hid_low, hid_out), copy(dx_low, dx_out)]
    for kind, target in enumerate((wv, wq, wk)):
        shared_loads[kind].wait()
        for block in range(blocks):
            shared_wide[kind, :, block * own : (block + 1) * own] = shared_low[kind, block].astype(WIDE)
        stores.append(copy(shared_wide.at[kind], target))
    for at, row in enumerate(rows_out):
        row[...] = vec[at, :]
    for at in range(tiles):
        bu[at * width : (at + 1) * width] = vec[len(rows_out) + at, :]
    for made in stores:
        made.wait()


def on_device(
    sizes,
    hidden_input,
    lengths,
    key_mask,
    query_weight,
    query_offset,
    key_weight,
    value_weight,
    value_offset,
    output_weight,
    output_offset,
    mixer_gain,
    mixer_shift,
    up_weight,
    up_offset,
    down_weight,
    down_offset,
    final_gain,
    final_shift,
    cotangent,
):
    seqs, rows, width = hidden_input.shape
    hidden = up_weight.shape[1]
    blocks = sizes["blk"]
    own = width // blocks
    scratch = layout_of(sizes, seqs, rows, width, hidden)
    anywhere = pl.BlockSpec(memory_space=pl.ANY)
    inside = pl.BlockSpec(memory_space=pltpu.VMEM)
    scalars = pl.BlockSpec(memory_space=pltpu.SMEM)
    scratch_shape = types.SimpleNamespace(**{name: shape for name, (shape, _) in scratch.items()})
    units = scratch_shape.work
    shared = (3, blocks, width, own)
    hid, dx, sums, own_sums, vec_sums = pl.pallas_call(
        functools.partial(layer_kernel, sizes, tuple(scratch)),
        out_shape=(
            jax.ShapeDtypeStruct(hidden_input.shape, LOW),
            jax.ShapeDtypeStruct(hidden_input.shape, LOW),
            jax.ShapeDtypeStruct(units, LOW),
            jax.ShapeDtypeStruct(shared, LOW),
            jax.ShapeDtypeStruct((VECTORS, width), WIDE),
        ),
        in_specs=[anywhere, scalars, inside] + [anywhere] * 16,
        out_specs=(anywhere,) * 4 + (inside,),
        scratch_shapes=[pltpu.VMEM(shape, kind) for shape, kind in scratch.values()]
        + [
            *(pltpu.SemaphoreType.DMA((count,)) for count in semaphore_counts(sizes, seqs, width)),
            pltpu.SemaphoreType.DMA((LOCALS,)),
        ],
        compiler_params=pltpu.CompilerParams(
            collective_id=0, has_side_effects=True, vmem_limit_bytes=60 * 1024 * 1024
        ),
    )(
        hidden_input,
        lengths,
        key_mask,
        query_weight,
        key_weight,
        value_weight,
        output_weight,
        up_weight,
        down_weight,
        cotangent,
        query_offset,
        value_offset,
        output_offset,
        mixer_gain,
        mixer_shift,
        down_offset,
        final_gain,
        final_shift,
        up_offset,
    )
    full = jax.ShapeDtypeStruct((width, width), WIDE)
    row = jax.ShapeDtypeStruct((width,), WIDE)
    flat = jax.ShapeDtypeStruct(hidden_input.shape, LOW)
    final = pl.pallas_call(
        functools.partial(widen_kernel, blocks),
        out_shape=(
            flat,
            flat,
            full,
            full,
            full,
            full,
            jax.ShapeDtypeStruct((width, hidden), WIDE),
            jax.ShapeDtypeStruct((hidden, width), WIDE),
        )
        + (row,) * 8
        + (jax.ShapeDtypeStruct((hidden,), WIDE),),
        in_specs=[anywhere] * 4 + [inside],
        out_specs=(anywhere,) * 8 + (inside,) * 9,
        scratch_shapes=[
            pltpu.VMEM(units, LOW),
            pltpu.VMEM(shared, LOW),
            pltpu.VMEM(units, WIDE),
            pltpu.VMEM((3, width, width), WIDE),
            pltpu.VMEM(hidden_input.shape, LOW),
            pltpu.VMEM(hidden_input.shape, LOW),
            pltpu.SemaphoreType.DMA((2 * units[0] // width + 10,)),
        ],
        compiler_params=pltpu.CompilerParams(vmem_limit_bytes=60 * 1024 * 1024),
    )(hid, dx, sums, own_sums, vec_sums)
    hid, dx, wq, wk, wv, wo, wu, wd, bq, bv, bo, g1, s1, bd, g2, s2, bu = final
    return hid, dx, wq, bq, wk, wv, bv, wo, bo, g1, s1, wu, bu, wd, bd, g2, s2


def solution(mesh):
    split = P("dp", "blk", None)
    in_specs = (split, P("dp"), P("dp", "blk")) + (P(),) * 15 + (split,)
    out_specs = (split, split) + (P(),) * 15
    return jax.shard_map(
        functools.partial(on_device, dict(mesh.shape)),
        mesh=mesh,
        in_specs=in_specs,
        out_specs=out_specs,
        check_vma=False,
    )
```

```python
import functools
import types

import jax
import jax.numpy as jnp
from jax import lax
from jax.experimental import pallas as pl
from jax.experimental.pallas import tpu as pltpu
from jax.sharding import PartitionSpec as P

HEAD = 64
EPSILON = 1e-06
MESH = pl.DeviceIdType.MESH
ROWS = 16
LOW = jnp.bfloat16
WIDE = jnp.float32
VECTORS = 16
LOCALS = 32

UNIT_ORDERS = ("cxaby", "caxby", "cabxy", "cxyab", "cabxy", "cxyab", "cyxab", "cyxz", "cxyz")
OWN_ORDERS = ("axb", "xz", "axb")
SUM_ORDER = "cxyab"
POLLS = (
    (),
    (),
    (),
    (),
    (),
    (),
    (),
    (),
    (0, 1,),
    (2,),
    (3,),
    (),
    (),
    (),
    (),
    (),
    (8, 4, 5, 6, 7,),
    (0, 1,),
    (),
    (3, 2,),
    (),
    (),
    (),
    (),
    (8,),
    (4, 6,),
    (0,),
    (),
    (5,),
    (9, 7, 1, 3, 2,),
    (10, 11, 6, 8,),
    (9, 4, 5, 0, 12, 3, 1, 7,),
    (11, 10, 2, 6,),
    (9, 8, 4, 5, 12, 3,),
    (0, 1, 7, 2, 11, 10, 6, 4, 9, 12, 0, 1, 2, 8, 5, 4, 3, 10, 9, 12, 7, 2, 11, 6, 8, 4, 3, 0, 9, 1, 7, 10, 5, 11, 10, 12, 6, 3, 8, 2, 1, 0, 9, 8, 5, 6, 9, 11, 4, 7, 3, 7, 5, 2, 3, 0, 2, 6, 1, 0, 6, 1, 11, 5, 4, 11, 5, 4,),
)


def stages_of(sizes):
    def split(step, rest):
        found = []
        while rest > 1:
            radix = 4 if rest % 4 == 0 else 2
            found.append(("dp", step, radix))
            step *= radix
            rest //= radix
        return found

    dp = sizes["dp"]
    return dict(
        c=[("blk", 1, 2)], y=[("blk", 2, 2)], x=[("dp", 1, 2)], a=[("dp", 2, 2)], b=split(4, dp // 4), z=split(2, dp // 2)
    )


def bits_of(sizes, letters):
    bits = []
    for letter in letters:
        for axis, step, radix in stages_of(sizes)[letter]:
            bits += [(axis, step, 2)] if radix == 2 else [(axis, step, 2), (axis, 2 * step, 2)]
    return bits


def digit_of(stage):
    axis, step, radix = stage
    index = lax.axis_index(axis)
    digit = lax.rem(lax.div(index, step), radix)
    others = []
    for offset in range(1, radix):
        other = lax.rem(digit + offset, radix)
        others.append((other, {axis: index + (other - digit) * step}))
    return digit, others


def flip(index, step):
    return index + step - 2 * step * lax.rem(lax.div(index, step), 2)


def aligned(start, unit):
    return start if isinstance(start, int) else pl.multiple_of(start, unit)


def span(start, count, unit=ROWS):
    return pl.ds(aligned(start, unit), count)


def send(src, dst, sems, at, peer, land_at=None):
    sends, receives = sems
    copy = pltpu.make_async_remote_copy(
        src_ref=src,
        dst_ref=dst,
        send_sem=sends.at[at],
        recv_sem=receives.at[at if land_at is None else land_at],
        device_id=peer,
        device_id_type=MESH,
    )
    copy.start()
    return copy


def plan_of(sizes, rows, letters):
    plan = []
    size = rows
    for letter in letters:
        for axis, step, radix in stages_of(sizes)[letter]:
            if size % (radix * ROWS) == 0:
                size //= radix
                plan.append(((axis, step, radix), True, size))
                continue
            bit = step
            while bit < step * radix:
                split = size % (2 * ROWS) == 0
                size = size // 2 if split else size
                plan.append(((axis, bit, 2), split, size))
                bit *= 2
    return plan


def landing_rows(sizes, rows, letters):
    return sum(size * (stage[2] - 1) for stage, _, size in plan_of(sizes, rows, letters))


def semaphores_of(sizes, rows, letters):
    peers = [stage[2] - 1 for stage, _, _ in plan_of(sizes, rows, letters)]
    return max(peers), 2 * sum(peers)


def semaphore_counts(sizes, seqs, width):
    sends, receives = 3 + 6 * seqs + 1, 3 + 12 * seqs + len(bits_of(sizes, SUM_ORDER))
    for letters in UNIT_ORDERS:
        sending, receiving = semaphores_of(sizes, width, letters)
        sends, receives = sends + sending, receives + receiving
    for letters in OWN_ORDERS:
        sending, receiving = semaphores_of(sizes, width, letters)
        sends, receives = sends + max(sending, 3), receives + receiving + 3
    return sends, receives


def add_rows(first, first_at, land, land_at, terms, out, out_at, count):
    total = first[span(first_at, count)].astype(WIDE)
    for term in range(terms):
        total = total + land[span(land_at + term * count, count)].astype(WIDE)
    out[span(out_at, count)] = total.astype(out.dtype)


def reduce_rows(sizes, work, land, out, sems, base, rows, land_at, send_at, receive_at, letters, sent):
    plan = plan_of(sizes, rows, letters)
    start = base
    trail = []
    for level, (stage, split, count) in enumerate(plan):
        digit, others = digit_of(stage)
        keep = start + digit * count if split else start
        for copy in sent:
            copy.wait_send()
        sent.clear()
        for offset, (other, peer) in enumerate(others):
            give = start + other * count if split else start
            slot = len(others) - 1 - offset
            sent.append(
                send(
                    work.at[span(give, count)],
                    land.at[span(land_at + slot * count, count)],
                    sems,
                    send_at + offset,
                    peer,
                    receive_at + slot,
                )
            )
        yield
        for copy in sent:
            copy.wait_recv()
        if split:
            trail.append((others, keep, count))
        else:
            for copy in sent:
                copy.wait_send()
            sent.clear()
        target = out if level == len(plan) - 1 else work
        add_rows(work, keep, land, land_at, len(others), target, keep, count)
        land_at += count * len(others)
        receive_at += len(others)
        start = keep
    for others, mine, count in reversed(trail):
        part = out.at[span(mine, count)]
        for copy in sent:
            copy.wait_send()
        sent.clear()
        for offset, (_, peer) in enumerate(others):
            sent.append(send(part, part, sems, send_at + offset, peer, receive_at + len(others) - 1 - offset))
        yield
        for copy in sent:
            copy.wait_recv()
        receive_at += len(others)


def reduce_whole(steps, land, sems, send_at, receive_at, bits):
    for level, bit in enumerate(bits):
        copy = send(steps.at[level], land.at[level], sems, send_at, digit_of(bit)[1][0][1], receive_at + level)
        yield
        copy.wait()
        steps[level + 1] = steps[level] + land[level]


def share_blocks(slots, sems, send_at, receive_at, me, sent):
    near, far = flip(me, 1), flip(me, 2)
    for copy in sent:
        copy.wait_send()
    across = send(slots.at[me], slots.at[me], sems, send_at, {"blk": far}, receive_at)
    beside = send(slots.at[me], slots.at[me], sems, send_at + 1, {"blk": near}, receive_at + 1)
    yield
    across.wait_recv()
    onward = send(slots.at[far], slots.at[far], sems, send_at + 2, {"blk": near}, receive_at + 2)
    yield
    beside.wait_recv()
    onward.wait_recv()
    sent[:] = [across, beside, onward]


def dot(left, right):
    return jnp.dot(left, right, preferred_element_type=WIDE)


def dot_right_t(left, right):
    return lax.dot_general(left, right, (((1,), (1,)), ((), ())), preferred_element_type=WIDE)


def dot_left_t(left, right):
    return lax.dot_general(left, right, (((0,), (0,)), ((), ())), preferred_element_type=WIDE)


def fold(values):
    rows, width = values.shape
    return jnp.sum(values.reshape(rows // 8, 8, width), axis=0)


def mean_of(values):
    return jnp.mean(values, axis=-1, keepdims=True)


def norm_back(upstream, scaled, inverse, gain):
    inner = upstream * gain
    return inverse * (inner - mean_of(inner) - scaled * mean_of(inner * scaled))


def layout_of(sizes, seqs, rows, width, hidden):
    tokens = seqs * rows
    blocks = sizes["blk"]
    length = rows * blocks
    own = width // blocks
    heads = own // HEAD
    levels = len(bits_of(sizes, SUM_ORDER))
    units = 2 * (hidden // width) + 1
    land_total = sum(landing_rows(sizes, width, UNIT_ORDERS[at]) for at in range(units))
    own_land = max(landing_rows(sizes, width, order) for order in OWN_ORDERS)
    return dict(
        x_all=((seqs, length, width), LOW),
        x_own=((seqs, rows, width), LOW),
        cot=((seqs, rows, width), LOW),
        w_qkv=((width, 3 * own), LOW),
        w_o=((width, width), LOW),
        w_up=((width, hidden), LOW),
        w_down=((hidden, width), LOW),
        vec_low=((VECTORS * width,), LOW),
        vec=((VECTORS, width), WIDE),
        flags=((blocks, 8, rows), WIDE),
        qkv=((seqs, length, 3 * own), LOW),
        probs=((seqs * heads, length, length), LOW),
        o_wide=((seqs, length, own), WIDE),
        o_send=((seqs, length, own), LOW),
        o_all=((seqs, rows, width), LOW),
        total=((tokens, width), WIDE),
        scaled=((tokens, width), WIDE),
        inverse=((tokens, 128), WIDE),
        normed=((tokens, width), WIDE),
        normed_low=((tokens, width), LOW),
        active=((tokens, hidden), LOW),
        slope=((tokens, hidden), WIDE),
        grad_b=((tokens, width), WIDE),
        grad_y=((tokens, width), LOW),
        grad_z=((tokens, hidden), LOW),
        grad_t=((tokens, width), LOW),
        do_send=((seqs, rows, width), LOW),
        do_all=((seqs, length, own), LOW),
        grad_s=((heads, length, length), LOW),
        d_qkv=((seqs, length, 3 * own), LOW),
        dx_part=((seqs, length, width), LOW),
        dx_near=((seqs, 2, rows, width), LOW),
        dx_chip=((seqs, rows, width), LOW),
        hid=((seqs, rows, width), LOW),
        dx=((seqs, rows, width), LOW),
        out=((units * width, width), LOW),
        own_out=((3, blocks, width, own), LOW),
        dx_far=((seqs, rows, width), LOW),
        work=((units * width, width), LOW),
        land=((land_total, width), LOW),
        own_work=((3, width, own), LOW),
        own_land=((3, own_land, own), LOW),
        steps=((levels + 1, VECTORS, width), WIDE),
        vec_land=((levels, VECTORS, width), WIDE),
    )


def layer_kernel(sizes, names, *refs):
    x, lengths, mask, wq, wk, wv, wo, wu, wd, cotangent = refs[:10]
    vectors_in = refs[10:19]
    hid_out, dx_out, sums_out, own_sums_out, vec_out = refs[19:24]
    r = types.SimpleNamespace(**dict(zip(names, refs[24:-3], strict=True)))
    sems = refs[-3:-1]
    local = refs[-1]
    x_all, qkv, vec, steps = r.x_all, r.qkv, r.vec, r.steps
    seqs, rows, width = r.x_own.shape
    tokens = seqs * rows
    length = x_all.shape[1]
    blocks = sizes["blk"]
    own = width // blocks
    heads = own // HEAD
    hidden = r.w_up.shape[1]
    tiles = hidden // width
    scale = HEAD ** (-0.5)
    me = lax.axis_index("blk")
    near, far = flip(me, 1), flip(me, 2)
    cross = flip(far, 1)
    peers = (near, far, cross)
    place = lambda index: span(index * rows, rows, rows)
    lanes = lambda index: span(index * own, own, own)

    used = {"send": 0, "receive": 0, "local": 0}
    pending, stores = [], []

    def take(which, count):
        at = used[which]
        used[which] += count
        return at

    def slot(count):
        return take("send", count), take("receive", count)

    def send_in(pair, offset, src, dst, peer):
        return send(src, dst, sems, pair[0] + offset, {"blk": peer}, pair[1] + offset)

    def fetch(src, dst):
        copy = pltpu.make_async_copy(src, dst, local.at[used["local"]])
        used["local"] += 1
        copy.start()
        return copy

    loads_x = [
        fetch(x, x_all.at[:, place(me), :]),
        fetch(x, r.x_own),
    ]
    loads_w = [
        fetch(weight.at[:, lanes(me)], r.w_qkv.at[:, pl.ds(at * own, own)])
        for at, weight in enumerate((wq, wk, wv))
    ]
    load_vectors = []
    at = 0
    for vector in vectors_in:
        count = vector.shape[0]
        load_vectors.append(fetch(vector, r.vec_low.at[pl.ds(at, count)]))
        at += count
    load_o = fetch(wo, r.w_o)
    load_up = fetch(wu, r.w_up)
    load_down = fetch(wd, r.w_down)
    load_cot = fetch(cotangent, r.cot)

    positions = me * rows + lax.broadcasted_iota(jnp.int32, (1, rows), 1)
    flag_rows = []
    for seq in range(seqs):
        good = (mask[seq : seq + 1, :] == 1) & (positions < lengths[seq])
        flag_rows.append(jnp.where(good, 0.0, -1000000000.0).astype(WIDE))
    flag_rows.append(jnp.zeros((8 - seqs, rows), WIDE))
    r.flags[me] = jnp.concatenate(flag_rows, axis=0)

    barrier = pltpu.get_barrier_semaphore()
    greeted = [{"blk": peer} for peer in peers] + [
        peer for letter in "xz" for stage in stages_of(sizes)[letter] for _, peer in digit_of(stage)[1]
    ]
    for peer in greeted:
        pl.semaphore_signal(barrier, inc=1, device_id=peer, device_id_type=MESH)
    pl.semaphore_wait(barrier, len(greeted))

    at_far, at_near, at_on, at_flag = slot(seqs), slot(seqs), slot(seqs), slot(len(peers))
    flag_copies = [
        send_in(at_flag, index, r.flags.at[me], r.flags.at[me], peer)
        for index, peer in enumerate(peers)
    ]
    x_far, x_near, x_on = [], [], []
    for seq in range(seqs):
        target = x_all.at[seq, place(me), :]
        x_far.append(send_in(at_far, seq, x.at[seq], target, far))
        x_near.append(send_in(at_near, seq, x.at[seq], target, near))
    pending += flag_copies

    def forward_x(seq):
        x_far[seq].wait_recv()
        block = x_all.at[seq, place(far), :]
        x_on.append(send_in(at_on, seq, block, block, near))

    lane = lax.broadcasted_iota(jnp.int32, (1, own), 1)
    of_head = [(lane >= head * HEAD) & (lane < (head + 1) * HEAD) for head in range(heads)]
    only = lambda values, head: jnp.where(of_head[head], values.astype(WIDE), 0.0)
    for copy in load_vectors:
        copy.wait()
    for at in range(8 + tiles):
        vec[at : at + 1, :] = r.vec_low[at * width : (at + 1) * width].astype(WIDE).reshape(1, width)
    bias_q = vec[0:1, lanes(me)]
    bias_v = vec[1:2, lanes(me)]
    bias_qkv = jnp.concatenate([bias_q, jnp.zeros_like(bias_q), bias_v], axis=1)
    o_all, o_send = r.o_all, r.o_send
    at_o = slot(seqs * len(peers))
    o_copies = []

    def project(seq):
        qkv[seq] = (dot(x_all[seq], r.w_qkv[...]) + bias_qkv).astype(LOW)

    column = lax.broadcasted_iota(jnp.int32, (length, length), 1)
    row = lax.broadcasted_iota(jnp.int32, (length, length), 0)

    def attend(seq):
        keys = qkv[seq, :, own : 2 * own]
        values = qkv[seq, :, 2 * own :]
        key_bias = jnp.concatenate([r.flags[block, seq : seq + 1, :] for block in range(blocks)], axis=1)
        bias = jnp.where(column == row, 0.0, key_bias)
        query = qkv[seq, :, 0:own].astype(WIDE) * scale
        joined = None
        for head in range(heads):
            scores = dot_right_t(only(query, head).astype(LOW), keys) + bias
            raised = jnp.exp(scores - jnp.max(scores, axis=-1, keepdims=True))
            probs = (raised / jnp.sum(raised, axis=-1, keepdims=True)).astype(LOW)
            r.probs[seq * heads + head] = probs
            result = dot(probs, values)
            joined = result if joined is None else jnp.where(of_head[head], result, joined)
        r.o_wide[seq] = joined
        o_send[seq] = joined.astype(LOW)
        for index, peer in enumerate(peers):
            part = o_send.at[seq, place(peer), :]
            o_copies.append(send_in(at_o, seq * len(peers) + index, part, o_all.at[seq, :, lanes(me)], peer))
        o_all[seq, :, lanes(me)] = o_send[seq, place(me), :]

    for copy in loads_w:
        copy.wait()
    for copy in loads_x:
        copy.wait()
    for copy in flag_copies:
        copy.wait_recv()
    forward_x(0)
    for seq in range(seqs):
        x_near[seq].wait_recv()
        x_on[seq].wait_recv()
        project(seq)
        if seq + 1 < seqs:
            forward_x(seq + 1)
        attend(seq)

    total, scaled, inverse = r.total, r.scaled, r.inverse
    normed, normed_low = r.normed, r.normed_low
    active, slope = r.active, r.slope
    grad_b, grad_y = r.grad_b, r.grad_y
    wide_row = lambda at: vec[at : at + 1, :]
    total_row = lambda values: jnp.sum(fold(values), axis=0, keepdims=True)
    flat = lambda ref: ref[...].reshape(tokens, width)
    steps[0] = jnp.zeros((VECTORS, width), WIDE)

    def normalize(values):
        center = values - mean_of(values)
        inv = lax.rsqrt(mean_of(center * center) + EPSILON)
        return center * inv, inv

    def feed_forward(first, count):
        some = slice(first, first + count)
        size = count * rows
        part = pl.ds(first * rows, size)
        mixed = o_all[some].reshape(size, width)
        made, inv = normalize(
            r.x_own[some].reshape(size, width).astype(WIDE) + dot(mixed, r.w_o[...]) + wide_row(2)
        )
        scaled[part, :] = made
        inverse[part, :] = jnp.broadcast_to(inv, (size, 128))
        result = made * wide_row(3) + wide_row(4)
        normed[part, :] = result
        normed_low[part, :] = result.astype(LOW)
        step = min(hidden, 2 * width * (2 * rows) // size)
        for at in range(0, hidden, step):
            columns = slice(at, at + step)
            offset = jnp.concatenate([wide_row(8 + tile) for tile in range(at // width, (at + step) // width)], axis=1)
            z = dot(normed_low[part, :], r.w_up[:, columns]) + offset
            below = 0.5 * (1.0 + lax.erf(z * 0.7071067811865476))
            active[part, columns] = (z * below).astype(LOW)
            slope[part, columns] = below + z * (0.3989422804014327 * jnp.exp(-0.5 * z * z))
        made, inv = normalize(normed[part, :] + dot(active[part, :], r.w_down[...]) + wide_row(5))
        r.hid[some] = (made * wide_row(6) + wide_row(7)).astype(LOW).reshape(count, rows, width)
        upstream = r.cot[some].reshape(size, width).astype(WIDE)
        back = norm_back(upstream, made, inv, wide_row(6))
        grad_b[part, :] = back
        rounded = back.astype(LOW)
        grad_y[part, :] = rounded
        steps[0, 7:8, :] += total_row(upstream)
        steps[0, 6:7, :] += total_row(upstream * made)
        steps[0, 5:6, :] += total_row(rounded.astype(WIDE))

    for copy in (load_o, load_up, load_down, load_cot):
        copy.wait()
    arrived = 0
    for first, count in ((0, seqs - 1), (seqs - 1, 1)) if seqs > 1 else ((0, 1),):
        for copy in o_copies[arrived : (first + count) * len(peers)]:
            copy.wait_recv()
        arrived = (first + count) * len(peers)
        feed_forward(first, count)
    stores.append(fetch(r.hid, hid_out))

    work = r.work
    running = {}
    last = []
    place_of = {"land": 0, "poll": 0}

    def launch(name, item):
        running[name] = item
        advance(name)

    def advance(name):
        if name in running and next(running[name], True) is not None:
            del running[name]

    def launch_unit(unit):
        letters = UNIT_ORDERS[unit]
        sending, receiving = semaphores_of(sizes, width, letters)
        ats = take("send", sending), take("receive", receiving)
        land_at = place_of["land"]
        place_of["land"] += landing_rows(sizes, width, letters)
        sent = []
        last.append(sent)
        def item():
            yield from reduce_rows(sizes, work, r.land, r.out, sems, unit * width, width, land_at, *ats, letters, sent)
            stores.append(fetch(r.out.at[cut(unit)], sums_out.at[cut(unit)]))

        launch(unit, item())

    def launch_own(kind):
        letters = OWN_ORDERS[kind]
        sending, receiving = semaphores_of(sizes, width, letters)
        ats = take("send", max(sending, 3)), take("receive", receiving)
        blocks_at = take("receive", 3)
        slots = r.own_out.at[kind]
        sent = []
        last.append(sent)

        def item():
            parts = r.own_work.at[kind], r.own_land.at[kind], slots.at[me]
            yield from reduce_rows(sizes, *parts, sems, 0, width, 0, *ats, letters, sent)
            yield from share_blocks(slots, sems, ats[0], blocks_at, me, sent)
            stores.append(fetch(slots, own_sums_out.at[kind]))

        launch(2 * tiles + 1 + kind, item())

    def poll():
        at = place_of["poll"]
        place_of["poll"] += 1
        for name in POLLS[at] if at < len(POLLS) else ():
            advance(name)

    cut = lambda tile: slice(tile * width, (tile + 1) * width)
    for tile in range(tiles):
        work[cut(tile), :] = dot_left_t(active[:, cut(tile)], grad_y[...]).astype(LOW)
        launch_unit(tile)
        poll()

    grad_z = r.grad_z

    for tile in range(tiles):
        made = (dot_right_t(grad_y[...], r.w_down[cut(tile), :]) * slope[:, cut(tile)]).astype(LOW)
        grad_z[:, cut(tile)] = made
        steps[0, 8 + tile : 9 + tile, :] = total_row(made.astype(WIDE))
        poll()
    upstream = grad_b[...] + dot_right_t(grad_z[...], r.w_up[...])
    total[...] = upstream
    poll()
    upstream = total[...]

    grad_t = r.grad_t
    made = scaled[...]
    back = norm_back(upstream, made, inverse[:, 0:1], wide_row(3))
    grad_b[...] = back
    rounded = back.astype(LOW)
    grad_t[...] = rounded
    steps[0, 4:5, :] = total_row(upstream)
    steps[0, 3:4, :] = total_row(upstream * made)
    steps[0, 2:3, :] = total_row(rounded.astype(WIDE))
    poll()

    do_send, do_all = r.do_send, r.do_all
    for copy in x_far + x_near + x_on:
        copy.wait_send()
    at_do = at_far[0], take("receive", seqs * len(peers))
    do_copies = []
    made = dot_right_t(grad_t[...], r.w_o[...]).astype(LOW)
    do_send[...] = made.reshape(seqs, rows, width)
    for seq in range(seqs):
        do_copies.append(
            [
                send_in(
                    at_do,
                    seq * len(peers) + index,
                    do_send.at[seq, :, lanes(peer)],
                    do_all.at[seq, place(me), :],
                    peer,
                )
                for index, peer in enumerate(peers)
            ]
        )
        do_all[seq, place(me), :] = do_send[seq, :, lanes(me)]
        pending += do_copies[-1]

    poll()
    work[2 * hidden :, :] = dot_left_t(o_all[...].reshape(tokens, width), grad_t[...]).astype(LOW)
    launch_unit(2 * tiles)
    poll()
    for tile in range(tiles):
        work[cut(tiles + tile), :] = dot_left_t(normed_low[...], grad_z[:, cut(tile)]).astype(LOW)
        launch_unit(tiles + tile)
        poll()

    d_qkv, grad_s, dx_part = r.d_qkv, r.grad_s, r.dx_part
    for copy in o_copies:
        copy.wait_send()
    at_dx_near = at_o[0], take("receive", 2 * seqs)
    at_dx_far = at_o[0] + 2 * seqs, take("receive", seqs)
    dx_near, dx_far = [], []

    def value_back(seq):
        upstream = do_all[seq].astype(WIDE)
        grads = [
            dot_left_t(r.probs[seq * heads + head], only(upstream, head).astype(LOW)) for head in range(heads)
        ]
        d_qkv[seq, :, 2 * own :] = functools.reduce(jnp.add, grads).astype(LOW)

    def score_back(seq):
        values = qkv[seq, :, 2 * own :]
        upstream = do_all[seq].astype(WIDE)
        inner = upstream * r.o_wide[seq]
        for head in range(heads):
            delta = jnp.sum(only(inner, head), axis=-1, keepdims=True)
            prob_grad = dot_right_t(only(upstream, head).astype(LOW), values)
            probs = r.probs[seq * heads + head].astype(WIDE)
            grad_s[head] = (probs * (prob_grad - delta)).astype(LOW)

    def query_key_back(seq):
        queries_wide = qkv[seq, :, 0:own].astype(WIDE) * scale
        keys_wide = qkv[seq, :, own : 2 * own].astype(WIDE) * scale
        query_grads, key_grads = [], []
        for head in range(heads):
            query_grads.append(dot(grad_s[head], only(keys_wide, head).astype(LOW)))
            key_grads.append(dot_left_t(grad_s[head], only(queries_wide, head).astype(LOW)))
        d_qkv[seq, :, 0:own] = functools.reduce(jnp.add, query_grads).astype(LOW)
        d_qkv[seq, :, own : 2 * own] = functools.reduce(jnp.add, key_grads).astype(LOW)

    def input_back(seq):
        dx_part[seq] = dot_right_t(d_qkv[seq], r.w_qkv[...]).astype(LOW)
        dx_near.append(
            [
                send_in(at_dx_near, 2 * seq + at, dx_part.at[seq, place(block), :], r.dx_near.at[seq, at], near)
                for at, block in enumerate((near, cross))
            ]
        )
        pending.extend(dx_near[-1])

    def own_grad(columns):
        tokens_in = x_all[...].reshape(seqs * length, width)
        return dot_left_t(tokens_in, d_qkv[:, :, columns].reshape(seqs * length, -1)).astype(LOW)

    def hand_on(seq):
        dx_near[seq][1].wait_recv()
        summed = dx_part[seq, place(far), :].astype(WIDE) + r.dx_near[seq, 1].astype(WIDE)
        r.dx_chip[seq] = summed.astype(LOW)
        dx_far.append(send_in(at_dx_far, seq, r.dx_chip.at[seq], r.dx_far.at[seq], far))
        pending.append(dx_far[-1])

    for seq in range(seqs):
        for copy in do_copies[seq]:
            copy.wait_recv()
        value_back(seq)
        poll()
    r.own_work[0] = own_grad(slice(2 * own, None))
    launch_own(0)
    poll()
    for seq in range(seqs):
        score_back(seq)
        poll()
        query_key_back(seq)
        poll()
    made = own_grad(slice(0, 2 * own))
    r.own_work[1] = made[:, :own]
    launch_own(1)
    r.own_work[2] = made[:, own:]
    launch_own(2)
    poll()
    for seq in range(seqs):
        input_back(seq)
        poll()
        if seq > 0:
            hand_on(seq - 1)
    hand_on(seqs - 1)

    sums = total_row(d_qkv[...].reshape(seqs * length, 3 * own).astype(WIDE))
    steps[0, 0:1, lanes(me)] = sums[:, 0:own]
    steps[0, 1:2, lanes(me)] = sums[:, 2 * own :]
    sum_bits = bits_of(sizes, SUM_ORDER)
    launch(2 * tiles + 4, reduce_whole(steps, r.vec_land, sems, take("send", 1), take("receive", len(sum_bits)), sum_bits))
    poll()

    for seq in range(seqs):
        dx_near[seq][0].wait_recv()
        dx_far[seq].wait_recv()

        summed = grad_b[seq * rows : (seq + 1) * rows, :] + dx_part[seq, place(me), :].astype(WIDE)
        summed = summed + r.dx_near[seq, 0].astype(WIDE) + r.dx_far[seq].astype(WIDE)
        r.dx[seq] = summed.astype(LOW)
        poll()
    stores.append(fetch(r.dx, dx_out))

    for name in sum(POLLS[place_of["poll"] :], ()):
        advance(name)
    while running:
        for name in list(running):
            advance(name)
    vec_out[...] = steps[len(sum_bits)]
    for copy in sum(last, pending):
        copy.wait_send()
    for copy in stores:
        copy.wait()
    assert (used["send"], used["receive"]) == semaphore_counts(sizes, seqs, width) and used["local"] == LOCALS


def widen_kernel(blocks, hid, dx, sums, shared, vec, *refs):
    hid_out, dx_out, wq, wk, wv, wo, wu, wd = refs[:8]
    rows_out, bu = refs[8:16], refs[16]
    low, shared_low, wide, shared_wide, hid_low, dx_low, flat_vec, sems = refs[17:]
    width = wq.shape[0]
    own = width // blocks
    units = sums.shape[0] // width
    tiles = (units - 1) // 2
    used = [0]

    def copy(src, dst):
        made = pltpu.make_async_copy(src, dst, sems.at[used[0]])
        used[0] += 1
        made.start()
        return made

    unit = lambda ref, at: ref.at[pl.ds(at * width, width)]
    loads = [copy(unit(sums, at), unit(low, at)) for at in range(units)]
    shared_loads = [copy(shared.at[kind], shared_low.at[kind]) for kind in range(3)]
    token_loads = [copy(hid, hid_low), copy(dx, dx_low)]
    stores = []
    count = len(rows_out)
    for at in range(count + tiles):
        flat_vec[at * width : (at + 1) * width] = vec[at, :]
    for at, row in enumerate(rows_out):
        stores.append(copy(flat_vec.at[pl.ds(at * width, width)], row))
    stores.append(copy(flat_vec.at[pl.ds(count * width, tiles * width)], bu))
    targets = (
        [unit(wd, at) for at in range(tiles)] + [wu.at[:, pl.ds(at * width, width)] for at in range(tiles)] + [wo]
    )
    for at in range(units):
        loads[at].wait()

        def body(step, carry):
            part = span(at * width + step * 256, 256)
            wide[part, :] = low[part, :].astype(WIDE)
            return carry

        lax.fori_loop(0, width // 256, body, 0)
        stores.append(copy(unit(wide, at), targets[at]))
    for load in token_loads:
        load.wait()
    stores += [copy(hid_low, hid_out), copy(dx_low, dx_out)]
    for kind, target in enumerate((wv, wq, wk)):
        shared_loads[kind].wait()
        for block in range(blocks):
            shared_wide[kind, :, block * own : (block + 1) * own] = shared_low[kind, block].astype(WIDE)
        stores.append(copy(shared_wide.at[kind], target))
    for made in stores:
        made.wait()


def on_device(
    sizes,
    hidden_input,
    lengths,
    key_mask,
    query_weight,
    query_offset,
    key_weight,
    value_weight,
    value_offset,
    output_weight,
    output_offset,
    mixer_gain,
    mixer_shift,
    up_weight,
    up_offset,
    down_weight,
    down_offset,
    final_gain,
    final_shift,
    cotangent,
):
    seqs, rows, width = hidden_input.shape
    hidden = up_weight.shape[1]
    blocks = sizes["blk"]
    own = width // blocks
    scratch = layout_of(sizes, seqs, rows, width, hidden)
    anywhere = pl.BlockSpec(memory_space=pl.ANY)
    inside = pl.BlockSpec(memory_space=pltpu.VMEM)
    scalars = pl.BlockSpec(memory_space=pltpu.SMEM)
    scratch_shape = types.SimpleNamespace(**{name: shape for name, (shape, _) in scratch.items()})
    units = scratch_shape.work
    shared = (3, blocks, width, own)
    hid, dx, sums, own_sums, vec_sums = pl.pallas_call(
        functools.partial(layer_kernel, sizes, tuple(scratch)),
        out_shape=(
            jax.ShapeDtypeStruct(hidden_input.shape, LOW),
            jax.ShapeDtypeStruct(hidden_input.shape, LOW),
            jax.ShapeDtypeStruct(units, LOW),
            jax.ShapeDtypeStruct(shared, LOW),
            jax.ShapeDtypeStruct((VECTORS, width), WIDE),
        ),
        in_specs=[anywhere, scalars, inside] + [anywhere] * 16,
        out_specs=(anywhere,) * 4 + (inside,),
        scratch_shapes=[pltpu.VMEM(shape, kind) for shape, kind in scratch.values()]
        + [
            *(pltpu.SemaphoreType.DMA((count,)) for count in semaphore_counts(sizes, seqs, width)),
            pltpu.SemaphoreType.DMA((LOCALS,)),
        ],
        compiler_params=pltpu.CompilerParams(
            collective_id=0, has_side_effects=True, vmem_limit_bytes=60 * 1024 * 1024
        ),
    )(
        hidden_input,
        lengths,
        key_mask,
        query_weight,
        key_weight,
        value_weight,
        output_weight,
        up_weight,
        down_weight,
        cotangent,
        query_offset,
        value_offset,
        output_offset,
        mixer_gain,
        mixer_shift,
        down_offset,
        final_gain,
        final_shift,
        up_offset,
    )
    full = jax.ShapeDtypeStruct((width, width), WIDE)
    row = jax.ShapeDtypeStruct((width,), WIDE)
    flat = jax.ShapeDtypeStruct(hidden_input.shape, LOW)
    final = pl.pallas_call(
        functools.partial(widen_kernel, blocks),
        out_shape=(
            flat,
            flat,
            full,
            full,
            full,
            full,
            jax.ShapeDtypeStruct((width, hidden), WIDE),
            jax.ShapeDtypeStruct((hidden, width), WIDE),
        )
        + (row,) * 8
        + (jax.ShapeDtypeStruct((hidden,), WIDE),),
        in_specs=[anywhere] * 4 + [inside],
        out_specs=(anywhere,) * 17,
        scratch_shapes=[
            pltpu.VMEM(units, LOW),
            pltpu.VMEM(shared, LOW),
            pltpu.VMEM(units, WIDE),
            pltpu.VMEM((3, width, width), WIDE),
            pltpu.VMEM(hidden_input.shape, LOW),
            pltpu.VMEM(hidden_input.shape, LOW),
            pltpu.VMEM((VECTORS * width,), WIDE),
            pltpu.SemaphoreType.DMA((2 * units[0] // width + 19,)),
        ],
        compiler_params=pltpu.CompilerParams(vmem_limit_bytes=60 * 1024 * 1024),
    )(hid, dx, sums, own_sums, vec_sums)
    hid, dx, wq, wk, wv, wo, wu, wd, bq, bv, bo, g1, s1, bd, g2, s2, bu = final
    return hid, dx, wq, bq, wk, wv, bv, wo, bo, g1, s1, wu, bu, wd, bd, g2, s2


def solution(mesh):
    split = P("dp", "blk", None)
    in_specs = (split, P("dp"), P("dp", "blk")) + (P(),) * 15 + (split,)
    out_specs = (split, split) + (P(),) * 15
    return jax.shard_map(
        functools.partial(on_device, dict(mesh.shape)),
        mesh=mesh,
        in_specs=in_specs,
        out_specs=out_specs,
        check_vma=False,
    )
```

```python
import functools
import types

import jax
import jax.numpy as jnp
from jax import lax
from jax.experimental import pallas as pl
from jax.experimental.pallas import tpu as pltpu
from jax.sharding import PartitionSpec as P

HEAD = 64
EPSILON = 1e-06
MESH = pl.DeviceIdType.MESH
ROWS = 16
LOW = jnp.bfloat16
WIDE = jnp.float32
VECTORS = 16
HALVES = 2

UNIT_ORDERS = ("cxzy", "caxby", "cyxab", "cabyx", "cayxb", "cxaby", "cxyab", "caxyb", "cyxab", "caxyb", "caxyb", "cyxab", "cxayb", "cyaxb", "cxayb", "cxyab", "cxyab", "caxyb")
OWN_ORDERS = ("xab", "xab", "xab")
SUM_ORDER = "cxyab"
POLLS = (
    (),
    (),
    (),
    (),
    (),
    (0,),
    (1,),
    (2,),
    (3, 4, 5,),
    (6, 7,),
    (),
    (),
    (),
    (),
    (),
    (),
    (16, 0, 17, 1, 8, 9, 2, 10, 11, 12, 5, 13, 3, 14, 15,),
    (),
    (6, 4,),
    (),
    (16, 7,),
    (1,),
    (2,),
    (0,),
    (8,),
    (17, 12,),
    (),
    (11,),
    (9, 14,),
    (13,),
    (10, 15, 6,),
    (5, 7,),
    (18, 4, 16, 0, 3, 2, 1,),
    (12, 8, 14, 17, 15, 7, 13, 11,),
    (6, 9, 5, 21, 18, 16, 19, 22, 0, 3, 20, 8, 2, 1, 15, 10, 4, 11, 7, 13, 6, 21, 18, 22, 19, 16, 0, 20, 3, 2, 8, 0, 1, 15, 22, 12, 4, 14, 6, 17, 11, 9, 18, 5, 13, 2, 10, 7, 16, 1, 21, 19, 3, 4, 8, 15, 6, 20, 11, 12, 18, 13, 2, 14, 7, 16, 17, 8, 2, 4, 9, 1, 15, 5, 12, 21, 6, 10, 1, 19, 11, 6, 3, 20, 16, 18, 13, 14, 17, 16, 15, 18, 7, 8, 15, 19, 9, 7, 10, 4, 8, 5, 20, 4, 11, 12, 17, 21, 11, 13, 9, 3, 10, 13, 14, 3, 5, 19, 17, 5, 12, 19, 9, 17, 12, 14, 9, 20, 10, 14, 20, 10,),
)


def stages_of(sizes):
    def split(step, rest):
        found = []
        while rest > 1:
            radix = 4 if rest % 4 == 0 else 2
            found.append(("dp", step, radix))
            step *= radix
            rest //= radix
        return found

    dp = sizes["dp"]
    return dict(
        c=[("blk", 1, 2)], y=[("blk", 2, 2)], x=[("dp", 1, 2)], a=[("dp", 2, 2)], b=split(4, dp // 4), z=split(2, dp // 2)
    )


def bits_of(sizes, letters):
    bits = []
    for letter in letters:
        for axis, step, radix in stages_of(sizes)[letter]:
            bits += [(axis, step, 2)] if radix == 2 else [(axis, step, 2), (axis, 2 * step, 2)]
    return bits


def digit_of(stage):
    axis, step, radix = stage
    index = lax.axis_index(axis)
    digit = lax.rem(lax.div(index, step), radix)
    others = []
    for offset in range(1, radix):
        other = lax.rem(digit + offset, radix)
        others.append((other, {axis: index + (other - digit) * step}))
    return digit, others


def flip(index, step):
    return index + step - 2 * step * lax.rem(lax.div(index, step), 2)


def aligned(start, unit):
    return start if isinstance(start, int) else pl.multiple_of(start, unit)


def span(start, count, unit=ROWS):
    return pl.ds(aligned(start, unit), count)


def send(src, dst, sems, at, peer, land_at=None):
    sends, receives = sems
    copy = pltpu.make_async_remote_copy(
        src_ref=src,
        dst_ref=dst,
        send_sem=sends.at[at],
        recv_sem=receives.at[at if land_at is None else land_at],
        device_id=peer,
        device_id_type=MESH,
    )
    copy.start()
    return copy


def plan_of(sizes, rows, letters):
    stages = [stage for letter in letters for stage in stages_of(sizes)[letter]]
    plan = []
    size = rows
    for axis, step, radix in stages[:-1]:
        size = cut_stage(plan, axis, step, radix, size)
    axis, step, radix = stages[-1]
    if radix == 2:
        plan.append((stages[-1], False, size))
    else:
        cut_stage(plan, axis, step, radix, size)
    return plan


def cut_stage(plan, axis, step, radix, size):
    if size % (radix * ROWS) == 0:
        plan.append(((axis, step, radix), True, size // radix))
        return size // radix
    bit = step
    while bit < step * radix:
        split = size % (2 * ROWS) == 0
        size = size // 2 if split else size
        plan.append(((axis, bit, 2), split, size))
        bit *= 2
    return size


def landing_rows(sizes, rows, letters):
    return sum(size * (stage[2] - 1) for stage, _, size in plan_of(sizes, rows, letters))


def semaphores_of(sizes, rows, letters):
    plan = plan_of(sizes, rows, letters)
    return max(stage[2] - 1 for stage, _, _ in plan), sum((stage[2] - 1) * (1 + split) for stage, split, _ in plan)


def semaphore_counts(sizes, seqs, width):
    sends, receives = 3 + 6 * seqs + 1, 3 + 12 * seqs + len(bits_of(sizes, SUM_ORDER))
    for letters in UNIT_ORDERS:
        sending, receiving = semaphores_of(sizes, width // HALVES, letters)
        sends, receives = sends + sending, receives + receiving
    for letters in OWN_ORDERS:
        sending, receiving = semaphores_of(sizes, width, letters)
        sends, receives = sends + max(sending, 3), receives + receiving + 3
    return sends, receives


def add_rows(first, first_at, land, land_at, terms, out, out_at, count):
    total = first[span(first_at, count)].astype(WIDE)
    for term in range(terms):
        total = total + land[span(land_at + term * count, count)].astype(WIDE)
    out[span(out_at, count)] = total.astype(out.dtype)


def reduce_rows(sizes, work, land, out, sems, base, rows, land_at, send_at, receive_at, letters, sent):
    plan = plan_of(sizes, rows, letters)
    start = base
    trail = []
    for level, (stage, split, count) in enumerate(plan):
        digit, others = digit_of(stage)
        keep = start + digit * count if split else start
        for copy in sent:
            copy.wait_send()
        sent.clear()
        for offset, (other, peer) in enumerate(others):
            give = start + other * count if split else start
            slot = len(others) - 1 - offset
            sent.append(
                send(
                    work.at[span(give, count)],
                    land.at[span(land_at + slot * count, count)],
                    sems,
                    send_at + offset,
                    peer,
                    receive_at + slot,
                )
            )
        yield
        for copy in sent:
            copy.wait_recv()
        if split:
            trail.append((others, keep, count))
        else:
            for copy in sent:
                copy.wait_send()
            sent.clear()
        target = out if level == len(plan) - 1 else work
        add_rows(work, keep, land, land_at, len(others), target, keep, count)
        land_at += count * len(others)
        receive_at += len(others)
        start = keep
    for others, mine, count in reversed(trail):
        part = out.at[span(mine, count)]
        for copy in sent:
            copy.wait_send()
        sent.clear()
        for offset, (_, peer) in enumerate(others):
            sent.append(send(part, part, sems, send_at + offset, peer, receive_at + len(others) - 1 - offset))
        yield
        for copy in sent:
            copy.wait_recv()
        receive_at += len(others)


def reduce_whole(steps, land, sems, send_at, receive_at, bits):
    for level, bit in enumerate(bits):
        copy = send(steps.at[level], land.at[level], sems, send_at, digit_of(bit)[1][0][1], receive_at + level)
        yield
        copy.wait()
        steps[level + 1] = steps[level] + land[level]


def share_blocks(slots, sems, send_at, receive_at, me, sent):
    near, far = flip(me, 1), flip(me, 2)
    for copy in sent:
        copy.wait_send()
    across = send(slots.at[me], slots.at[me], sems, send_at, {"blk": far}, receive_at)
    beside = send(slots.at[me], slots.at[me], sems, send_at + 1, {"blk": near}, receive_at + 1)
    yield
    across.wait_recv()
    onward = send(slots.at[far], slots.at[far], sems, send_at + 2, {"blk": near}, receive_at + 2)
    yield
    beside.wait_recv()
    onward.wait_recv()
    sent[:] = [across, beside, onward]


def dot(left, right):
    return jnp.dot(left, right, preferred_element_type=WIDE)


def dot_right_t(left, right):
    return lax.dot_general(left, right, (((1,), (1,)), ((), ())), preferred_element_type=WIDE)


def dot_left_t(left, right):
    return lax.dot_general(left, right, (((0,), (0,)), ((), ())), preferred_element_type=WIDE)


def fold(values):
    rows, width = values.shape
    return jnp.sum(values.reshape(rows // 8, 8, width), axis=0)


def mean_of(values):
    return jnp.mean(values, axis=-1, keepdims=True)


def norm_back(upstream, scaled, inverse, gain):
    inner = upstream * gain
    return inverse * (inner - mean_of(inner) - scaled * mean_of(inner * scaled))


def layout_of(sizes, seqs, rows, width, hidden):
    tokens = seqs * rows
    blocks = sizes["blk"]
    length = rows * blocks
    own = width // blocks
    heads = own // HEAD
    levels = len(bits_of(sizes, SUM_ORDER))
    units = 2 * (hidden // width) + 1
    land_total = sum(landing_rows(sizes, width // HALVES, letters) for letters in UNIT_ORDERS)
    own_land = max(landing_rows(sizes, width, order) for order in OWN_ORDERS)
    return dict(
        x_all=((seqs, length, width), LOW),
        x_own=((seqs, rows, width), LOW),
        cot=((seqs, rows, width), LOW),
        w_qkv=((width, 3 * own), LOW),
        w_o=((width, width), LOW),
        w_up=((width, hidden), LOW),
        w_down=((hidden, width), LOW),
        vec_low=((VECTORS * width,), LOW),
        vec=((VECTORS, width), WIDE),
        flags=((blocks, 8, rows), WIDE),
        qkv=((seqs, length, 3 * own), LOW),
        probs=((seqs * heads, length, length), LOW),
        o_wide=((seqs, length, own), WIDE),
        o_send=((seqs, length, own), LOW),
        o_all=((seqs, rows, width), LOW),
        total=((tokens, width), WIDE),
        scaled=((tokens, width), WIDE),
        inverse=((tokens, 128), WIDE),
        normed=((tokens, width), WIDE),
        normed_low=((tokens, width), LOW),
        active=((tokens, hidden), LOW),
        slope=((tokens, hidden), WIDE),
        grad_b=((tokens, width), WIDE),
        grad_y=((tokens, width), LOW),
        grad_z=((tokens, hidden), LOW),
        grad_t=((tokens, width), LOW),
        do_send=((seqs, rows, width), LOW),
        do_all=((seqs, length, own), LOW),
        grad_s=((heads, length, length), LOW),
        d_qkv=((seqs, length, 3 * own), LOW),
        dx_part=((seqs, length, width), LOW),
        dx_near=((seqs, 2, rows, width), LOW),
        dx_chip=((seqs, rows, width), LOW),
        hid=((seqs, rows, width), LOW),
        dx=((seqs, rows, width), LOW),
        out=((units * width, width), LOW),
        own_out=((3, blocks, width, own), LOW),
        dx_far=((seqs, rows, width), LOW),
        work=((units * width, width), LOW),
        land=((land_total, width), LOW),
        own_work=((3, width, own), LOW),
        own_land=((3, own_land, own), LOW),
        steps=((levels + 1, VECTORS, width), WIDE),
        vec_land=((levels, VECTORS, width), WIDE),
    )


def layer_kernel(sizes, names, *refs):
    x, lengths, mask, wq, wk, wv, wo, wu, wd, cotangent = refs[:10]
    vectors_in = refs[10:19]
    hid_out, dx_out, sums_out, own_sums_out, vec_out = refs[19:24]
    r = types.SimpleNamespace(**dict(zip(names, refs[24:-3], strict=True)))
    sems = refs[-3:-1]
    local = refs[-1]
    x_all, qkv, vec, steps = r.x_all, r.qkv, r.vec, r.steps
    seqs, rows, width = r.x_own.shape
    tokens = seqs * rows
    length = x_all.shape[1]
    blocks = sizes["blk"]
    own = width // blocks
    heads = own // HEAD
    hidden = r.w_up.shape[1]
    tiles = hidden // width
    scale = HEAD ** (-0.5)
    me = lax.axis_index("blk")
    near, far = flip(me, 1), flip(me, 2)
    cross = flip(far, 1)
    peers = (near, far, cross)
    place = lambda index: span(index * rows, rows, rows)
    lanes = lambda index: span(index * own, own, own)

    used = {"send": 0, "receive": 0, "local": 0}
    pending, stores = [], []

    def take(which, count):
        at = used[which]
        used[which] += count
        return at

    def slot(count):
        return take("send", count), take("receive", count)

    def send_in(pair, offset, src, dst, peer):
        return send(src, dst, sems, pair[0] + offset, {"blk": peer}, pair[1] + offset)

    def fetch(src, dst, at=None):
        copy = pltpu.make_async_copy(src, dst, local.at[take("local", 1) if at is None else at])
        copy.start()
        return copy

    unit_store, own_store = take("local", 1), take("local", 1)
    whole_stores = [
        pltpu.make_async_copy(r.out, sums_out, local.at[unit_store]),
        pltpu.make_async_copy(r.own_out, own_sums_out, local.at[own_store]),
    ]

    loads_x = [
        fetch(x, x_all.at[:, place(me), :]),
        fetch(x, r.x_own),
    ]
    loads_w = [
        fetch(weight.at[:, lanes(me)], r.w_qkv.at[:, pl.ds(at * own, own)])
        for at, weight in enumerate((wq, wk, wv))
    ]
    load_vectors = []
    at = 0
    for vector in vectors_in:
        count = vector.shape[0]
        load_vectors.append(fetch(vector, r.vec_low.at[pl.ds(at, count)]))
        at += count
    load_o = fetch(wo, r.w_o)
    load_up = fetch(wu, r.w_up)
    load_down = fetch(wd, r.w_down)
    load_cot = fetch(cotangent, r.cot)

    positions = me * rows + lax.broadcasted_iota(jnp.int32, (1, rows), 1)
    flag_rows = []
    for seq in range(seqs):
        good = (mask[seq : seq + 1, :] == 1) & (positions < lengths[seq])
        flag_rows.append(jnp.where(good, 0.0, -1000000000.0).astype(WIDE))
    flag_rows.append(jnp.zeros((8 - seqs, rows), WIDE))
    r.flags[me] = jnp.concatenate(flag_rows, axis=0)

    barrier = pltpu.get_barrier_semaphore()
    greeted = [{"blk": peer} for peer in peers] + [
        peer for letter in "xz" for stage in stages_of(sizes)[letter] for _, peer in digit_of(stage)[1]
    ]
    for peer in greeted:
        pl.semaphore_signal(barrier, inc=1, device_id=peer, device_id_type=MESH)
    pl.semaphore_wait(barrier, len(greeted))

    at_far, at_near, at_on, at_flag = slot(seqs), slot(seqs), slot(seqs), slot(len(peers))
    flag_copies = [
        send_in(at_flag, index, r.flags.at[me], r.flags.at[me], peer)
        for index, peer in enumerate(peers)
    ]
    x_far, x_near, x_on = [], [], []
    for seq in range(seqs):
        target = x_all.at[seq, place(me), :]
        x_far.append(send_in(at_far, seq, x.at[seq], target, far))
        x_near.append(send_in(at_near, seq, x.at[seq], target, near))
    pending += flag_copies

    def forward_x(seq):
        x_far[seq].wait_recv()
        block = x_all.at[seq, place(far), :]
        x_on.append(send_in(at_on, seq, block, block, near))

    lane = lax.broadcasted_iota(jnp.int32, (1, own), 1)
    of_head = [(lane >= head * HEAD) & (lane < (head + 1) * HEAD) for head in range(heads)]
    only = lambda values, head: jnp.where(of_head[head], values.astype(WIDE), 0.0)
    for copy in load_vectors:
        copy.wait()
    for at in range(8 + tiles):
        vec[at : at + 1, :] = r.vec_low[at * width : (at + 1) * width].astype(WIDE).reshape(1, width)
    bias_q = vec[0:1, lanes(me)]
    bias_v = vec[1:2, lanes(me)]
    bias_qkv = jnp.concatenate([bias_q, jnp.zeros_like(bias_q), bias_v], axis=1)
    o_all, o_send = r.o_all, r.o_send
    at_o = slot(seqs * len(peers))
    o_copies = []

    def project(seq):
        qkv[seq] = (dot(x_all[seq], r.w_qkv[...]) + bias_qkv).astype(LOW)

    column = lax.broadcasted_iota(jnp.int32, (length, length), 1)
    row = lax.broadcasted_iota(jnp.int32, (length, length), 0)

    def attend(seq):
        keys = qkv[seq, :, own : 2 * own]
        values = qkv[seq, :, 2 * own :]
        key_bias = jnp.concatenate([r.flags[block, seq : seq + 1, :] for block in range(blocks)], axis=1)
        bias = jnp.where(column == row, 0.0, key_bias)
        query = qkv[seq, :, 0:own].astype(WIDE) * scale
        joined = None
        for head in range(heads):
            scores = dot_right_t(only(query, head).astype(LOW), keys) + bias
            raised = jnp.exp(scores - jnp.max(scores, axis=-1, keepdims=True))
            probs = (raised / jnp.sum(raised, axis=-1, keepdims=True)).astype(LOW)
            r.probs[seq * heads + head] = probs
            result = dot(probs, values)
            joined = result if joined is None else jnp.where(of_head[head], result, joined)
        r.o_wide[seq] = joined
        o_send[seq] = joined.astype(LOW)
        for index, peer in enumerate(peers):
            part = o_send.at[seq, place(peer), :]
            o_copies.append(send_in(at_o, seq * len(peers) + index, part, o_all.at[seq, :, lanes(me)], peer))
        o_all[seq, :, lanes(me)] = o_send[seq, place(me), :]

    for copy in loads_w:
        copy.wait()
    for copy in loads_x:
        copy.wait()
    for copy in flag_copies:
        copy.wait_recv()
    forward_x(0)
    for seq in range(seqs):
        x_near[seq].wait_recv()
        x_on[seq].wait_recv()
        project(seq)
        if seq + 1 < seqs:
            forward_x(seq + 1)
        attend(seq)

    total, scaled, inverse = r.total, r.scaled, r.inverse
    normed, normed_low = r.normed, r.normed_low
    active, slope = r.active, r.slope
    grad_b, grad_y = r.grad_b, r.grad_y
    wide_row = lambda at: vec[at : at + 1, :]
    total_row = lambda values: jnp.sum(fold(values), axis=0, keepdims=True)
    flat = lambda ref: ref[...].reshape(tokens, width)
    steps[0] = jnp.zeros((VECTORS, width), WIDE)

    def normalize(values):
        center = values - mean_of(values)
        inv = lax.rsqrt(mean_of(center * center) + EPSILON)
        return center * inv, inv

    def feed_forward(first, count):
        some = slice(first, first + count)
        size = count * rows
        part = pl.ds(first * rows, size)
        mixed = o_all[some].reshape(size, width)
        made, inv = normalize(
            r.x_own[some].reshape(size, width).astype(WIDE) + dot(mixed, r.w_o[...]) + wide_row(2)
        )
        scaled[part, :] = made
        inverse[part, :] = jnp.broadcast_to(inv, (size, 128))
        result = made * wide_row(3) + wide_row(4)
        normed[part, :] = result
        normed_low[part, :] = result.astype(LOW)
        step = min(hidden, 2 * width * (2 * rows) // size)
        for at in range(0, hidden, step):
            columns = slice(at, at + step)
            offset = jnp.concatenate([wide_row(8 + tile) for tile in range(at // width, (at + step) // width)], axis=1)
            z = dot(normed_low[part, :], r.w_up[:, columns]) + offset
            below = 0.5 * (1.0 + lax.erf(z * 0.7071067811865476))
            active[part, columns] = (z * below).astype(LOW)
            slope[part, columns] = below + z * (0.3989422804014327 * jnp.exp(-0.5 * z * z))
        made, inv = normalize(normed[part, :] + dot(active[part, :], r.w_down[...]) + wide_row(5))
        r.hid[some] = (made * wide_row(6) + wide_row(7)).astype(LOW).reshape(count, rows, width)
        upstream = r.cot[some].reshape(size, width).astype(WIDE)
        back = norm_back(upstream, made, inv, wide_row(6))
        grad_b[part, :] = back
        rounded = back.astype(LOW)
        grad_y[part, :] = rounded
        steps[0, 7:8, :] += total_row(upstream)
        steps[0, 6:7, :] += total_row(upstream * made)
        steps[0, 5:6, :] += total_row(rounded.astype(WIDE))

    for copy in (load_o, load_up, load_down, load_cot):
        copy.wait()
    arrived = 0
    for first, count in ((0, seqs - 1), (seqs - 1, 1)) if seqs > 1 else ((0, 1),):
        for copy in o_copies[arrived : (first + count) * len(peers)]:
            copy.wait_recv()
        arrived = (first + count) * len(peers)
        feed_forward(first, count)
    stores.append(fetch(r.hid, hid_out))

    work = r.work
    running = {}
    last = []
    place_of = {"land": 0, "poll": 0}

    def launch(name, item):
        running[name] = item
        advance(name)

    def advance(name):
        if name in running and next(running[name], True) is not None:
            del running[name]

    def launch_unit(unit):
        letters = UNIT_ORDERS[unit]
        count = width // HALVES
        sending, receiving = semaphores_of(sizes, count, letters)
        ats = take("send", sending), take("receive", receiving)
        land_at = place_of["land"]
        place_of["land"] += landing_rows(sizes, count, letters)
        sent = []
        last.append(sent)

        def item():
            yield from reduce_rows(sizes, work, r.land, r.out, sems, unit * count, count, land_at, *ats, letters, sent)
            part = pl.ds(unit * count, count)
            fetch(r.out.at[part], sums_out.at[part], unit_store)

        launch(unit, item())

    def launch_units(tile):
        for half in range(HALVES):
            launch_unit(tile * HALVES + half)

    def launch_own(kind):
        letters = OWN_ORDERS[kind]
        sending, receiving = semaphores_of(sizes, width, letters)
        ats = take("send", max(sending, 3)), take("receive", receiving)
        blocks_at = take("receive", 3)
        slots = r.own_out.at[kind]
        sent = []
        last.append(sent)

        def item():
            parts = r.own_work.at[kind], r.own_land.at[kind], slots.at[me]
            yield from reduce_rows(sizes, *parts, sems, 0, width, 0, *ats, letters, sent)
            yield from share_blocks(slots, sems, ats[0], blocks_at, me, sent)
            fetch(slots, own_sums_out.at[kind], own_store)

        launch(len(UNIT_ORDERS) + kind, item())

    def poll():
        at = place_of["poll"]
        place_of["poll"] += 1
        for name in POLLS[at] if at < len(POLLS) else ():
            advance(name)

    cut = lambda tile: slice(tile * width, (tile + 1) * width)
    for tile in range(tiles):
        work[cut(tile), :] = dot_left_t(active[:, cut(tile)], grad_y[...]).astype(LOW)
        launch_units(tile)
        poll()

    grad_z = r.grad_z

    for tile in range(tiles):
        made = (dot_right_t(grad_y[...], r.w_down[cut(tile), :]) * slope[:, cut(tile)]).astype(LOW)
        grad_z[:, cut(tile)] = made
        steps[0, 8 + tile : 9 + tile, :] = total_row(made.astype(WIDE))
        poll()
    upstream = grad_b[...] + dot_right_t(grad_z[...], r.w_up[...])
    total[...] = upstream
    poll()
    upstream = total[...]

    grad_t = r.grad_t
    made = scaled[...]
    back = norm_back(upstream, made, inverse[:, 0:1], wide_row(3))
    grad_b[...] = back
    rounded = back.astype(LOW)
    grad_t[...] = rounded
    steps[0, 4:5, :] = total_row(upstream)
    steps[0, 3:4, :] = total_row(upstream * made)
    steps[0, 2:3, :] = total_row(rounded.astype(WIDE))
    poll()

    do_send, do_all = r.do_send, r.do_all
    for copy in x_far + x_near + x_on:
        copy.wait_send()
    at_do = at_far[0], take("receive", seqs * len(peers))
    do_copies = []
    made = dot_right_t(grad_t[...], r.w_o[...]).astype(LOW)
    do_send[...] = made.reshape(seqs, rows, width)
    for seq in range(seqs):
        do_copies.append(
            [
                send_in(
                    at_do,
                    seq * len(peers) + index,
                    do_send.at[seq, :, lanes(peer)],
                    do_all.at[seq, place(me), :],
                    peer,
                )
                for index, peer in enumerate(peers)
            ]
        )
        do_all[seq, place(me), :] = do_send[seq, :, lanes(me)]
        pending += do_copies[-1]

    poll()
    work[2 * hidden :, :] = dot_left_t(o_all[...].reshape(tokens, width), grad_t[...]).astype(LOW)
    launch_units(2 * tiles)
    poll()
    for tile in range(tiles):
        work[cut(tiles + tile), :] = dot_left_t(normed_low[...], grad_z[:, cut(tile)]).astype(LOW)
        launch_units(tiles + tile)
        poll()

    d_qkv, grad_s, dx_part = r.d_qkv, r.grad_s, r.dx_part
    for copy in o_copies:
        copy.wait_send()
    at_dx_near = at_o[0], take("receive", 2 * seqs)
    at_dx_far = at_o[0] + 2 * seqs, take("receive", seqs)
    dx_near, dx_far = [], []

    def value_back(seq):
        upstream = do_all[seq].astype(WIDE)
        grads = [
            dot_left_t(r.probs[seq * heads + head], only(upstream, head).astype(LOW)) for head in range(heads)
        ]
        d_qkv[seq, :, 2 * own :] = functools.reduce(jnp.add, grads).astype(LOW)

    def score_back(seq):
        values = qkv[seq, :, 2 * own :]
        upstream = do_all[seq].astype(WIDE)
        inner = upstream * r.o_wide[seq]
        for head in range(heads):
            delta = jnp.sum(only(inner, head), axis=-1, keepdims=True)
            prob_grad = dot_right_t(only(upstream, head).astype(LOW), values)
            probs = r.probs[seq * heads + head].astype(WIDE)
            grad_s[head] = (probs * (prob_grad - delta)).astype(LOW)

    def query_key_back(seq):
        queries_wide = qkv[seq, :, 0:own].astype(WIDE) * scale
        keys_wide = qkv[seq, :, own : 2 * own].astype(WIDE) * scale
        query_grads, key_grads = [], []
        for head in range(heads):
            query_grads.append(dot(grad_s[head], only(keys_wide, head).astype(LOW)))
            key_grads.append(dot_left_t(grad_s[head], only(queries_wide, head).astype(LOW)))
        d_qkv[seq, :, 0:own] = functools.reduce(jnp.add, query_grads).astype(LOW)
        d_qkv[seq, :, own : 2 * own] = functools.reduce(jnp.add, key_grads).astype(LOW)

    def input_back(seq):
        dx_part[seq] = dot_right_t(d_qkv[seq], r.w_qkv[...]).astype(LOW)
        dx_near.append(
            [
                send_in(at_dx_near, 2 * seq + at, dx_part.at[seq, place(block), :], r.dx_near.at[seq, at], near)
                for at, block in enumerate((near, cross))
            ]
        )
        pending.extend(dx_near[-1])

    def own_grad(columns):
        tokens_in = x_all[...].reshape(seqs * length, width)
        return dot_left_t(tokens_in, d_qkv[:, :, columns].reshape(seqs * length, -1)).astype(LOW)

    def hand_on(seq):
        dx_near[seq][1].wait_recv()
        summed = dx_part[seq, place(far), :].astype(WIDE) + r.dx_near[seq, 1].astype(WIDE)
        r.dx_chip[seq] = summed.astype(LOW)
        dx_far.append(send_in(at_dx_far, seq, r.dx_chip.at[seq], r.dx_far.at[seq], far))
        pending.append(dx_far[-1])

    for seq in range(seqs):
        poll()
        for copy in do_copies[seq]:
            copy.wait_recv()
        value_back(seq)
        poll()
    r.own_work[0] = own_grad(slice(2 * own, None))
    launch_own(0)
    poll()
    for seq in range(seqs):
        score_back(seq)
        poll()
        query_key_back(seq)
        poll()
    made = own_grad(slice(0, 2 * own))
    r.own_work[1] = made[:, :own]
    launch_own(1)
    r.own_work[2] = made[:, own:]
    launch_own(2)
    poll()
    for seq in range(seqs):
        input_back(seq)
        poll()
        if seq > 0:
            hand_on(seq - 1)
    hand_on(seqs - 1)

    sums = total_row(d_qkv[...].reshape(seqs * length, 3 * own).astype(WIDE))
    steps[0, 0:1, lanes(me)] = sums[:, 0:own]
    steps[0, 1:2, lanes(me)] = sums[:, 2 * own :]
    sum_bits = bits_of(sizes, SUM_ORDER)
    launch(len(UNIT_ORDERS) + 3, reduce_whole(steps, r.vec_land, sems, take("send", 1), take("receive", len(sum_bits)), sum_bits))
    poll()

    def finish_input():
        for seq in range(seqs):
            yield
            dx_near[seq][0].wait_recv()
            dx_far[seq].wait_recv()
            summed = grad_b[seq * rows : (seq + 1) * rows, :] + dx_part[seq, place(me), :].astype(WIDE)
            summed = summed + r.dx_near[seq, 0].astype(WIDE) + r.dx_far[seq].astype(WIDE)
            r.dx[seq] = summed.astype(LOW)
        stores.append(fetch(r.dx, dx_out))

    launch(len(UNIT_ORDERS) + 4, finish_input())
    for name in sum(POLLS[place_of["poll"] :], ()):
        advance(name)
    while running:
        for name in list(running):
            advance(name)
    vec_out[...] = steps[len(sum_bits)]
    for copy in sum(last, pending):
        copy.wait_send()
    for copy in stores + whole_stores:
        copy.wait()
    assert (used["send"], used["receive"]) == semaphore_counts(sizes, seqs, width) and used["local"] == local.shape[0]


def widen_kernel(blocks, hid, dx, sums, shared, vec, *refs):
    hid_out, dx_out, wq, wk, wv, wo, wu, wd = refs[:8]
    rows_out, bu = refs[8:16], refs[16]
    low, shared_low, wide, shared_wide, hid_low, dx_low, vec_in, flat_vec, sems = refs[17:]
    width = wq.shape[0]
    own = width // blocks
    units = sums.shape[0] // width
    tiles = (units - 1) // 2
    used = [0]

    def copy(src, dst):
        made = pltpu.make_async_copy(src, dst, sems.at[used[0]])
        used[0] += 1
        made.start()
        return made

    unit = lambda ref, at: ref.at[pl.ds(at * width, width)]
    load_vec = copy(vec, vec_in)
    shared_loads = [copy(shared.at[kind], shared_low.at[kind]) for kind in range(3)]
    loads = [copy(unit(sums, at), unit(low, at)) for at in range(units)]
    token_loads = [copy(hid, hid_low), copy(dx, dx_low)]
    stores = []
    for kind, target in enumerate((wv, wq, wk)):
        shared_loads[kind].wait()
        for block in range(blocks):
            shared_wide[kind, :, block * own : (block + 1) * own] = shared_low[kind, block].astype(WIDE)
        stores.append(copy(shared_wide.at[kind], target))
    targets = (
        [unit(wd, at) for at in range(tiles)] + [wu.at[:, pl.ds(at * width, width)] for at in range(tiles)] + [wo]
    )
    for at in range(units):
        loads[at].wait()
        part = slice(at * width, (at + 1) * width)
        wide[part, :] = low[part, :].astype(WIDE)
        stores.append(copy(unit(wide, at), targets[at]))
        if at == 0:
            load_vec.wait()
            count = len(rows_out)
            for index in range(count + tiles):
                flat_vec[index * width : (index + 1) * width] = vec_in[index, :]
            for index, row in enumerate(rows_out):
                stores.append(copy(flat_vec.at[pl.ds(index * width, width)], row))
            stores.append(copy(flat_vec.at[pl.ds(count * width, tiles * width)], bu))
        if at == units // 2:
            for load in token_loads:
                load.wait()
            stores += [copy(hid_low, hid_out), copy(dx_low, dx_out)]
    for made in stores:
        made.wait()


def on_device(
    sizes,
    hidden_input,
    lengths,
    key_mask,
    query_weight,
    query_offset,
    key_weight,
    value_weight,
    value_offset,
    output_weight,
    output_offset,
    mixer_gain,
    mixer_shift,
    up_weight,
    up_offset,
    down_weight,
    down_offset,
    final_gain,
    final_shift,
    cotangent,
):
    seqs, rows, width = hidden_input.shape
    hidden = up_weight.shape[1]
    blocks = sizes["blk"]
    own = width // blocks
    scratch = layout_of(sizes, seqs, rows, width, hidden)
    anywhere = pl.BlockSpec(memory_space=pl.ANY)
    inside = pl.BlockSpec(memory_space=pltpu.VMEM)
    scalars = pl.BlockSpec(memory_space=pltpu.SMEM)
    scratch_shape = types.SimpleNamespace(**{name: shape for name, (shape, _) in scratch.items()})
    units = scratch_shape.work
    shared = (3, blocks, width, own)
    hid, dx, sums, own_sums, vec_sums = pl.pallas_call(
        functools.partial(layer_kernel, sizes, tuple(scratch)),
        out_shape=(
            jax.ShapeDtypeStruct(hidden_input.shape, LOW),
            jax.ShapeDtypeStruct(hidden_input.shape, LOW),
            jax.ShapeDtypeStruct(units, LOW),
            jax.ShapeDtypeStruct(shared, LOW),
            jax.ShapeDtypeStruct((VECTORS, width), WIDE),
        ),
        in_specs=[anywhere, scalars, inside] + [anywhere] * 16,
        out_specs=(anywhere,) * 4 + (inside,),
        scratch_shapes=[pltpu.VMEM(shape, kind) for shape, kind in scratch.values()]
        + [
            *(pltpu.SemaphoreType.DMA((count,)) for count in semaphore_counts(sizes, seqs, width)),
            pltpu.SemaphoreType.DMA((22,)),
        ],
        compiler_params=pltpu.CompilerParams(
            collective_id=0, has_side_effects=True, vmem_limit_bytes=60 * 1024 * 1024
        ),
    )(
        hidden_input,
        lengths,
        key_mask,
        query_weight,
        key_weight,
        value_weight,
        output_weight,
        up_weight,
        down_weight,
        cotangent,
        query_offset,
        value_offset,
        output_offset,
        mixer_gain,
        mixer_shift,
        down_offset,
        final_gain,
        final_shift,
        up_offset,
    )
    full = jax.ShapeDtypeStruct((width, width), WIDE)
    row = jax.ShapeDtypeStruct((width,), WIDE)
    flat = jax.ShapeDtypeStruct(hidden_input.shape, LOW)
    final = pl.pallas_call(
        functools.partial(widen_kernel, blocks),
        out_shape=(
            flat,
            flat,
            full,
            full,
            full,
            full,
            jax.ShapeDtypeStruct((width, hidden), WIDE),
            jax.ShapeDtypeStruct((hidden, width), WIDE),
        )
        + (row,) * 8
        + (jax.ShapeDtypeStruct((hidden,), WIDE),),
        in_specs=[anywhere] * 5,
        out_specs=(anywhere,) * 17,
        scratch_shapes=[
            pltpu.VMEM(units, LOW),
            pltpu.VMEM(shared, LOW),
            pltpu.VMEM(units, WIDE),
            pltpu.VMEM((3, width, width), WIDE),
            pltpu.VMEM(hidden_input.shape, LOW),
            pltpu.VMEM(hidden_input.shape, LOW),
            pltpu.VMEM((VECTORS, width), WIDE),
            pltpu.VMEM((VECTORS * width,), WIDE),
            pltpu.SemaphoreType.DMA((2 * units[0] // width + 20,)),
        ],
        compiler_params=pltpu.CompilerParams(vmem_limit_bytes=60 * 1024 * 1024),
    )(hid, dx, sums, own_sums, vec_sums)
    hid, dx, wq, wk, wv, wo, wu, wd, bq, bv, bo, g1, s1, bd, g2, s2, bu = final
    return hid, dx, wq, bq, wk, wv, bv, wo, bo, g1, s1, wu, bu, wd, bd, g2, s2


def solution(mesh):
    split = P("dp", "blk", None)
    in_specs = (split, P("dp"), P("dp", "blk")) + (P(),) * 15 + (split,)
    out_specs = (split, split) + (P(),) * 15
    return jax.shard_map(
        functools.partial(on_device, dict(mesh.shape)),
        mesh=mesh,
        in_specs=in_specs,
        out_specs=out_specs,
        check_vma=False,
    )
```

```python
import functools
import types

import jax
import jax.numpy as jnp
from jax import lax
from jax.experimental import pallas as pl
from jax.experimental.pallas import tpu as pltpu
from jax.sharding import PartitionSpec as P

HEAD = 64
EPSILON = 1e-06
MESH = pl.DeviceIdType.MESH
ROWS = 16
LOW = jnp.bfloat16
WIDE = jnp.float32
VECTORS = 16
HALVES = 2

UNIT_ORDERS = ("caxyb", "cxzy", "cyxab", "cyxab", "cxyab", "cayxb", "cabyx", "cxaby", "cxyab", "cabxy", "cxaby", "cabxy", "cxayb", "cxyab", "caxyb", "cyxab", "cxyab", "cyaxb")
OWN_ORDERS = ("xab", "xab", "xab")
SUM_ORDER = "cxyab"
POLLS = (
    (),
    (),
    (),
    (),
    (0,),
    (1,),
    (2,),
    (3, 4,),
    (5, 6, 7,),
    (),
    (),
    (),
    (),
    (),
    (),
    (0, 16,),
    (1, 17, 8, 2, 9, 10, 11, 12, 5, 4, 13, 14, 3, 15, 6, 7,),
    (0,),
    (),
    (1, 16,),
    (9,),
    (8,),
    (11,),
    (2,),
    (17,),
    (5, 14,),
    (10, 4,),
    (6,),
    (7, 12,),
    (15, 0, 9, 1,),
    (13, 2, 11, 16,),
    (3, 17, 8,),
    (18, 6, 10, 4, 5,),
    (19, 7, 12, 14, 0, 13,),
    (16, 1, 3, 8, 2, 21, 20, 18, 15, 9, 10, 11, 22, 4, 17, 5, 6, 19, 13, 16, 1, 3, 2, 21, 8, 22, 20, 1, 5, 15, 18, 4, 17, 22, 2, 7, 16, 19, 12, 3, 14, 8, 13, 0, 9, 10, 11, 17, 20, 6, 18, 15, 21, 19, 5, 7, 3, 4, 12, 0, 13, 9, 14, 11, 17, 2, 10, 20, 16, 18, 2, 8, 15, 6, 19, 21, 3, 12, 4, 5, 13, 3, 14, 7, 4, 20, 5, 17, 0, 16, 17, 9, 0, 16, 11, 8, 10, 18, 15, 8, 6, 18, 13, 21, 14, 6, 12, 19, 13, 7, 9, 19, 7, 10, 11, 9, 20, 10, 12, 14, 11, 20, 15, 12, 14, 15,),
)


def stages_of(sizes):
    def split(step, rest):
        found = []
        while rest > 1:
            radix = 4 if rest % 4 == 0 else 2
            found.append(("dp", step, radix))
            step *= radix
            rest //= radix
        return found

    dp = sizes["dp"]
    return dict(
        c=[("blk", 1, 2)], y=[("blk", 2, 2)], x=[("dp", 1, 2)], a=[("dp", 2, 2)], b=split(4, dp // 4), z=split(2, dp // 2)
    )


def bits_of(sizes, letters):
    bits = []
    for letter in letters:
        for axis, step, radix in stages_of(sizes)[letter]:
            bits += [(axis, step, 2)] if radix == 2 else [(axis, step, 2), (axis, 2 * step, 2)]
    return bits


def digit_of(stage):
    axis, step, radix = stage
    index = lax.axis_index(axis)
    digit = lax.rem(lax.div(index, step), radix)
    others = []
    for offset in range(1, radix):
        other = lax.rem(digit + offset, radix)
        others.append((other, {axis: index + (other - digit) * step}))
    return digit, others


def flip(index, step):
    return index + step - 2 * step * lax.rem(lax.div(index, step), 2)


def aligned(start, unit):
    return start if isinstance(start, int) else pl.multiple_of(start, unit)


def span(start, count, unit=ROWS):
    return pl.ds(aligned(start, unit), count)


def send(src, dst, sems, at, peer, land_at=None):
    sends, receives = sems
    copy = pltpu.make_async_remote_copy(
        src_ref=src,
        dst_ref=dst,
        send_sem=sends.at[at],
        recv_sem=receives.at[at if land_at is None else land_at],
        device_id=peer,
        device_id_type=MESH,
    )
    copy.start()
    return copy


def plan_of(sizes, rows, letters):
    stages = [stage for letter in letters for stage in stages_of(sizes)[letter]]
    plan = []
    size = rows
    for axis, step, radix in stages[:-1]:
        size = cut_stage(plan, axis, step, radix, size)
    axis, step, radix = stages[-1]
    if radix == 2:
        plan.append((stages[-1], False, size))
    else:
        cut_stage(plan, axis, step, radix, size)
    return plan


def cut_stage(plan, axis, step, radix, size):
    if size % (radix * ROWS) == 0:
        plan.append(((axis, step, radix), True, size // radix))
        return size // radix
    bit = step
    while bit < step * radix:
        split = size % (2 * ROWS) == 0
        size = size // 2 if split else size
        plan.append(((axis, bit, 2), split, size))
        bit *= 2
    return size


def landing_rows(sizes, rows, letters):
    return sum(size * (stage[2] - 1) for stage, _, size in plan_of(sizes, rows, letters))


def semaphores_of(sizes, rows, letters):
    plan = plan_of(sizes, rows, letters)
    return max(stage[2] - 1 for stage, _, _ in plan), sum((stage[2] - 1) * (1 + split) for stage, split, _ in plan)


def semaphore_counts(sizes, seqs, width):
    sends, receives = 3 + 6 * seqs + 1, 3 + 12 * seqs + len(bits_of(sizes, SUM_ORDER))
    for letters in UNIT_ORDERS:
        sending, receiving = semaphores_of(sizes, width // HALVES, letters)
        sends, receives = sends + sending, receives + receiving
    for letters in OWN_ORDERS:
        sending, receiving = semaphores_of(sizes, width, letters)
        sends, receives = sends + max(sending, 3), receives + receiving + 3
    return sends, receives


def add_rows(first, first_at, land, land_at, terms, out, out_at, count):
    total = first[span(first_at, count)].astype(WIDE)
    for term in range(terms):
        total = total + land[span(land_at + term * count, count)].astype(WIDE)
    out[span(out_at, count)] = total.astype(out.dtype)


def reduce_rows(sizes, work, land, out, sems, base, rows, land_at, send_at, receive_at, letters, sent):
    plan = plan_of(sizes, rows, letters)
    start = base
    trail = []
    for level, (stage, split, count) in enumerate(plan):
        digit, others = digit_of(stage)
        keep = start + digit * count if split else start
        for copy in sent:
            copy.wait_send()
        sent.clear()
        for offset, (other, peer) in enumerate(others):
            give = start + other * count if split else start
            slot = len(others) - 1 - offset
            sent.append(
                send(
                    work.at[span(give, count)],
                    land.at[span(land_at + slot * count, count)],
                    sems,
                    send_at + offset,
                    peer,
                    receive_at + slot,
                )
            )
        yield
        for copy in sent:
            copy.wait_recv()
        if split:
            trail.append((others, keep, count))
        else:
            for copy in sent:
                copy.wait_send()
            sent.clear()
        target = out if level == len(plan) - 1 else work
        add_rows(work, keep, land, land_at, len(others), target, keep, count)
        land_at += count * len(others)
        receive_at += len(others)
        start = keep
    for others, mine, count in reversed(trail):
        part = out.at[span(mine, count)]
        for copy in sent:
            copy.wait_send()
        sent.clear()
        for offset, (_, peer) in enumerate(others):
            sent.append(send(part, part, sems, send_at + offset, peer, receive_at + len(others) - 1 - offset))
        yield
        for copy in sent:
            copy.wait_recv()
        receive_at += len(others)


def reduce_whole(steps, land, sems, send_at, receive_at, bits):
    for level, bit in enumerate(bits):
        copy = send(steps.at[level], land.at[level], sems, send_at, digit_of(bit)[1][0][1], receive_at + level)
        yield
        copy.wait()
        steps[level + 1] = steps[level] + land[level]


def share_blocks(slots, sems, send_at, receive_at, me, sent):
    near, far = flip(me, 1), flip(me, 2)
    for copy in sent:
        copy.wait_send()
    across = send(slots.at[me], slots.at[me], sems, send_at, {"blk": far}, receive_at)
    beside = send(slots.at[me], slots.at[me], sems, send_at + 1, {"blk": near}, receive_at + 1)
    yield
    across.wait_recv()
    onward = send(slots.at[far], slots.at[far], sems, send_at + 2, {"blk": near}, receive_at + 2)
    yield
    beside.wait_recv()
    onward.wait_recv()
    sent[:] = [across, beside, onward]


def dot(left, right):
    return jnp.dot(left, right, preferred_element_type=WIDE)


def dot_right_t(left, right):
    return lax.dot_general(left, right, (((1,), (1,)), ((), ())), preferred_element_type=WIDE)


def dot_left_t(left, right):
    return lax.dot_general(left, right, (((0,), (0,)), ((), ())), preferred_element_type=WIDE)


def fold(values):
    rows, width = values.shape
    return jnp.sum(values.reshape(rows // 8, 8, width), axis=0)


def mean_of(values):
    return jnp.mean(values, axis=-1, keepdims=True)


def norm_back(upstream, scaled, inverse, gain):
    inner = upstream * gain
    return inverse * (inner - mean_of(inner) - scaled * mean_of(inner * scaled))


def layout_of(sizes, seqs, rows, width, hidden):
    tokens = seqs * rows
    blocks = sizes["blk"]
    length = rows * blocks
    own = width // blocks
    heads = own // HEAD
    levels = len(bits_of(sizes, SUM_ORDER))
    units = 2 * (hidden // width) + 1
    land_total = sum(landing_rows(sizes, width // HALVES, letters) for letters in UNIT_ORDERS)
    own_land = max(landing_rows(sizes, width, order) for order in OWN_ORDERS)
    return dict(
        x_all=((seqs, length, width), LOW),
        x_own=((seqs, rows, width), LOW),
        cot=((seqs, rows, width), LOW),
        w_qkv=((width, 3 * own), LOW),
        w_o=((width, width), LOW),
        w_up=((width, hidden), LOW),
        w_down=((hidden, width), LOW),
        vec_low=((VECTORS * width,), LOW),
        vec=((VECTORS, width), WIDE),
        flags=((blocks, 8, rows), WIDE),
        mask=((seqs, rows), jnp.int32),
        qkv=((seqs, length, 3 * own), LOW),
        probs=((seqs * heads, length, length), LOW),
        o_wide=((seqs, length, own), WIDE),
        o_send=((seqs, length, own), LOW),
        o_all=((seqs, rows, width), LOW),
        total=((tokens, width), WIDE),
        scaled=((tokens, width), WIDE),
        inverse=((tokens, 128), WIDE),
        normed=((tokens, width), WIDE),
        normed_low=((tokens, width), LOW),
        active=((tokens, hidden), LOW),
        slope=((tokens, hidden), WIDE),
        grad_b=((tokens, width), WIDE),
        grad_y=((tokens, width), LOW),
        grad_z=((tokens, hidden), LOW),
        grad_t=((tokens, width), LOW),
        do_send=((seqs, rows, width), LOW),
        do_all=((seqs, length, own), LOW),
        grad_s=((heads, length, length), LOW),
        d_qkv=((seqs, length, 3 * own), LOW),
        dx_part=((seqs, length, width), LOW),
        dx_near=((seqs, 2, rows, width), LOW),
        dx_chip=((seqs, rows, width), LOW),
        hid=((seqs, rows, width), LOW),
        dx=((seqs, rows, width), LOW),
        out=((units * width, width), LOW),
        own_out=((3, blocks, width, own), LOW),
        dx_far=((seqs, rows, width), LOW),
        work=((units * width, width), LOW),
        land=((land_total, width), LOW),
        own_work=((3, width, own), LOW),
        own_land=((3, own_land, own), LOW),
        steps=((levels + 1, VECTORS, width), WIDE),
        vec_land=((levels, VECTORS, width), WIDE),
    )


def layer_kernel(sizes, names, *refs):
    x, lengths, mask, wq, wk, wv, wo, wu, wd, cotangent = refs[:10]
    vectors_in = refs[10:19]
    hid_out, dx_out, sums_out, own_sums_out, vec_out = refs[19:24]
    r = types.SimpleNamespace(**dict(zip(names, refs[24:-4], strict=True)), lengths=refs[-4])
    sems = refs[-3:-1]
    local = refs[-1]
    x_all, qkv, vec, steps = r.x_all, r.qkv, r.vec, r.steps
    seqs, rows, width = r.x_own.shape
    tokens = seqs * rows
    length = x_all.shape[1]
    blocks = sizes["blk"]
    own = width // blocks
    heads = own // HEAD
    hidden = r.w_up.shape[1]
    tiles = hidden // width
    scale = HEAD ** (-0.5)
    me = lax.axis_index("blk")
    near, far = flip(me, 1), flip(me, 2)
    cross = flip(far, 1)
    peers = (near, far, cross)
    place = lambda index: span(index * rows, rows, rows)
    lanes = lambda index: span(index * own, own, own)

    used = {"send": 0, "receive": 0, "local": 0}
    pending, stores = [], []

    def take(which, count):
        at = used[which]
        used[which] += count
        return at

    def slot(count):
        return take("send", count), take("receive", count)

    def send_in(pair, offset, src, dst, peer):
        return send(src, dst, sems, pair[0] + offset, {"blk": peer}, pair[1] + offset)

    def fetch(src, dst, at=None):
        copy = pltpu.make_async_copy(src, dst, local.at[take("local", 1) if at is None else at])
        copy.start()
        return copy

    unit_store, own_store = take("local", 1), take("local", 1)
    whole_stores = [
        pltpu.make_async_copy(r.out, sums_out, local.at[unit_store]),
        pltpu.make_async_copy(r.own_out, own_sums_out, local.at[own_store]),
    ]

    barrier = pltpu.get_barrier_semaphore()
    greeted = [peer for letter in "zx" for stage in stages_of(sizes)[letter] for _, peer in digit_of(stage)[1]]
    greeted += [{"blk": peer} for peer in peers]
    for peer in greeted:
        pl.semaphore_signal(barrier, inc=1, device_id=peer, device_id_type=MESH)

    load_mask = fetch(mask, r.mask)
    load_lengths = fetch(lengths, r.lengths)
    loads_x = [
        fetch(x, x_all.at[:, place(me), :]),
        fetch(x, r.x_own),
    ]
    loads_w = [
        fetch(weight.at[:, lanes(me)], r.w_qkv.at[:, pl.ds(at * own, own)])
        for at, weight in enumerate((wq, wk, wv))
    ]
    load_vectors = []
    at = 0
    for vector in vectors_in:
        count = vector.shape[0]
        load_vectors.append(fetch(vector, r.vec_low.at[pl.ds(at, count)]))
        at += count
    load_o = fetch(wo, r.w_o)
    load_up = fetch(wu, r.w_up)
    load_down = fetch(wd, r.w_down)
    load_cot = fetch(cotangent, r.cot)

    load_mask.wait()
    load_lengths.wait()
    positions = me * rows + lax.broadcasted_iota(jnp.int32, (1, rows), 1)
    flag_rows = []
    for seq in range(seqs):
        good = (r.mask[seq : seq + 1, :] == 1) & (positions < r.lengths[seq])
        flag_rows.append(jnp.where(good, 0.0, -1000000000.0).astype(WIDE))
    flag_rows.append(jnp.zeros((8 - seqs, rows), WIDE))
    r.flags[me] = jnp.concatenate(flag_rows, axis=0)

    pl.semaphore_wait(barrier, len(greeted))

    at_far, at_near, at_on, at_flag = slot(seqs), slot(seqs), slot(seqs), slot(len(peers))
    flag_copies = [
        send_in(at_flag, index, r.flags.at[me], r.flags.at[me], peer)
        for index, peer in enumerate(peers)
    ]
    for copy in loads_x:
        copy.wait()
    x_far, x_near, x_on = [], [], []
    for seq in range(seqs):
        target = x_all.at[seq, place(me), :]
        x_far.append(send_in(at_far, seq, r.x_own.at[seq], target, far))
        x_near.append(send_in(at_near, seq, r.x_own.at[seq], target, near))
    pending += flag_copies

    def forward_x(seq):
        x_far[seq].wait_recv()
        block = x_all.at[seq, place(far), :]
        x_on.append(send_in(at_on, seq, block, block, near))

    lane = lax.broadcasted_iota(jnp.int32, (1, own), 1)
    of_head = [(lane >= head * HEAD) & (lane < (head + 1) * HEAD) for head in range(heads)]
    only = lambda values, head: jnp.where(of_head[head], values.astype(WIDE), 0.0)
    for copy in load_vectors:
        copy.wait()
    for at in range(8 + tiles):
        vec[at : at + 1, :] = r.vec_low[at * width : (at + 1) * width].astype(WIDE).reshape(1, width)
    bias_q = vec[0:1, lanes(me)]
    bias_v = vec[1:2, lanes(me)]
    bias_qkv = jnp.concatenate([bias_q, jnp.zeros_like(bias_q), bias_v], axis=1)
    o_all, o_send = r.o_all, r.o_send
    at_o = slot(seqs * len(peers))
    o_copies = []

    def project(seq):
        qkv[seq] = (dot(x_all[seq], r.w_qkv[...]) + bias_qkv).astype(LOW)

    column = lax.broadcasted_iota(jnp.int32, (length, length), 1)
    row = lax.broadcasted_iota(jnp.int32, (length, length), 0)

    def attend(seq):
        keys = qkv[seq, :, own : 2 * own]
        values = qkv[seq, :, 2 * own :]
        key_bias = jnp.concatenate([r.flags[block, seq : seq + 1, :] for block in range(blocks)], axis=1)
        bias = jnp.where(column == row, 0.0, key_bias)
        query = qkv[seq, :, 0:own].astype(WIDE) * scale
        joined = None
        for head in range(heads):
            scores = dot_right_t(only(query, head).astype(LOW), keys) + bias
            raised = jnp.exp(scores - jnp.max(scores, axis=-1, keepdims=True))
            probs = (raised / jnp.sum(raised, axis=-1, keepdims=True)).astype(LOW)
            r.probs[seq * heads + head] = probs
            result = dot(probs, values)
            joined = result if joined is None else jnp.where(of_head[head], result, joined)
        r.o_wide[seq] = joined
        o_send[seq] = joined.astype(LOW)
        for index, peer in enumerate(peers):
            part = o_send.at[seq, place(peer), :]
            o_copies.append(send_in(at_o, seq * len(peers) + index, part, o_all.at[seq, :, lanes(me)], peer))
        o_all[seq, :, lanes(me)] = o_send[seq, place(me), :]

    for copy in loads_w:
        copy.wait()
    for copy in flag_copies:
        copy.wait_recv()
    forward_x(0)
    for seq in range(seqs):
        x_near[seq].wait_recv()
        x_on[seq].wait_recv()
        project(seq)
        if seq + 1 < seqs:
            forward_x(seq + 1)
        attend(seq)

    total, scaled, inverse = r.total, r.scaled, r.inverse
    normed, normed_low = r.normed, r.normed_low
    active, slope = r.active, r.slope
    grad_b, grad_y = r.grad_b, r.grad_y
    wide_row = lambda at: vec[at : at + 1, :]
    total_row = lambda values: jnp.sum(fold(values), axis=0, keepdims=True)
    flat = lambda ref: ref[...].reshape(tokens, width)
    steps[0] = jnp.zeros((VECTORS, width), WIDE)

    def normalize(values):
        center = values - mean_of(values)
        inv = lax.rsqrt(mean_of(center * center) + EPSILON)
        return center * inv, inv

    def feed_forward(first, count):
        some = slice(first, first + count)
        size = count * rows
        part = pl.ds(first * rows, size)
        mixed = o_all[some].reshape(size, width)
        made, inv = normalize(
            r.x_own[some].reshape(size, width).astype(WIDE) + dot(mixed, r.w_o[...]) + wide_row(2)
        )
        scaled[part, :] = made
        inverse[part, :] = jnp.broadcast_to(inv, (size, 128))
        result = made * wide_row(3) + wide_row(4)
        normed[part, :] = result
        normed_low[part, :] = result.astype(LOW)
        step = min(hidden, 2 * width * (2 * rows) // size)
        for at in range(0, hidden, step):
            columns = slice(at, at + step)
            offset = jnp.concatenate([wide_row(8 + tile) for tile in range(at // width, (at + step) // width)], axis=1)
            z = dot(normed_low[part, :], r.w_up[:, columns]) + offset
            below = 0.5 * (1.0 + lax.erf(z * 0.7071067811865476))
            active[part, columns] = (z * below).astype(LOW)
            slope[part, columns] = below + z * (0.3989422804014327 * jnp.exp(-0.5 * z * z))
        made, inv = normalize(normed[part, :] + dot(active[part, :], r.w_down[...]) + wide_row(5))
        r.hid[some] = (made * wide_row(6) + wide_row(7)).astype(LOW).reshape(count, rows, width)
        upstream = r.cot[some].reshape(size, width).astype(WIDE)
        back = norm_back(upstream, made, inv, wide_row(6))
        grad_b[part, :] = back
        rounded = back.astype(LOW)
        grad_y[part, :] = rounded
        steps[0, 7:8, :] += total_row(upstream)
        steps[0, 6:7, :] += total_row(upstream * made)
        steps[0, 5:6, :] += total_row(rounded.astype(WIDE))

    for copy in (load_o, load_up, load_down, load_cot):
        copy.wait()
    arrived = 0
    for first, count in ((0, seqs - 1), (seqs - 1, 1)) if seqs > 1 else ((0, 1),):
        for copy in o_copies[arrived : (first + count) * len(peers)]:
            copy.wait_recv()
        arrived = (first + count) * len(peers)
        feed_forward(first, count)
    stores.append(fetch(r.hid, hid_out))

    work = r.work
    running = {}
    last = []
    place_of = {"land": 0, "poll": 0}

    def launch(name, item):
        running[name] = item
        advance(name)

    def advance(name):
        if name in running and next(running[name], True) is not None:
            del running[name]

    def launch_unit(unit):
        letters = UNIT_ORDERS[unit]
        count = width // HALVES
        sending, receiving = semaphores_of(sizes, count, letters)
        ats = take("send", sending), take("receive", receiving)
        land_at = place_of["land"]
        place_of["land"] += landing_rows(sizes, count, letters)
        sent = []
        last.append(sent)

        def item():
            yield from reduce_rows(sizes, work, r.land, r.out, sems, unit * count, count, land_at, *ats, letters, sent)
            part = pl.ds(unit * count, count)
            fetch(r.out.at[part], sums_out.at[part], unit_store)

        launch(unit, item())

    def launch_units(tile):
        for half in range(HALVES):
            launch_unit(tile * HALVES + half)

    def launch_own(kind):
        letters = OWN_ORDERS[kind]
        sending, receiving = semaphores_of(sizes, width, letters)
        ats = take("send", max(sending, 3)), take("receive", receiving)
        blocks_at = take("receive", 3)
        slots = r.own_out.at[kind]
        sent = []
        last.append(sent)

        def item():
            parts = r.own_work.at[kind], r.own_land.at[kind], slots.at[me]
            yield from reduce_rows(sizes, *parts, sems, 0, width, 0, *ats, letters, sent)
            yield from share_blocks(slots, sems, ats[0], blocks_at, me, sent)
            fetch(slots, own_sums_out.at[kind], own_store)

        launch(len(UNIT_ORDERS) + kind, item())

    def poll():
        at = place_of["poll"]
        place_of["poll"] += 1
        for name in POLLS[at] if at < len(POLLS) else ():
            advance(name)

    cut = lambda tile: slice(tile * width, (tile + 1) * width)
    for tile in range(tiles):
        work[cut(tile), :] = dot_left_t(active[:, cut(tile)], grad_y[...]).astype(LOW)
        launch_units(tile)
        poll()

    grad_z = r.grad_z

    for tile in range(tiles):
        made = (dot_right_t(grad_y[...], r.w_down[cut(tile), :]) * slope[:, cut(tile)]).astype(LOW)
        grad_z[:, cut(tile)] = made
        steps[0, 8 + tile : 9 + tile, :] = total_row(made.astype(WIDE))
        poll()
    upstream = grad_b[...] + dot_right_t(grad_z[...], r.w_up[...])
    total[...] = upstream
    poll()
    upstream = total[...]

    grad_t = r.grad_t
    made = scaled[...]
    back = norm_back(upstream, made, inverse[:, 0:1], wide_row(3))
    grad_b[...] = back
    rounded = back.astype(LOW)
    grad_t[...] = rounded
    steps[0, 4:5, :] = total_row(upstream)
    steps[0, 3:4, :] = total_row(upstream * made)
    steps[0, 2:3, :] = total_row(rounded.astype(WIDE))
    poll()

    do_send, do_all = r.do_send, r.do_all
    for copy in x_far + x_near + x_on:
        copy.wait_send()
    at_do = at_far[0], take("receive", seqs * len(peers))
    do_copies = []
    made = dot_right_t(grad_t[...], r.w_o[...]).astype(LOW)
    do_send[...] = made.reshape(seqs, rows, width)
    for seq in range(seqs):
        do_copies.append(
            [
                send_in(
                    at_do,
                    seq * len(peers) + index,
                    do_send.at[seq, :, lanes(peer)],
                    do_all.at[seq, place(me), :],
                    peer,
                )
                for index, peer in enumerate(peers)
            ]
        )
        do_all[seq, place(me), :] = do_send[seq, :, lanes(me)]
        pending += do_copies[-1]

    poll()
    work[2 * hidden :, :] = dot_left_t(o_all[...].reshape(tokens, width), grad_t[...]).astype(LOW)
    launch_units(2 * tiles)
    poll()
    for tile in range(tiles):
        work[cut(tiles + tile), :] = dot_left_t(normed_low[...], grad_z[:, cut(tile)]).astype(LOW)
        launch_units(tiles + tile)
        poll()

    d_qkv, grad_s, dx_part = r.d_qkv, r.grad_s, r.dx_part
    for copy in o_copies:
        copy.wait_send()
    at_dx_near = at_o[0], take("receive", 2 * seqs)
    at_dx_far = at_o[0] + 2 * seqs, take("receive", seqs)
    dx_near, dx_far = [], []

    def value_back(seq):
        upstream = do_all[seq].astype(WIDE)
        grads = [
            dot_left_t(r.probs[seq * heads + head], only(upstream, head).astype(LOW)) for head in range(heads)
        ]
        d_qkv[seq, :, 2 * own :] = functools.reduce(jnp.add, grads).astype(LOW)

    def score_back(seq):
        values = qkv[seq, :, 2 * own :]
        upstream = do_all[seq].astype(WIDE)
        inner = upstream * r.o_wide[seq]
        for head in range(heads):
            delta = jnp.sum(only(inner, head), axis=-1, keepdims=True)
            prob_grad = dot_right_t(only(upstream, head).astype(LOW), values)
            probs = r.probs[seq * heads + head].astype(WIDE)
            grad_s[head] = (probs * (prob_grad - delta)).astype(LOW)

    def query_key_back(seq):
        queries_wide = qkv[seq, :, 0:own].astype(WIDE) * scale
        keys_wide = qkv[seq, :, own : 2 * own].astype(WIDE) * scale
        query_grads, key_grads = [], []
        for head in range(heads):
            query_grads.append(dot(grad_s[head], only(keys_wide, head).astype(LOW)))
            key_grads.append(dot_left_t(grad_s[head], only(queries_wide, head).astype(LOW)))
        d_qkv[seq, :, 0:own] = functools.reduce(jnp.add, query_grads).astype(LOW)
        d_qkv[seq, :, own : 2 * own] = functools.reduce(jnp.add, key_grads).astype(LOW)

    def input_back(seq):
        dx_part[seq] = dot_right_t(d_qkv[seq], r.w_qkv[...]).astype(LOW)
        dx_near.append(
            [
                send_in(at_dx_near, 2 * seq + at, dx_part.at[seq, place(block), :], r.dx_near.at[seq, at], near)
                for at, block in enumerate((near, cross))
            ]
        )
        pending.extend(dx_near[-1])

    def own_grad(columns):
        tokens_in = x_all[...].reshape(seqs * length, width)
        return dot_left_t(tokens_in, d_qkv[:, :, columns].reshape(seqs * length, -1)).astype(LOW)

    def hand_on(seq):
        dx_near[seq][1].wait_recv()
        summed = dx_part[seq, place(far), :].astype(WIDE) + r.dx_near[seq, 1].astype(WIDE)
        r.dx_chip[seq] = summed.astype(LOW)
        dx_far.append(send_in(at_dx_far, seq, r.dx_chip.at[seq], r.dx_far.at[seq], far))
        pending.append(dx_far[-1])

    for seq in range(seqs):
        poll()
        for copy in do_copies[seq]:
            copy.wait_recv()
        value_back(seq)
        poll()
    r.own_work[0] = own_grad(slice(2 * own, None))
    launch_own(0)
    poll()
    for seq in range(seqs):
        score_back(seq)
        poll()
        query_key_back(seq)
        poll()
    made = own_grad(slice(0, 2 * own))
    r.own_work[1] = made[:, :own]
    launch_own(1)
    r.own_work[2] = made[:, own:]
    launch_own(2)
    poll()
    for seq in range(seqs):
        input_back(seq)
        poll()
        if seq > 0:
            hand_on(seq - 1)
    hand_on(seqs - 1)

    sums = total_row(d_qkv[...].reshape(seqs * length, 3 * own).astype(WIDE))
    steps[0, 0:1, lanes(me)] = sums[:, 0:own]
    steps[0, 1:2, lanes(me)] = sums[:, 2 * own :]
    sum_bits = bits_of(sizes, SUM_ORDER)
    launch(len(UNIT_ORDERS) + 3, reduce_whole(steps, r.vec_land, sems, take("send", 1), take("receive", len(sum_bits)), sum_bits))
    poll()

    def finish_input():
        for seq in range(seqs):
            yield
            dx_near[seq][0].wait_recv()
            dx_far[seq].wait_recv()
            summed = grad_b[seq * rows : (seq + 1) * rows, :] + dx_part[seq, place(me), :].astype(WIDE)
            summed = summed + r.dx_near[seq, 0].astype(WIDE) + r.dx_far[seq].astype(WIDE)
            r.dx[seq] = summed.astype(LOW)
        stores.append(fetch(r.dx, dx_out))

    launch(len(UNIT_ORDERS) + 4, finish_input())
    for name in sum(POLLS[place_of["poll"] :], ()):
        advance(name)
    while running:
        for name in list(running):
            advance(name)
    stores.append(fetch(steps.at[len(sum_bits)], vec_out))
    for copy in sum(last, pending):
        copy.wait_send()
    for copy in stores + whole_stores:
        copy.wait()
    assert (used["send"], used["receive"]) == semaphore_counts(sizes, seqs, width) and used["local"] == local.shape[0]


def widen_kernel(blocks, hid, dx, sums, shared, vec, *refs):
    hid_out, dx_out, wq, wk, wv, wo, wu, wd = refs[:8]
    rows_out, bu = refs[8:16], refs[16]
    low, shared_low, wide, shared_wide, hid_low, dx_low, vec_in, flat_vec, sems = refs[17:]
    width = wq.shape[0]
    own = width // blocks
    units = sums.shape[0] // width
    tiles = (units - 1) // 2
    used = [0]

    def copy(src, dst):
        made = pltpu.make_async_copy(src, dst, sems.at[used[0]])
        used[0] += 1
        made.start()
        return made

    unit = lambda ref, at: ref.at[pl.ds(at * width, width)]
    load_vec = copy(vec, vec_in)
    shared_loads = [copy(shared.at[kind], shared_low.at[kind]) for kind in range(3)]
    loads = [copy(unit(sums, at), unit(low, at)) for at in range(units)]
    token_loads = [copy(hid, hid_low), copy(dx, dx_low)]
    stores = []
    for kind, target in enumerate((wv, wq, wk)):
        shared_loads[kind].wait()
        for block in range(blocks):
            shared_wide[kind, :, block * own : (block + 1) * own] = shared_low[kind, block].astype(WIDE)
        stores.append(copy(shared_wide.at[kind], target))
    targets = (
        [unit(wd, at) for at in range(tiles)] + [wu.at[:, pl.ds(at * width, width)] for at in range(tiles)] + [wo]
    )
    for at in range(units):
        loads[at].wait()
        part = slice(at * width, (at + 1) * width)
        wide[part, :] = low[part, :].astype(WIDE)
        stores.append(copy(unit(wide, at), targets[at]))
        if at == 0:
            load_vec.wait()
            count = len(rows_out)
            for index in range(count + tiles):
                flat_vec[index * width : (index + 1) * width] = vec_in[index, :]
            for index, row in enumerate(rows_out):
                stores.append(copy(flat_vec.at[pl.ds(index * width, width)], row))
            stores.append(copy(flat_vec.at[pl.ds(count * width, tiles * width)], bu))
        if at == units // 2:
            for load in token_loads:
                load.wait()
            stores += [copy(hid_low, hid_out), copy(dx_low, dx_out)]
    for made in stores:
        made.wait()


def on_device(
    sizes,
    hidden_input,
    lengths,
    key_mask,
    query_weight,
    query_offset,
    key_weight,
    value_weight,
    value_offset,
    output_weight,
    output_offset,
    mixer_gain,
    mixer_shift,
    up_weight,
    up_offset,
    down_weight,
    down_offset,
    final_gain,
    final_shift,
    cotangent,
):
    seqs, rows, width = hidden_input.shape
    hidden = up_weight.shape[1]
    blocks = sizes["blk"]
    own = width // blocks
    scratch = layout_of(sizes, seqs, rows, width, hidden)
    anywhere = pl.BlockSpec(memory_space=pl.ANY)
    scratch_shape = types.SimpleNamespace(**{name: shape for name, (shape, _) in scratch.items()})
    units = scratch_shape.work
    shared = (3, blocks, width, own)
    hid, dx, sums, own_sums, vec_sums = pl.pallas_call(
        functools.partial(layer_kernel, sizes, tuple(scratch)),
        out_shape=(
            jax.ShapeDtypeStruct(hidden_input.shape, LOW),
            jax.ShapeDtypeStruct(hidden_input.shape, LOW),
            jax.ShapeDtypeStruct(units, LOW),
            jax.ShapeDtypeStruct(shared, LOW),
            jax.ShapeDtypeStruct((VECTORS, width), WIDE),
        ),
        in_specs=[anywhere, anywhere] + [anywhere] * 17,
        out_specs=(anywhere,) * 5,
        scratch_shapes=[pltpu.VMEM(shape, kind) for shape, kind in scratch.values()]
        + [
            pltpu.SMEM((seqs,), jnp.int32),
            *(pltpu.SemaphoreType.DMA((count,)) for count in semaphore_counts(sizes, seqs, width)),
            pltpu.SemaphoreType.DMA((25,)),
        ],
        compiler_params=pltpu.CompilerParams(
            collective_id=0, has_side_effects=True, vmem_limit_bytes=60 * 1024 * 1024
        ),
    )(
        hidden_input,
        lengths,
        key_mask,
        query_weight,
        key_weight,
        value_weight,
        output_weight,
        up_weight,
        down_weight,
        cotangent,
        query_offset,
        value_offset,
        output_offset,
        mixer_gain,
        mixer_shift,
        down_offset,
        final_gain,
        final_shift,
        up_offset,
    )
    full = jax.ShapeDtypeStruct((width, width), WIDE)
    row = jax.ShapeDtypeStruct((width,), WIDE)
    flat = jax.ShapeDtypeStruct(hidden_input.shape, LOW)
    final = pl.pallas_call(
        functools.partial(widen_kernel, blocks),
        out_shape=(
            flat,
            flat,
            full,
            full,
            full,
            full,
            jax.ShapeDtypeStruct((width, hidden), WIDE),
            jax.ShapeDtypeStruct((hidden, width), WIDE),
        )
        + (row,) * 8
        + (jax.ShapeDtypeStruct((hidden,), WIDE),),
        in_specs=[anywhere] * 5,
        out_specs=(anywhere,) * 17,
        scratch_shapes=[
            pltpu.VMEM(units, LOW),
            pltpu.VMEM(shared, LOW),
            pltpu.VMEM(units, WIDE),
            pltpu.VMEM((3, width, width), WIDE),
            pltpu.VMEM(hidden_input.shape, LOW),
            pltpu.VMEM(hidden_input.shape, LOW),
            pltpu.VMEM((VECTORS, width), WIDE),
            pltpu.VMEM((VECTORS * width,), WIDE),
            pltpu.SemaphoreType.DMA((2 * units[0] // width + 20,)),
        ],
        compiler_params=pltpu.CompilerParams(vmem_limit_bytes=60 * 1024 * 1024),
    )(hid, dx, sums, own_sums, vec_sums)
    hid, dx, wq, wk, wv, wo, wu, wd, bq, bv, bo, g1, s1, bd, g2, s2, bu = final
    return hid, dx, wq, bq, wk, wv, bv, wo, bo, g1, s1, wu, bu, wd, bd, g2, s2


def solution(mesh):
    split = P("dp", "blk", None)
    in_specs = (split, P("dp"), P("dp", "blk")) + (P(),) * 15 + (split,)
    out_specs = (split, split) + (P(),) * 15
    return jax.shard_map(
        functools.partial(on_device, dict(mesh.shape)),
        mesh=mesh,
        in_specs=in_specs,
        out_specs=out_specs,
        check_vma=False,
    )
```

```python
import functools
import types

import jax
import jax.numpy as jnp
from jax import lax
from jax.experimental import pallas as pl
from jax.experimental.pallas import tpu as pltpu
from jax.sharding import PartitionSpec as P

HEAD = 64
EPSILON = 1e-06
MESH = pl.DeviceIdType.MESH
ROWS = 16
LOW = jnp.bfloat16
WIDE = jnp.float32
VECTORS = 16
HALVES = 2

UNIT_ORDERS = ("cyaxb", "cxyab", "caxyb", "cyxab", "caxyb", "cxyab", "cxaby", "cayxb", "cyaxb", "cxaby", "caxby", "cabxy", "cyxab", "cxyab", "cxayb", "cabxy", "cxyab", "cyaxb")
OWN_ORDERS = ("xab", "xab", "xab")
SUM_ORDER = "cxyab"
POLLS = (
    (),
    (),
    (),
    (),
    (0,),
    (1,),
    (2,),
    (3, 4,),
    (5, 6,),
    (7,),
    (),
    (),
    (),
    (),
    (),
    (0, 16,),
    (1, 17, 8, 2, 9, 10, 11, 3, 12, 5, 13, 14, 4, 15,),
    (6,),
    (7, 0,),
    (16,),
    (2, 10,),
    (),
    (1, 9,),
    (11,),
    (3,),
    (17,),
    (15,),
    (13,),
    (6, 8,),
    (1, 14, 9,),
    (12, 4,),
    (0, 5, 11, 3,),
    (18, 10, 7, 17, 16, 15, 2,),
    (19, 6, 13, 8, 4, 1, 14, 9,),
    (0, 5, 20, 3, 21, 12, 18, 11, 7, 10, 16, 17, 15, 2, 22, 8, 19, 0, 13, 4, 1, 21, 5, 20, 22, 3, 12, 18, 7, 16, 17, 22, 8, 6, 14, 3, 9, 0, 11, 19, 10, 5, 15, 7, 13, 2, 4, 17, 8, 1, 18, 20, 16, 21, 12, 11, 6, 15, 3, 19, 14, 2, 13, 9, 4, 0, 3, 17, 10, 5, 8, 1, 7, 0, 20, 16, 21, 14, 18, 1, 12, 13, 11, 19, 6, 17, 10, 15, 8, 5, 17, 2, 9, 20, 8, 5, 2, 4, 18, 16, 12, 7, 4, 18, 16, 21, 13, 14, 7, 19, 6, 13, 11, 19, 9, 6, 10, 11, 20, 9, 14, 15, 10, 12, 20, 14, 15, 12,),
)


def stages_of(sizes):
    def split(step, rest):
        found = []
        while rest > 1:
            radix = 4 if rest % 4 == 0 else 2
            found.append(("dp", step, radix))
            step *= radix
            rest //= radix
        return found

    dp = sizes["dp"]
    return dict(
        c=[("blk", 1, 2)], y=[("blk", 2, 2)], x=[("dp", 1, 2)], a=[("dp", 2, 2)], b=split(4, dp // 4), z=split(2, dp // 2)
    )


def bits_of(sizes, letters):
    bits = []
    for letter in letters:
        for axis, step, radix in stages_of(sizes)[letter]:
            bits += [(axis, step, 2)] if radix == 2 else [(axis, step, 2), (axis, 2 * step, 2)]
    return bits


def digit_of(stage):
    axis, step, radix = stage
    index = lax.axis_index(axis)
    digit = lax.rem(lax.div(index, step), radix)
    others = []
    for offset in range(1, radix):
        other = lax.rem(digit + offset, radix)
        others.append((other, {axis: index + (other - digit) * step}))
    return digit, others


def flip(index, step):
    return index + step - 2 * step * lax.rem(lax.div(index, step), 2)


def aligned(start, unit):
    return start if isinstance(start, int) else pl.multiple_of(start, unit)


def span(start, count, unit=ROWS):
    return pl.ds(aligned(start, unit), count)


def send(src, dst, sems, at, peer, land_at=None):
    sends, receives = sems
    copy = pltpu.make_async_remote_copy(
        src_ref=src,
        dst_ref=dst,
        send_sem=sends.at[at],
        recv_sem=receives.at[at if land_at is None else land_at],
        device_id=peer,
        device_id_type=MESH,
    )
    copy.start()
    return copy


def plan_of(sizes, rows, letters):
    stages = [stage for letter in letters for stage in stages_of(sizes)[letter]]
    plan = []
    size = rows
    for axis, step, radix in stages[:-1]:
        size = cut_stage(plan, axis, step, radix, size)
    axis, step, radix = stages[-1]
    if radix == 2:
        plan.append((stages[-1], False, size))
    else:
        cut_stage(plan, axis, step, radix, size)
    return plan


def cut_stage(plan, axis, step, radix, size):
    if size % (radix * ROWS) == 0:
        plan.append(((axis, step, radix), True, size // radix))
        return size // radix
    bit = step
    while bit < step * radix:
        split = size % (2 * ROWS) == 0
        size = size // 2 if split else size
        plan.append(((axis, bit, 2), split, size))
        bit *= 2
    return size


def landing_rows(sizes, rows, letters):
    return sum(size * (stage[2] - 1) for stage, _, size in plan_of(sizes, rows, letters))


def semaphores_of(sizes, rows, letters):
    plan = plan_of(sizes, rows, letters)
    return max(stage[2] - 1 for stage, _, _ in plan), sum((stage[2] - 1) * (1 + split) for stage, split, _ in plan)


def semaphore_counts(sizes, seqs, width):
    sends, receives = 3 + 6 * seqs + 1, 3 + 12 * seqs + len(bits_of(sizes, SUM_ORDER))
    for letters in UNIT_ORDERS:
        sending, receiving = semaphores_of(sizes, width // HALVES, letters)
        sends, receives = sends + sending, receives + receiving
    for letters in OWN_ORDERS:
        sending, receiving = semaphores_of(sizes, width, letters)
        sends, receives = sends + max(sending, 3), receives + receiving + 3
    return sends, receives


def add_rows(first, first_at, land, land_at, terms, out, out_at, count):
    total = first[span(first_at, count)].astype(WIDE)
    for term in range(terms):
        total = total + land[span(land_at + term * count, count)].astype(WIDE)
    out[span(out_at, count)] = total.astype(out.dtype)


def reduce_rows(sizes, work, land, out, sems, base, rows, land_at, send_at, receive_at, letters, sent):
    plan = plan_of(sizes, rows, letters)
    start = base
    trail = []
    for level, (stage, split, count) in enumerate(plan):
        digit, others = digit_of(stage)
        keep = start + digit * count if split else start
        for copy in sent:
            copy.wait_send()
        sent.clear()
        for offset, (other, peer) in enumerate(others):
            give = start + other * count if split else start
            slot = len(others) - 1 - offset
            sent.append(
                send(
                    work.at[span(give, count)],
                    land.at[span(land_at + slot * count, count)],
                    sems,
                    send_at + offset,
                    peer,
                    receive_at + slot,
                )
            )
        yield
        for copy in sent:
            copy.wait_recv()
        if split:
            trail.append((others, keep, count))
        else:
            for copy in sent:
                copy.wait_send()
            sent.clear()
        target = out if level == len(plan) - 1 else work
        add_rows(work, keep, land, land_at, len(others), target, keep, count)
        land_at += count * len(others)
        receive_at += len(others)
        start = keep
    for others, mine, count in reversed(trail):
        part = out.at[span(mine, count)]
        for copy in sent:
            copy.wait_send()
        sent.clear()
        for offset, (_, peer) in enumerate(others):
            sent.append(send(part, part, sems, send_at + offset, peer, receive_at + len(others) - 1 - offset))
        yield
        for copy in sent:
            copy.wait_recv()
        receive_at += len(others)


def reduce_whole(steps, land, sems, send_at, receive_at, bits):
    for level, bit in enumerate(bits):
        copy = send(steps.at[level], land.at[level], sems, send_at, digit_of(bit)[1][0][1], receive_at + level)
        yield
        copy.wait()
        steps[level + 1] = steps[level] + land[level]


def share_blocks(slots, sems, send_at, receive_at, me, sent):
    near, far = flip(me, 1), flip(me, 2)
    for copy in sent:
        copy.wait_send()
    across = send(slots.at[me], slots.at[me], sems, send_at, {"blk": far}, receive_at)
    beside = send(slots.at[me], slots.at[me], sems, send_at + 1, {"blk": near}, receive_at + 1)
    yield
    across.wait_recv()
    onward = send(slots.at[far], slots.at[far], sems, send_at + 2, {"blk": near}, receive_at + 2)
    yield
    beside.wait_recv()
    onward.wait_recv()
    sent[:] = [across, beside, onward]


def dot(left, right):
    return jnp.dot(left, right, preferred_element_type=WIDE)


def dot_right_t(left, right):
    return lax.dot_general(left, right, (((1,), (1,)), ((), ())), preferred_element_type=WIDE)


def dot_left_t(left, right):
    return lax.dot_general(left, right, (((0,), (0,)), ((), ())), preferred_element_type=WIDE)


def fold(values):
    rows, width = values.shape
    return jnp.sum(values.reshape(rows // 8, 8, width), axis=0)


def mean_of(values):
    return jnp.mean(values, axis=-1, keepdims=True)


def norm_back(upstream, scaled, inverse, gain):
    inner = upstream * gain
    return inverse * (inner - mean_of(inner) - scaled * mean_of(inner * scaled))


def layout_of(sizes, seqs, rows, width, hidden):
    tokens = seqs * rows
    blocks = sizes["blk"]
    length = rows * blocks
    own = width // blocks
    heads = own // HEAD
    levels = len(bits_of(sizes, SUM_ORDER))
    units = 2 * (hidden // width) + 1
    land_total = sum(landing_rows(sizes, width // HALVES, letters) for letters in UNIT_ORDERS)
    own_land = max(landing_rows(sizes, width, order) for order in OWN_ORDERS)
    return dict(
        x_all=((seqs, length, width), LOW),
        x_own=((seqs, rows, width), LOW),
        cot=((seqs, rows, width), LOW),
        w_qkv=((width, 3 * own), LOW),
        w_o=((width, width), LOW),
        w_up=((width, hidden), LOW),
        w_down=((hidden, width), LOW),
        vec_low=((VECTORS * width,), LOW),
        vec=((VECTORS, width), WIDE),
        flags=((blocks, 8, rows), WIDE),
        mask=((seqs, rows), jnp.int32),
        qkv=((seqs, length, 3 * own), LOW),
        probs=((seqs * heads, length, length), LOW),
        o_wide=((seqs, length, own), WIDE),
        o_send=((seqs, length, own), LOW),
        o_all=((seqs, rows, width), LOW),
        total=((tokens, width), WIDE),
        scaled=((tokens, width), WIDE),
        inverse=((tokens, 128), WIDE),
        normed=((tokens, width), WIDE),
        normed_low=((tokens, width), LOW),
        active=((tokens, hidden), LOW),
        slope=((tokens, hidden), WIDE),
        grad_b=((tokens, width), WIDE),
        grad_y=((tokens, width), LOW),
        grad_z=((tokens, hidden), LOW),
        grad_t=((tokens, width), LOW),
        do_send=((seqs, rows, width), LOW),
        do_all=((seqs, length, own), LOW),
        grad_s=((heads, length, length), LOW),
        d_qkv=((seqs, length, 3 * own), LOW),
        dx_part=((seqs, length, width), LOW),
        dx_near=((seqs, 2, rows, width), LOW),
        dx_chip=((seqs, rows, width), LOW),
        hid=((seqs, rows, width), LOW),
        dx=((seqs, rows, width), LOW),
        out=((units * width, width), LOW),
        own_out=((3, blocks, width, own), LOW),
        dx_far=((seqs, rows, width), LOW),
        work=((units * width, width), LOW),
        land=((land_total, width), LOW),
        own_work=((3, width, own), LOW),
        own_land=((3, own_land, own), LOW),
        steps=((levels + 1, VECTORS, width), WIDE),
        vec_land=((levels, VECTORS, width), WIDE),
    )


def layer_kernel(sizes, names, *refs):
    x, lengths, mask, wq, wk, wv, wo, wu, wd, cotangent = refs[:10]
    vectors_in = refs[10:19]
    hid_out, dx_out, sums_out, own_sums_out, vec_out = refs[19:24]
    r = types.SimpleNamespace(**dict(zip(names, refs[24:-4], strict=True)), lengths=refs[-4])
    sems = refs[-3:-1]
    local = refs[-1]
    x_all, qkv, vec, steps = r.x_all, r.qkv, r.vec, r.steps
    seqs, rows, width = r.x_own.shape
    tokens = seqs * rows
    length = x_all.shape[1]
    blocks = sizes["blk"]
    own = width // blocks
    heads = own // HEAD
    hidden = r.w_up.shape[1]
    tiles = hidden // width
    scale = HEAD ** (-0.5)
    me = lax.axis_index("blk")
    near, far = flip(me, 1), flip(me, 2)
    cross = flip(far, 1)
    peers = (near, far, cross)
    place = lambda index: span(index * rows, rows, rows)
    lanes = lambda index: span(index * own, own, own)

    used = {"send": 0, "receive": 0, "local": 0}
    pending, stores = [], []

    def take(which, count):
        at = used[which]
        used[which] += count
        return at

    def slot(count):
        return take("send", count), take("receive", count)

    def send_in(pair, offset, src, dst, peer):
        return send(src, dst, sems, pair[0] + offset, {"blk": peer}, pair[1] + offset)

    def fetch(src, dst, at=None):
        copy = pltpu.make_async_copy(src, dst, local.at[take("local", 1) if at is None else at])
        copy.start()
        return copy

    unit_store, own_store = take("local", 1), take("local", 1)
    whole_stores = [
        pltpu.make_async_copy(r.out, sums_out, local.at[unit_store]),
        pltpu.make_async_copy(r.own_out, own_sums_out, local.at[own_store]),
    ]

    barrier = pltpu.get_barrier_semaphore()
    far_letters = "z" if "z" in set("".join(UNIT_ORDERS + OWN_ORDERS)) else "ba"
    greeted = [
        peer for letter in far_letters + "x" for stage in stages_of(sizes)[letter] for _, peer in digit_of(stage)[1]
    ]
    greeted += [{"blk": peer} for peer in peers]
    for peer in greeted:
        pl.semaphore_signal(barrier, inc=1, device_id=peer, device_id_type=MESH)

    load_mask = fetch(mask, r.mask)
    load_lengths = fetch(lengths, r.lengths)
    loads_x = [
        fetch(x, x_all.at[:, place(me), :]),
        fetch(x, r.x_own),
    ]
    loads_w = [
        fetch(weight.at[:, lanes(me)], r.w_qkv.at[:, pl.ds(at * own, own)])
        for at, weight in enumerate((wq, wk, wv))
    ]
    load_vectors = []
    at = 0
    for vector in vectors_in:
        count = vector.shape[0]
        load_vectors.append(fetch(vector, r.vec_low.at[pl.ds(at, count)]))
        at += count
    load_o = fetch(wo, r.w_o)
    load_up = fetch(wu, r.w_up)
    load_down = fetch(wd, r.w_down)
    load_cot = fetch(cotangent, r.cot)

    load_mask.wait()
    load_lengths.wait()
    positions = me * rows + lax.broadcasted_iota(jnp.int32, (1, rows), 1)
    flag_rows = []
    for seq in range(seqs):
        good = (r.mask[seq : seq + 1, :] == 1) & (positions < r.lengths[seq])
        flag_rows.append(jnp.where(good, 0.0, -1000000000.0).astype(WIDE))
    flag_rows.append(jnp.zeros((8 - seqs, rows), WIDE))
    r.flags[me] = jnp.concatenate(flag_rows, axis=0)

    pl.semaphore_wait(barrier, len(greeted))

    at_far, at_near, at_on, at_flag = slot(seqs), slot(seqs), slot(seqs), slot(len(peers))
    flag_copies = [
        send_in(at_flag, index, r.flags.at[me], r.flags.at[me], peer)
        for index, peer in enumerate(peers)
    ]
    for copy in loads_x:
        copy.wait()
    x_far, x_near, x_on = [], [], []
    for seq in range(seqs):
        target = x_all.at[seq, place(me), :]
        x_far.append(send_in(at_far, seq, r.x_own.at[seq], target, far))
        x_near.append(send_in(at_near, seq, r.x_own.at[seq], target, near))
    pending += flag_copies

    def forward_x(seq):
        x_far[seq].wait_recv()
        block = x_all.at[seq, place(far), :]
        x_on.append(send_in(at_on, seq, block, block, near))

    lane = lax.broadcasted_iota(jnp.int32, (1, own), 1)
    of_head = [(lane >= head * HEAD) & (lane < (head + 1) * HEAD) for head in range(heads)]
    only = lambda values, head: jnp.where(of_head[head], values.astype(WIDE), 0.0)
    for copy in load_vectors:
        copy.wait()
    for at in range(8 + tiles):
        vec[at : at + 1, :] = r.vec_low[at * width : (at + 1) * width].astype(WIDE).reshape(1, width)
    bias_q = vec[0:1, lanes(me)]
    bias_v = vec[1:2, lanes(me)]
    bias_qkv = jnp.concatenate([bias_q, jnp.zeros_like(bias_q), bias_v], axis=1)
    o_all, o_send = r.o_all, r.o_send
    at_o = slot(seqs * len(peers))
    o_copies = []

    def project(seq):
        qkv[seq] = (dot(x_all[seq], r.w_qkv[...]) + bias_qkv).astype(LOW)

    def attend(seq, start, count, receivers):
        part = span(start, count, count)
        keys = qkv[seq, :, own : 2 * own]
        values = qkv[seq, :, 2 * own :]
        key_bias = jnp.concatenate([r.flags[block, seq : seq + 1, :] for block in range(blocks)], axis=1)
        column = lax.broadcasted_iota(jnp.int32, (count, length), 1)
        row = lax.broadcasted_iota(jnp.int32, (count, length), 0) + start
        bias = jnp.where(column == row, 0.0, key_bias)
        query = qkv[seq, part, 0:own].astype(WIDE) * scale
        joined = None
        for head in range(heads):
            scores = dot_right_t(only(query, head).astype(LOW), keys) + bias
            raised = jnp.exp(scores - jnp.max(scores, axis=-1, keepdims=True))
            probs = (raised / jnp.sum(raised, axis=-1, keepdims=True)).astype(LOW)
            r.probs[seq * heads + head, part, :] = probs
            result = dot(probs, values)
            joined = result if joined is None else jnp.where(of_head[head], result, joined)
        r.o_wide[seq, part, :] = joined
        o_send[seq, part, :] = joined.astype(LOW)
        for index in receivers:
            peer = peers[index]
            given = o_send.at[seq, place(peer), :]
            o_copies.append(send_in(at_o, seq * len(peers) + index, given, o_all.at[seq, :, lanes(me)], peer))

    for copy in loads_w:
        copy.wait()
    for copy in flag_copies:
        copy.wait_recv()
    forward_x(0)
    for seq in range(seqs):
        x_near[seq].wait_recv()
        x_on[seq].wait_recv()
        project(seq)
        if seq + 1 < seqs:
            forward_x(seq + 1)
        if seq + 1 < seqs:
            attend(seq, 0, length, (0, 1, 2))
        else:
            half = 2 * rows
            attend(seq, lax.div(far, 2) * half, half, (1, 2))
            attend(seq, lax.div(me, 2) * half, half, (0,))
        o_all[seq, :, lanes(me)] = o_send[seq, place(me), :]

    total, scaled, inverse = r.total, r.scaled, r.inverse
    normed, normed_low = r.normed, r.normed_low
    active, slope = r.active, r.slope
    grad_b, grad_y = r.grad_b, r.grad_y
    wide_row = lambda at: vec[at : at + 1, :]
    total_row = lambda values: jnp.sum(fold(values), axis=0, keepdims=True)
    flat = lambda ref: ref[...].reshape(tokens, width)
    steps[0] = jnp.zeros((VECTORS, width), WIDE)

    def normalize(values):
        center = values - mean_of(values)
        inv = lax.rsqrt(mean_of(center * center) + EPSILON)
        return center * inv, inv

    def feed_forward(first, count):
        some = slice(first, first + count)
        size = count * rows
        part = pl.ds(first * rows, size)
        mixed = o_all[some].reshape(size, width)
        made, inv = normalize(
            r.x_own[some].reshape(size, width).astype(WIDE) + dot(mixed, r.w_o[...]) + wide_row(2)
        )
        scaled[part, :] = made
        inverse[part, :] = jnp.broadcast_to(inv, (size, 128))
        result = made * wide_row(3) + wide_row(4)
        normed[part, :] = result
        normed_low[part, :] = result.astype(LOW)
        step = min(hidden, 2 * width * (2 * rows) // size)
        for at in range(0, hidden, step):
            columns = slice(at, at + step)
            offset = jnp.concatenate([wide_row(8 + tile) for tile in range(at // width, (at + step) // width)], axis=1)
            z = dot(normed_low[part, :], r.w_up[:, columns]) + offset
            below = 0.5 * (1.0 + lax.erf(z * 0.7071067811865476))
            active[part, columns] = (z * below).astype(LOW)
            slope[part, columns] = below + z * (0.3989422804014327 * jnp.exp(-0.5 * z * z))
        made, inv = normalize(normed[part, :] + dot(active[part, :], r.w_down[...]) + wide_row(5))
        r.hid[some] = (made * wide_row(6) + wide_row(7)).astype(LOW).reshape(count, rows, width)
        upstream = r.cot[some].reshape(size, width).astype(WIDE)
        back = norm_back(upstream, made, inv, wide_row(6))
        grad_b[part, :] = back
        rounded = back.astype(LOW)
        grad_y[part, :] = rounded
        steps[0, 7:8, :] += total_row(upstream)
        steps[0, 6:7, :] += total_row(upstream * made)
        steps[0, 5:6, :] += total_row(rounded.astype(WIDE))

    for copy in (load_o, load_up, load_down, load_cot):
        copy.wait()
    arrived = 0
    for first, count in ((0, seqs - 1), (seqs - 1, 1)) if seqs > 1 else ((0, 1),):
        for copy in o_copies[arrived : (first + count) * len(peers)]:
            copy.wait_recv()
        arrived = (first + count) * len(peers)
        feed_forward(first, count)
    stores.append(fetch(r.hid, hid_out))

    work = r.work
    running = {}
    last = []
    place_of = {"land": 0, "poll": 0}

    def launch(name, item):
        running[name] = item
        advance(name)

    def advance(name):
        if name in running and next(running[name], True) is not None:
            del running[name]

    def launch_unit(unit):
        letters = UNIT_ORDERS[unit]
        count = width // HALVES
        sending, receiving = semaphores_of(sizes, count, letters)
        ats = take("send", sending), take("receive", receiving)
        land_at = place_of["land"]
        place_of["land"] += landing_rows(sizes, count, letters)
        sent = []
        last.append(sent)

        def item():
            yield from reduce_rows(sizes, work, r.land, r.out, sems, unit * count, count, land_at, *ats, letters, sent)
            part = pl.ds(unit * count, count)
            fetch(r.out.at[part], sums_out.at[part], unit_store)

        launch(unit, item())

    def launch_units(tile):
        for half in range(HALVES):
            launch_unit(tile * HALVES + half)

    def launch_own(kind):
        letters = OWN_ORDERS[kind]
        sending, receiving = semaphores_of(sizes, width, letters)
        ats = take("send", max(sending, 3)), take("receive", receiving)
        blocks_at = take("receive", 3)
        slots = r.own_out.at[kind]
        sent = []
        last.append(sent)

        def item():
            parts = r.own_work.at[kind], r.own_land.at[kind], slots.at[me]
            yield from reduce_rows(sizes, *parts, sems, 0, width, 0, *ats, letters, sent)
            yield from share_blocks(slots, sems, ats[0], blocks_at, me, sent)
            fetch(slots, own_sums_out.at[kind], own_store)

        launch(len(UNIT_ORDERS) + kind, item())

    def poll():
        at = place_of["poll"]
        place_of["poll"] += 1
        for name in POLLS[at] if at < len(POLLS) else ():
            advance(name)

    cut = lambda tile: slice(tile * width, (tile + 1) * width)
    for tile in range(tiles):
        work[cut(tile), :] = dot_left_t(active[:, cut(tile)], grad_y[...]).astype(LOW)
        launch_units(tile)
        poll()

    grad_z = r.grad_z

    for tile in range(tiles):
        made = (dot_right_t(grad_y[...], r.w_down[cut(tile), :]) * slope[:, cut(tile)]).astype(LOW)
        grad_z[:, cut(tile)] = made
        steps[0, 8 + tile : 9 + tile, :] = total_row(made.astype(WIDE))
        poll()
    upstream = grad_b[...] + dot_right_t(grad_z[...], r.w_up[...])
    total[...] = upstream
    poll()
    upstream = total[...]

    grad_t = r.grad_t
    made = scaled[...]
    back = norm_back(upstream, made, inverse[:, 0:1], wide_row(3))
    grad_b[...] = back
    rounded = back.astype(LOW)
    grad_t[...] = rounded
    steps[0, 4:5, :] = total_row(upstream)
    steps[0, 3:4, :] = total_row(upstream * made)
    steps[0, 2:3, :] = total_row(rounded.astype(WIDE))
    poll()

    do_send, do_all = r.do_send, r.do_all
    for copy in x_far + x_near + x_on:
        copy.wait_send()
    at_do = at_far[0], take("receive", seqs * len(peers))
    do_copies = []
    made = dot_right_t(grad_t[...], r.w_o[...]).astype(LOW)
    do_send[...] = made.reshape(seqs, rows, width)
    for seq in range(seqs):
        do_copies.append(
            [
                send_in(
                    at_do,
                    seq * len(peers) + index,
                    do_send.at[seq, :, lanes(peer)],
                    do_all.at[seq, place(me), :],
                    peer,
                )
                for index, peer in enumerate(peers)
            ]
        )
        do_all[seq, place(me), :] = do_send[seq, :, lanes(me)]
        pending += do_copies[-1]

    poll()
    work[2 * hidden :, :] = dot_left_t(o_all[...].reshape(tokens, width), grad_t[...]).astype(LOW)
    launch_units(2 * tiles)
    poll()
    for tile in range(tiles):
        work[cut(tiles + tile), :] = dot_left_t(normed_low[...], grad_z[:, cut(tile)]).astype(LOW)
        launch_units(tiles + tile)
        poll()

    d_qkv, grad_s, dx_part = r.d_qkv, r.grad_s, r.dx_part
    for copy in o_copies:
        copy.wait_send()
    at_dx_near = at_o[0], take("receive", 2 * seqs)
    at_dx_far = at_o[0] + 2 * seqs, take("receive", seqs)
    dx_near, dx_far = [], []

    def value_back(seq):
        upstream = do_all[seq].astype(WIDE)
        grads = [
            dot_left_t(r.probs[seq * heads + head], only(upstream, head).astype(LOW)) for head in range(heads)
        ]
        d_qkv[seq, :, 2 * own :] = functools.reduce(jnp.add, grads).astype(LOW)

    def score_back(seq):
        values = qkv[seq, :, 2 * own :]
        upstream = do_all[seq].astype(WIDE)
        inner = upstream * r.o_wide[seq]
        for head in range(heads):
            delta = jnp.sum(only(inner, head), axis=-1, keepdims=True)
            prob_grad = dot_right_t(only(upstream, head).astype(LOW), values)
            probs = r.probs[seq * heads + head].astype(WIDE)
            grad_s[head] = (probs * (prob_grad - delta)).astype(LOW)

    def query_key_back(seq):
        queries_wide = qkv[seq, :, 0:own].astype(WIDE) * scale
        keys_wide = qkv[seq, :, own : 2 * own].astype(WIDE) * scale
        query_grads, key_grads = [], []
        for head in range(heads):
            query_grads.append(dot(grad_s[head], only(keys_wide, head).astype(LOW)))
            key_grads.append(dot_left_t(grad_s[head], only(queries_wide, head).astype(LOW)))
        d_qkv[seq, :, 0:own] = functools.reduce(jnp.add, query_grads).astype(LOW)
        d_qkv[seq, :, own : 2 * own] = functools.reduce(jnp.add, key_grads).astype(LOW)

    def input_back(seq):
        dx_part[seq] = dot_right_t(d_qkv[seq], r.w_qkv[...]).astype(LOW)
        dx_near.append(
            [
                send_in(at_dx_near, 2 * seq + at, dx_part.at[seq, place(block), :], r.dx_near.at[seq, at], near)
                for at, block in enumerate((near, cross))
            ]
        )
        pending.extend(dx_near[-1])

    def own_grad(columns):
        tokens_in = x_all[...].reshape(seqs * length, width)
        return dot_left_t(tokens_in, d_qkv[:, :, columns].reshape(seqs * length, -1)).astype(LOW)

    def hand_on(seq):
        dx_near[seq][1].wait_recv()
        summed = dx_part[seq, place(far), :].astype(WIDE) + r.dx_near[seq, 1].astype(WIDE)
        r.dx_chip[seq] = summed.astype(LOW)
        dx_far.append(send_in(at_dx_far, seq, r.dx_chip.at[seq], r.dx_far.at[seq], far))
        pending.append(dx_far[-1])

    for seq in range(seqs):
        poll()
        for copy in do_copies[seq]:
            copy.wait_recv()
        value_back(seq)
        poll()
    r.own_work[0] = own_grad(slice(2 * own, None))
    launch_own(0)
    poll()
    for seq in range(seqs):
        score_back(seq)
        poll()
        query_key_back(seq)
        poll()
    made = own_grad(slice(0, 2 * own))
    r.own_work[1] = made[:, :own]
    launch_own(1)
    r.own_work[2] = made[:, own:]
    launch_own(2)
    poll()
    for seq in range(seqs):
        input_back(seq)
        poll()
        if seq > 0:
            hand_on(seq - 1)
    hand_on(seqs - 1)

    sums = total_row(d_qkv[...].reshape(seqs * length, 3 * own).astype(WIDE))
    steps[0, 0:1, lanes(me)] = sums[:, 0:own]
    steps[0, 1:2, lanes(me)] = sums[:, 2 * own :]
    sum_bits = bits_of(sizes, SUM_ORDER)
    launch(len(UNIT_ORDERS) + 3, reduce_whole(steps, r.vec_land, sems, take("send", 1), take("receive", len(sum_bits)), sum_bits))
    poll()

    def finish_input():
        for seq in range(seqs):
            yield
            dx_near[seq][0].wait_recv()
            dx_far[seq].wait_recv()
            summed = grad_b[seq * rows : (seq + 1) * rows, :] + dx_part[seq, place(me), :].astype(WIDE)
            summed = summed + r.dx_near[seq, 0].astype(WIDE) + r.dx_far[seq].astype(WIDE)
            r.dx[seq] = summed.astype(LOW)
        stores.append(fetch(r.dx, dx_out))

    launch(len(UNIT_ORDERS) + 4, finish_input())
    for name in sum(POLLS[place_of["poll"] :], ()):
        advance(name)
    while running:
        for name in list(running):
            advance(name)
    stores.append(fetch(steps.at[len(sum_bits)], vec_out))
    for copy in sum(last, pending):
        copy.wait_send()
    for copy in stores + whole_stores:
        copy.wait()
    assert (used["send"], used["receive"]) == semaphore_counts(sizes, seqs, width) and used["local"] == local.shape[0]


def widen_kernel(blocks, hid, dx, sums, shared, vec, *refs):
    hid_out, dx_out, wq, wk, wv, wo, wu, wd = refs[:8]
    rows_out, bu = refs[8:16], refs[16]
    low, shared_low, wide, shared_wide, hid_low, dx_low, vec_in, flat_vec, sems = refs[17:]
    width = wq.shape[0]
    own = width // blocks
    units = sums.shape[0] // width
    tiles = (units - 1) // 2
    used = [0]

    def copy(src, dst):
        made = pltpu.make_async_copy(src, dst, sems.at[used[0]])
        used[0] += 1
        made.start()
        return made

    unit = lambda ref, at: ref.at[pl.ds(at * width, width)]
    load_vec = copy(vec, vec_in)
    shared_loads = [copy(shared.at[kind], shared_low.at[kind]) for kind in range(3)]
    loads = [copy(unit(sums, at), unit(low, at)) for at in range(units)]
    token_loads = [copy(hid, hid_low), copy(dx, dx_low)]
    stores = []
    for kind, target in enumerate((wv, wq, wk)):
        shared_loads[kind].wait()
        for block in range(blocks):
            shared_wide[kind, :, block * own : (block + 1) * own] = shared_low[kind, block].astype(WIDE)
        stores.append(copy(shared_wide.at[kind], target))
    targets = (
        [unit(wd, at) for at in range(tiles)] + [wu.at[:, pl.ds(at * width, width)] for at in range(tiles)] + [wo]
    )
    for at in range(units):
        loads[at].wait()
        part = slice(at * width, (at + 1) * width)
        wide[part, :] = low[part, :].astype(WIDE)
        stores.append(copy(unit(wide, at), targets[at]))
        if at == 0:
            load_vec.wait()
            count = len(rows_out)
            for index in range(count + tiles):
                flat_vec[index * width : (index + 1) * width] = vec_in[index, :]
            for index, row in enumerate(rows_out):
                stores.append(copy(flat_vec.at[pl.ds(index * width, width)], row))
            stores.append(copy(flat_vec.at[pl.ds(count * width, tiles * width)], bu))
        if at == units // 2:
            for load in token_loads:
                load.wait()
            stores += [copy(hid_low, hid_out), copy(dx_low, dx_out)]
    for made in stores:
        made.wait()


def on_device(
    sizes,
    hidden_input,
    lengths,
    key_mask,
    query_weight,
    query_offset,
    key_weight,
    value_weight,
    value_offset,
    output_weight,
    output_offset,
    mixer_gain,
    mixer_shift,
    up_weight,
    up_offset,
    down_weight,
    down_offset,
    final_gain,
    final_shift,
    cotangent,
):
    seqs, rows, width = hidden_input.shape
    hidden = up_weight.shape[1]
    blocks = sizes["blk"]
    own = width // blocks
    scratch = layout_of(sizes, seqs, rows, width, hidden)
    anywhere = pl.BlockSpec(memory_space=pl.ANY)
    scratch_shape = types.SimpleNamespace(**{name: shape for name, (shape, _) in scratch.items()})
    units = scratch_shape.work
    shared = (3, blocks, width, own)
    hid, dx, sums, own_sums, vec_sums = pl.pallas_call(
        functools.partial(layer_kernel, sizes, tuple(scratch)),
        out_shape=(
            jax.ShapeDtypeStruct(hidden_input.shape, LOW),
            jax.ShapeDtypeStruct(hidden_input.shape, LOW),
            jax.ShapeDtypeStruct(units, LOW),
            jax.ShapeDtypeStruct(shared, LOW),
            jax.ShapeDtypeStruct((VECTORS, width), WIDE),
        ),
        in_specs=[anywhere, anywhere] + [anywhere] * 17,
        out_specs=(anywhere,) * 5,
        scratch_shapes=[pltpu.VMEM(shape, kind) for shape, kind in scratch.values()]
        + [
            pltpu.SMEM((seqs,), jnp.int32),
            *(pltpu.SemaphoreType.DMA((count,)) for count in semaphore_counts(sizes, seqs, width)),
            pltpu.SemaphoreType.DMA((25,)),
        ],
        compiler_params=pltpu.CompilerParams(
            collective_id=0, has_side_effects=True, vmem_limit_bytes=60 * 1024 * 1024
        ),
    )(
        hidden_input,
        lengths,
        key_mask,
        query_weight,
        key_weight,
        value_weight,
        output_weight,
        up_weight,
        down_weight,
        cotangent,
        query_offset,
        value_offset,
        output_offset,
        mixer_gain,
        mixer_shift,
        down_offset,
        final_gain,
        final_shift,
        up_offset,
    )
    full = jax.ShapeDtypeStruct((width, width), WIDE)
    row = jax.ShapeDtypeStruct((width,), WIDE)
    flat = jax.ShapeDtypeStruct(hidden_input.shape, LOW)
    final = pl.pallas_call(
        functools.partial(widen_kernel, blocks),
        out_shape=(
            flat,
            flat,
            full,
            full,
            full,
            full,
            jax.ShapeDtypeStruct((width, hidden), WIDE),
            jax.ShapeDtypeStruct((hidden, width), WIDE),
        )
        + (row,) * 8
        + (jax.ShapeDtypeStruct((hidden,), WIDE),),
        in_specs=[anywhere] * 5,
        out_specs=(anywhere,) * 17,
        scratch_shapes=[
            pltpu.VMEM(units, LOW),
            pltpu.VMEM(shared, LOW),
            pltpu.VMEM(units, WIDE),
            pltpu.VMEM((3, width, width), WIDE),
            pltpu.VMEM(hidden_input.shape, LOW),
            pltpu.VMEM(hidden_input.shape, LOW),
            pltpu.VMEM((VECTORS, width), WIDE),
            pltpu.VMEM((VECTORS * width,), WIDE),
            pltpu.SemaphoreType.DMA((2 * units[0] // width + 20,)),
        ],
        compiler_params=pltpu.CompilerParams(vmem_limit_bytes=60 * 1024 * 1024),
    )(hid, dx, sums, own_sums, vec_sums)
    hid, dx, wq, wk, wv, wo, wu, wd, bq, bv, bo, g1, s1, bd, g2, s2, bu = final
    return hid, dx, wq, bq, wk, wv, bv, wo, bo, g1, s1, wu, bu, wd, bd, g2, s2


def solution(mesh):
    split = P("dp", "blk", None)
    in_specs = (split, P("dp"), P("dp", "blk")) + (P(),) * 15 + (split,)
    out_specs = (split, split) + (P(),) * 15
    return jax.shard_map(
        functools.partial(on_device, dict(mesh.shape)),
        mesh=mesh,
        in_specs=in_specs,
        out_specs=out_specs,
        check_vma=False,
    )
```

```python
import functools
import types

import jax
import jax.numpy as jnp
from jax import lax
from jax.experimental import pallas as pl
from jax.experimental.pallas import tpu as pltpu
from jax.sharding import PartitionSpec as P

HEAD = 64
EPSILON = 1e-06
MESH = pl.DeviceIdType.MESH
ROWS = 16
LOW = jnp.bfloat16
WIDE = jnp.float32
VECTORS = 16
HALVES = 2

UNIT_ORDERS = ("caxyb", "cxzy", "cyxab", "cyxab", "cxyab", "cayxb", "cabyx", "cxaby", "cxyab", "cabxy", "cxaby", "cabxy", "cxayb", "cxyab", "caxyb", "cyxab", "cxyab", "cyaxb")
OWN_ORDERS = ("xab", "xab", "xab")
SUM_ORDER = "cxyab"
POLLS = (
    (),
    (),
    (),
    (),
    (0,),
    (1,),
    (2,),
    (3, 4,),
    (5, 6, 7,),
    (),
    (),
    (),
    (),
    (),
    (),
    (0, 16,),
    (1, 17, 8, 2, 9, 10, 11, 12, 5, 4, 13, 14, 3, 15, 6, 7,),
    (0,),
    (),
    (1, 16,),
    (9,),
    (8,),
    (11,),
    (2,),
    (17,),
    (5, 14,),
    (10, 4,),
    (6,),
    (7, 12,),
    (15, 0, 9, 1,),
    (13, 2, 11, 16,),
    (3, 17, 8,),
    (18, 6, 10, 4, 5,),
    (19, 7, 12, 14, 0, 13,),
    (16, 1, 3, 8, 2, 21, 20, 18, 15, 9, 10, 11, 22, 4, 17, 5, 6, 19, 13, 16, 1, 3, 2, 21, 8, 22, 20, 1, 5, 15, 18, 4, 17, 22, 2, 7, 16, 19, 12, 3, 14, 8, 13, 0, 9, 10, 11, 17, 20, 6, 18, 15, 21, 19, 5, 7, 3, 4, 12, 0, 13, 9, 14, 11, 17, 2, 10, 20, 16, 18, 2, 8, 15, 6, 19, 21, 3, 12, 4, 5, 13, 3, 14, 7, 4, 20, 5, 17, 0, 16, 17, 9, 0, 16, 11, 8, 10, 18, 15, 8, 6, 18, 13, 21, 14, 6, 12, 19, 13, 7, 9, 19, 7, 10, 11, 9, 20, 10, 12, 14, 11, 20, 15, 12, 14, 15,),
)


def stages_of(sizes):
    def split(step, rest):
        found = []
        while rest > 1:
            radix = 4 if rest % 4 == 0 else 2
            found.append(("dp", step, radix))
            step *= radix
            rest //= radix
        return found

    dp = sizes["dp"]
    return dict(
        c=[("blk", 1, 2)], y=[("blk", 2, 2)], x=[("dp", 1, 2)], a=[("dp", 2, 2)], b=split(4, dp // 4), z=split(2, dp // 2)
    )


def bits_of(sizes, letters):
    bits = []
    for letter in letters:
        for axis, step, radix in stages_of(sizes)[letter]:
            bits += [(axis, step, 2)] if radix == 2 else [(axis, step, 2), (axis, 2 * step, 2)]
    return bits


def digit_of(stage):
    axis, step, radix = stage
    index = lax.axis_index(axis)
    digit = lax.rem(lax.div(index, step), radix)
    others = []
    for offset in range(1, radix):
        other = lax.rem(digit + offset, radix)
        others.append((other, {axis: index + (other - digit) * step}))
    return digit, others


def flip(index, step):
    return index + step - 2 * step * lax.rem(lax.div(index, step), 2)


def aligned(start, unit):
    return start if isinstance(start, int) else pl.multiple_of(start, unit)


def span(start, count, unit=ROWS):
    return pl.ds(aligned(start, unit), count)


def send(src, dst, sems, at, peer, land_at=None):
    sends, receives = sems
    copy = pltpu.make_async_remote_copy(
        src_ref=src,
        dst_ref=dst,
        send_sem=sends.at[at],
        recv_sem=receives.at[at if land_at is None else land_at],
        device_id=peer,
        device_id_type=MESH,
    )
    copy.start()
    return copy


def plan_of(sizes, rows, letters):
    stages = [stage for letter in letters for stage in stages_of(sizes)[letter]]
    plan = []
    size = rows
    for axis, step, radix in stages[:-1]:
        size = cut_stage(plan, axis, step, radix, size)
    axis, step, radix = stages[-1]
    if radix == 2:
        plan.append((stages[-1], False, size))
    else:
        cut_stage(plan, axis, step, radix, size)
    return plan


def cut_stage(plan, axis, step, radix, size):
    if size % (radix * ROWS) == 0:
        plan.append(((axis, step, radix), True, size // radix))
        return size // radix
    bit = step
    while bit < step * radix:
        split = size % (2 * ROWS) == 0
        size = size // 2 if split else size
        plan.append(((axis, bit, 2), split, size))
        bit *= 2
    return size


def landing_rows(sizes, rows, letters):
    return sum(size * (stage[2] - 1) for stage, _, size in plan_of(sizes, rows, letters))


def semaphores_of(sizes, rows, letters):
    plan = plan_of(sizes, rows, letters)
    return max(stage[2] - 1 for stage, _, _ in plan), sum((stage[2] - 1) * (1 + split) for stage, split, _ in plan)


def semaphore_counts(sizes, seqs, width):
    sends, receives = 3 + 6 * seqs + 1, 3 + 12 * seqs + len(bits_of(sizes, SUM_ORDER))
    for letters in UNIT_ORDERS:
        sending, receiving = semaphores_of(sizes, width // HALVES, letters)
        sends, receives = sends + sending, receives + receiving
    for letters in OWN_ORDERS:
        sending, receiving = semaphores_of(sizes, width, letters)
        sends, receives = sends + max(sending, 3), receives + receiving + 3
    return sends, receives


def add_rows(first, first_at, land, land_at, terms, out, out_at, count):
    total = first[span(first_at, count)].astype(WIDE)
    for term in range(terms):
        total = total + land[span(land_at + term * count, count)].astype(WIDE)
    out[span(out_at, count)] = total.astype(out.dtype)


def reduce_rows(sizes, work, land, out, sems, base, rows, land_at, send_at, receive_at, letters, sent):
    plan = plan_of(sizes, rows, letters)
    start = base
    trail = []
    for level, (stage, split, count) in enumerate(plan):
        digit, others = digit_of(stage)
        keep = start + digit * count if split else start
        for copy in sent:
            copy.wait_send()
        sent.clear()
        for offset, (other, peer) in enumerate(others):
            give = start + other * count if split else start
            slot = len(others) - 1 - offset
            sent.append(
                send(
                    work.at[span(give, count)],
                    land.at[span(land_at + slot * count, count)],
                    sems,
                    send_at + offset,
                    peer,
                    receive_at + slot,
                )
            )
        yield
        for copy in sent:
            copy.wait_recv()
        if split:
            trail.append((others, keep, count))
        else:
            for copy in sent:
                copy.wait_send()
            sent.clear()
        target = out if level == len(plan) - 1 else work
        add_rows(work, keep, land, land_at, len(others), target, keep, count)
        land_at += count * len(others)
        receive_at += len(others)
        start = keep
    for others, mine, count in reversed(trail):
        part = out.at[span(mine, count)]
        for copy in sent:
            copy.wait_send()
        sent.clear()
        for offset, (_, peer) in enumerate(others):
            sent.append(send(part, part, sems, send_at + offset, peer, receive_at + len(others) - 1 - offset))
        yield
        for copy in sent:
            copy.wait_recv()
        receive_at += len(others)


def reduce_whole(steps, land, sems, send_at, receive_at, bits):
    for level, bit in enumerate(bits):
        copy = send(steps.at[level], land.at[level], sems, send_at, digit_of(bit)[1][0][1], receive_at + level)
        yield
        copy.wait()
        steps[level + 1] = steps[level] + land[level]


def share_blocks(slots, sems, send_at, receive_at, me, sent):
    near, far = flip(me, 1), flip(me, 2)
    for copy in sent:
        copy.wait_send()
    across = send(slots.at[me], slots.at[me], sems, send_at, {"blk": far}, receive_at)
    beside = send(slots.at[me], slots.at[me], sems, send_at + 1, {"blk": near}, receive_at + 1)
    yield
    across.wait_recv()
    onward = send(slots.at[far], slots.at[far], sems, send_at + 2, {"blk": near}, receive_at + 2)
    yield
    beside.wait_recv()
    onward.wait_recv()
    sent[:] = [across, beside, onward]


def dot(left, right):
    return jnp.dot(left, right, preferred_element_type=WIDE)


def dot_right_t(left, right):
    return lax.dot_general(left, right, (((1,), (1,)), ((), ())), preferred_element_type=WIDE)


def dot_left_t(left, right):
    return lax.dot_general(left, right, (((0,), (0,)), ((), ())), preferred_element_type=WIDE)


def fold(values):
    rows, width = values.shape
    return jnp.sum(values.reshape(rows // 8, 8, width), axis=0)


def mean_of(values):
    return jnp.mean(values, axis=-1, keepdims=True)


def norm_back(upstream, scaled, inverse, gain):
    inner = upstream * gain
    return inverse * (inner - mean_of(inner) - scaled * mean_of(inner * scaled))


def layout_of(sizes, seqs, rows, width, hidden):
    tokens = seqs * rows
    blocks = sizes["blk"]
    length = rows * blocks
    own = width // blocks
    heads = own // HEAD
    levels = len(bits_of(sizes, SUM_ORDER))
    units = 2 * (hidden // width) + 1
    land_total = sum(landing_rows(sizes, width // HALVES, letters) for letters in UNIT_ORDERS)
    own_land = max(landing_rows(sizes, width, order) for order in OWN_ORDERS)
    return dict(
        x_all=((seqs, length, width), LOW),
        x_own=((seqs, rows, width), LOW),
        cot=((seqs, rows, width), LOW),
        w_qkv=((width, 3 * own), LOW),
        w_o=((width, width), LOW),
        w_up=((width, hidden), LOW),
        w_down=((hidden, width), LOW),
        vec_low=((VECTORS * width,), LOW),
        vec=((VECTORS, width), WIDE),
        flags=((blocks, 8, rows), WIDE),
        mask=((seqs, rows), jnp.int32),
        qkv=((seqs, length, 3 * own), LOW),
        probs=((seqs * heads, length, length), LOW),
        o_wide=((seqs, length, own), WIDE),
        o_send=((seqs, length, own), LOW),
        o_all=((seqs, rows, width), LOW),
        total=((tokens, width), WIDE),
        scaled=((tokens, width), WIDE),
        inverse=((tokens, 128), WIDE),
        normed=((tokens, width), WIDE),
        normed_low=((tokens, width), LOW),
        active=((tokens, hidden), LOW),
        slope=((tokens, hidden), WIDE),
        grad_b=((tokens, width), WIDE),
        grad_y=((tokens, width), LOW),
        grad_z=((tokens, hidden), LOW),
        grad_t=((tokens, width), LOW),
        do_send=((seqs, rows, width), LOW),
        do_all=((seqs, length, own), LOW),
        grad_s=((heads, length, length), LOW),
        d_qkv=((seqs, length, 3 * own), LOW),
        dx_part=((seqs, length, width), LOW),
        dx_near=((seqs, 2, rows, width), LOW),
        dx_chip=((seqs, rows, width), LOW),
        hid=((seqs, rows, width), LOW),
        dx=((seqs, rows, width), LOW),
        out=((units * width, width), LOW),
        own_out=((3, blocks, width, own), LOW),
        dx_far=((seqs, rows, width), LOW),
        work=((units * width, width), LOW),
        land=((land_total, width), LOW),
        own_work=((3, width, own), LOW),
        own_land=((3, own_land, own), LOW),
        steps=((levels + 1, VECTORS, width), WIDE),
        vec_land=((levels, VECTORS, width), WIDE),
    )


def layer_kernel(sizes, names, *refs):
    x, lengths, mask, wq, wk, wv, wo, wu, wd, cotangent = refs[:10]
    vectors_in = refs[10:19]
    hid_out, dx_out, sums_out, own_sums_out, vec_out = refs[19:24]
    r = types.SimpleNamespace(**dict(zip(names, refs[24:-4], strict=True)), lengths=refs[-4])
    sems = refs[-3:-1]
    local = refs[-1]
    x_all, qkv, vec, steps = r.x_all, r.qkv, r.vec, r.steps
    seqs, rows, width = r.x_own.shape
    tokens = seqs * rows
    length = x_all.shape[1]
    blocks = sizes["blk"]
    own = width // blocks
    heads = own // HEAD
    hidden = r.w_up.shape[1]
    tiles = hidden // width
    scale = HEAD ** (-0.5)
    me = lax.axis_index("blk")
    near, far = flip(me, 1), flip(me, 2)
    cross = flip(far, 1)
    peers = (near, far, cross)
    place = lambda index: span(index * rows, rows, rows)
    lanes = lambda index: span(index * own, own, own)

    used = {"send": 0, "receive": 0, "local": 0}
    pending, stores = [], []

    def take(which, count):
        at = used[which]
        used[which] += count
        return at

    def slot(count):
        return take("send", count), take("receive", count)

    def send_in(pair, offset, src, dst, peer):
        return send(src, dst, sems, pair[0] + offset, {"blk": peer}, pair[1] + offset)

    def fetch(src, dst, at=None):
        copy = pltpu.make_async_copy(src, dst, local.at[take("local", 1) if at is None else at])
        copy.start()
        return copy

    unit_store, own_store = take("local", 1), take("local", 1)
    whole_stores = [
        pltpu.make_async_copy(r.out, sums_out, local.at[unit_store]),
        pltpu.make_async_copy(r.own_out, own_sums_out, local.at[own_store]),
    ]

    barrier = pltpu.get_barrier_semaphore()
    greeted = [peer for letter in "zx" for stage in stages_of(sizes)[letter] for _, peer in digit_of(stage)[1]]
    greeted += [{"blk": peer} for peer in peers]
    for peer in greeted:
        pl.semaphore_signal(barrier, inc=1, device_id=peer, device_id_type=MESH)

    load_mask = fetch(mask, r.mask)
    load_lengths = fetch(lengths, r.lengths)
    loads_x = [
        fetch(x, x_all.at[:, place(me), :]),
        fetch(x, r.x_own),
    ]
    loads_w = [
        fetch(weight.at[:, lanes(me)], r.w_qkv.at[:, pl.ds(at * own, own)])
        for at, weight in enumerate((wq, wk, wv))
    ]
    load_vectors = []
    at = 0
    for vector in vectors_in:
        count = vector.shape[0]
        load_vectors.append(fetch(vector, r.vec_low.at[pl.ds(at, count)]))
        at += count
    load_o = fetch(wo, r.w_o)
    load_up = fetch(wu, r.w_up)
    load_down = fetch(wd, r.w_down)
    load_cot = fetch(cotangent, r.cot)

    load_mask.wait()
    load_lengths.wait()
    positions = me * rows + lax.broadcasted_iota(jnp.int32, (1, rows), 1)
    flag_rows = []
    for seq in range(seqs):
        good = (r.mask[seq : seq + 1, :] == 1) & (positions < r.lengths[seq])
        flag_rows.append(jnp.where(good, 0.0, -1000000000.0).astype(WIDE))
    flag_rows.append(jnp.zeros((8 - seqs, rows), WIDE))
    r.flags[me] = jnp.concatenate(flag_rows, axis=0)

    pl.semaphore_wait(barrier, len(greeted))

    at_far, at_near, at_on, at_flag = slot(seqs), slot(seqs), slot(seqs), slot(len(peers))
    flag_copies = [
        send_in(at_flag, index, r.flags.at[me], r.flags.at[me], peer)
        for index, peer in enumerate(peers)
    ]
    for copy in loads_x:
        copy.wait()
    x_far, x_near, x_on = [], [], []
    for seq in range(seqs):
        target = x_all.at[seq, place(me), :]
        x_far.append(send_in(at_far, seq, r.x_own.at[seq], target, far))
        x_near.append(send_in(at_near, seq, r.x_own.at[seq], target, near))
    pending += flag_copies

    def forward_x(seq):
        x_far[seq].wait_recv()
        block = x_all.at[seq, place(far), :]
        x_on.append(send_in(at_on, seq, block, block, near))

    lane = lax.broadcasted_iota(jnp.int32, (1, own), 1)
    of_head = [(lane >= head * HEAD) & (lane < (head + 1) * HEAD) for head in range(heads)]
    only = lambda values, head: jnp.where(of_head[head], values.astype(WIDE), 0.0)
    for copy in load_vectors:
        copy.wait()
    for at in range(8 + tiles):
        vec[at : at + 1, :] = r.vec_low[at * width : (at + 1) * width].astype(WIDE).reshape(1, width)
    bias_q = vec[0:1, lanes(me)]
    bias_v = vec[1:2, lanes(me)]
    bias_qkv = jnp.concatenate([bias_q, jnp.zeros_like(bias_q), bias_v], axis=1)
    o_all, o_send = r.o_all, r.o_send
    at_o = slot(seqs * len(peers))
    o_copies = []

    def project(seq):
        qkv[seq] = (dot(x_all[seq], r.w_qkv[...]) + bias_qkv).astype(LOW)

    def attend(seq, start, count, receivers):
        part = span(start, count, count)
        keys = qkv[seq, :, own : 2 * own]
        values = qkv[seq, :, 2 * own :]
        key_bias = jnp.concatenate([r.flags[block, seq : seq + 1, :] for block in range(blocks)], axis=1)
        column = lax.broadcasted_iota(jnp.int32, (count, length), 1)
        row = lax.broadcasted_iota(jnp.int32, (count, length), 0) + start
        bias = jnp.where(column == row, 0.0, key_bias)
        query = qkv[seq, part, 0:own].astype(WIDE) * scale
        joined = None
        for head in range(heads):
            scores = dot_right_t(only(query, head).astype(LOW), keys) + bias
            raised = jnp.exp(scores - jnp.max(scores, axis=-1, keepdims=True))
            probs = (raised / jnp.sum(raised, axis=-1, keepdims=True)).astype(LOW)
            r.probs[seq * heads + head, part, :] = probs
            result = dot(probs, values)
            joined = result if joined is None else jnp.where(of_head[head], result, joined)
        r.o_wide[seq, part, :] = joined
        o_send[seq, part, :] = joined.astype(LOW)
        for index in receivers:
            peer = peers[index]
            given = o_send.at[seq, place(peer), :]
            o_copies.append(send_in(at_o, seq * len(peers) + index, given, o_all.at[seq, :, lanes(me)], peer))

    for copy in loads_w:
        copy.wait()
    for copy in flag_copies:
        copy.wait_recv()
    forward_x(0)
    for seq in range(seqs):
        x_near[seq].wait_recv()
        x_on[seq].wait_recv()
        project(seq)
        if seq + 1 < seqs:
            forward_x(seq + 1)
        if seq + 1 < seqs:
            attend(seq, 0, length, (0, 1, 2))
        else:
            half = 2 * rows
            attend(seq, lax.div(far, 2) * half, half, (1, 2))
            attend(seq, lax.div(me, 2) * half, half, (0,))
        o_all[seq, :, lanes(me)] = o_send[seq, place(me), :]

    total, scaled, inverse = r.total, r.scaled, r.inverse
    normed, normed_low = r.normed, r.normed_low
    active, slope = r.active, r.slope
    grad_b, grad_y = r.grad_b, r.grad_y
    wide_row = lambda at: vec[at : at + 1, :]
    total_row = lambda values: jnp.sum(fold(values), axis=0, keepdims=True)
    flat = lambda ref: ref[...].reshape(tokens, width)
    steps[0] = jnp.zeros((VECTORS, width), WIDE)

    def normalize(values):
        center = values - mean_of(values)
        inv = lax.rsqrt(mean_of(center * center) + EPSILON)
        return center * inv, inv

    def feed_forward(first, count):
        some = slice(first, first + count)
        size = count * rows
        part = pl.ds(first * rows, size)
        mixed = o_all[some].reshape(size, width)
        made, inv = normalize(
            r.x_own[some].reshape(size, width).astype(WIDE) + dot(mixed, r.w_o[...]) + wide_row(2)
        )
        scaled[part, :] = made
        inverse[part, :] = jnp.broadcast_to(inv, (size, 128))
        result = made * wide_row(3) + wide_row(4)
        normed[part, :] = result
        normed_low[part, :] = result.astype(LOW)
        step = min(hidden, 2 * width * (2 * rows) // size)
        for at in range(0, hidden, step):
            columns = slice(at, at + step)
            offset = jnp.concatenate([wide_row(8 + tile) for tile in range(at // width, (at + step) // width)], axis=1)
            z = dot(normed_low[part, :], r.w_up[:, columns]) + offset
            below = 0.5 * (1.0 + lax.erf(z * 0.7071067811865476))
            active[part, columns] = (z * below).astype(LOW)
            slope[part, columns] = below + z * (0.3989422804014327 * jnp.exp(-0.5 * z * z))
        made, inv = normalize(normed[part, :] + dot(active[part, :], r.w_down[...]) + wide_row(5))
        r.hid[some] = (made * wide_row(6) + wide_row(7)).astype(LOW).reshape(count, rows, width)
        upstream = r.cot[some].reshape(size, width).astype(WIDE)
        back = norm_back(upstream, made, inv, wide_row(6))
        grad_b[part, :] = back
        rounded = back.astype(LOW)
        grad_y[part, :] = rounded
        steps[0, 7:8, :] += total_row(upstream)
        steps[0, 6:7, :] += total_row(upstream * made)
        steps[0, 5:6, :] += total_row(rounded.astype(WIDE))

    for copy in (load_o, load_up, load_down, load_cot):
        copy.wait()
    arrived = 0
    for first, count in ((0, seqs - 1), (seqs - 1, 1)) if seqs > 1 else ((0, 1),):
        for copy in o_copies[arrived : (first + count) * len(peers)]:
            copy.wait_recv()
        arrived = (first + count) * len(peers)
        feed_forward(first, count)
    stores.append(fetch(r.hid, hid_out))

    work = r.work
    running = {}
    last = []
    place_of = {"land": 0, "poll": 0}

    def launch(name, item):
        running[name] = item
        advance(name)

    def advance(name):
        if name in running and next(running[name], True) is not None:
            del running[name]

    def launch_unit(unit):
        letters = UNIT_ORDERS[unit]
        count = width // HALVES
        sending, receiving = semaphores_of(sizes, count, letters)
        ats = take("send", sending), take("receive", receiving)
        land_at = place_of["land"]
        place_of["land"] += landing_rows(sizes, count, letters)
        sent = []
        last.append(sent)

        def item():
            yield from reduce_rows(sizes, work, r.land, r.out, sems, unit * count, count, land_at, *ats, letters, sent)
            part = pl.ds(unit * count, count)
            fetch(r.out.at[part], sums_out.at[part], unit_store)

        launch(unit, item())

    def launch_units(tile):
        for half in range(HALVES):
            launch_unit(tile * HALVES + half)

    def launch_own(kind):
        letters = OWN_ORDERS[kind]
        sending, receiving = semaphores_of(sizes, width, letters)
        ats = take("send", max(sending, 3)), take("receive", receiving)
        blocks_at = take("receive", 3)
        slots = r.own_out.at[kind]
        sent = []
        last.append(sent)

        def item():
            parts = r.own_work.at[kind], r.own_land.at[kind], slots.at[me]
            yield from reduce_rows(sizes, *parts, sems, 0, width, 0, *ats, letters, sent)
            yield from share_blocks(slots, sems, ats[0], blocks_at, me, sent)
            fetch(slots, own_sums_out.at[kind], own_store)

        launch(len(UNIT_ORDERS) + kind, item())

    def poll():
        at = place_of["poll"]
        place_of["poll"] += 1
        for name in POLLS[at] if at < len(POLLS) else ():
            advance(name)

    cut = lambda tile: slice(tile * width, (tile + 1) * width)
    for tile in range(tiles):
        work[cut(tile), :] = dot_left_t(active[:, cut(tile)], grad_y[...]).astype(LOW)
        launch_units(tile)
        poll()

    grad_z = r.grad_z

    for tile in range(tiles):
        made = (dot_right_t(grad_y[...], r.w_down[cut(tile), :]) * slope[:, cut(tile)]).astype(LOW)
        grad_z[:, cut(tile)] = made
        steps[0, 8 + tile : 9 + tile, :] = total_row(made.astype(WIDE))
        poll()
    upstream = grad_b[...] + dot_right_t(grad_z[...], r.w_up[...])
    total[...] = upstream
    poll()
    upstream = total[...]

    grad_t = r.grad_t
    made = scaled[...]
    back = norm_back(upstream, made, inverse[:, 0:1], wide_row(3))
    grad_b[...] = back
    rounded = back.astype(LOW)
    grad_t[...] = rounded
    steps[0, 4:5, :] = total_row(upstream)
    steps[0, 3:4, :] = total_row(upstream * made)
    steps[0, 2:3, :] = total_row(rounded.astype(WIDE))
    poll()

    do_send, do_all = r.do_send, r.do_all
    for copy in x_far + x_near + x_on:
        copy.wait_send()
    at_do = at_far[0], take("receive", seqs * len(peers))
    do_copies = []
    made = dot_right_t(grad_t[...], r.w_o[...]).astype(LOW)
    do_send[...] = made.reshape(seqs, rows, width)
    for seq in range(seqs):
        do_copies.append(
            [
                send_in(
                    at_do,
                    seq * len(peers) + index,
                    do_send.at[seq, :, lanes(peer)],
                    do_all.at[seq, place(me), :],
                    peer,
                )
                for index, peer in enumerate(peers)
            ]
        )
        do_all[seq, place(me), :] = do_send[seq, :, lanes(me)]
        pending += do_copies[-1]

    poll()
    work[2 * hidden :, :] = dot_left_t(o_all[...].reshape(tokens, width), grad_t[...]).astype(LOW)
    launch_units(2 * tiles)
    poll()
    for tile in range(tiles):
        work[cut(tiles + tile), :] = dot_left_t(normed_low[...], grad_z[:, cut(tile)]).astype(LOW)
        launch_units(tiles + tile)
        poll()

    d_qkv, grad_s, dx_part = r.d_qkv, r.grad_s, r.dx_part
    for copy in o_copies:
        copy.wait_send()
    at_dx_near = at_o[0], take("receive", 2 * seqs)
    at_dx_far = at_o[0] + 2 * seqs, take("receive", seqs)
    dx_near, dx_far = [], []

    def value_back(seq):
        upstream = do_all[seq].astype(WIDE)
        grads = [
            dot_left_t(r.probs[seq * heads + head], only(upstream, head).astype(LOW)) for head in range(heads)
        ]
        d_qkv[seq, :, 2 * own :] = functools.reduce(jnp.add, grads).astype(LOW)

    def score_back(seq):
        values = qkv[seq, :, 2 * own :]
        upstream = do_all[seq].astype(WIDE)
        inner = upstream * r.o_wide[seq]
        for head in range(heads):
            delta = jnp.sum(only(inner, head), axis=-1, keepdims=True)
            prob_grad = dot_right_t(only(upstream, head).astype(LOW), values)
            probs = r.probs[seq * heads + head].astype(WIDE)
            grad_s[head] = (probs * (prob_grad - delta)).astype(LOW)

    def query_key_back(seq):
        queries_wide = qkv[seq, :, 0:own].astype(WIDE) * scale
        keys_wide = qkv[seq, :, own : 2 * own].astype(WIDE) * scale
        query_grads, key_grads = [], []
        for head in range(heads):
            query_grads.append(dot(grad_s[head], only(keys_wide, head).astype(LOW)))
            key_grads.append(dot_left_t(grad_s[head], only(queries_wide, head).astype(LOW)))
        d_qkv[seq, :, 0:own] = functools.reduce(jnp.add, query_grads).astype(LOW)
        d_qkv[seq, :, own : 2 * own] = functools.reduce(jnp.add, key_grads).astype(LOW)

    def input_back(seq):
        dx_part[seq] = dot_right_t(d_qkv[seq], r.w_qkv[...]).astype(LOW)
        dx_near.append(
            [
                send_in(at_dx_near, 2 * seq + at, dx_part.at[seq, place(block), :], r.dx_near.at[seq, at], near)
                for at, block in enumerate((near, cross))
            ]
        )
        pending.extend(dx_near[-1])

    def own_grad(columns):
        tokens_in = x_all[...].reshape(seqs * length, width)
        return dot_left_t(tokens_in, d_qkv[:, :, columns].reshape(seqs * length, -1)).astype(LOW)

    def hand_on(seq):
        dx_near[seq][1].wait_recv()
        summed = dx_part[seq, place(far), :].astype(WIDE) + r.dx_near[seq, 1].astype(WIDE)
        r.dx_chip[seq] = summed.astype(LOW)
        dx_far.append(send_in(at_dx_far, seq, r.dx_chip.at[seq], r.dx_far.at[seq], far))
        pending.append(dx_far[-1])

    for seq in range(seqs):
        poll()
        for copy in do_copies[seq]:
            copy.wait_recv()
        value_back(seq)
        poll()
    r.own_work[0] = own_grad(slice(2 * own, None))
    launch_own(0)
    poll()
    for seq in range(seqs):
        score_back(seq)
        poll()
        query_key_back(seq)
        poll()
    made = own_grad(slice(0, 2 * own))
    r.own_work[1] = made[:, :own]
    launch_own(1)
    r.own_work[2] = made[:, own:]
    launch_own(2)
    poll()
    for seq in range(seqs):
        input_back(seq)
        poll()
        if seq > 0:
            hand_on(seq - 1)
    hand_on(seqs - 1)

    sums = total_row(d_qkv[...].reshape(seqs * length, 3 * own).astype(WIDE))
    steps[0, 0:1, lanes(me)] = sums[:, 0:own]
    steps[0, 1:2, lanes(me)] = sums[:, 2 * own :]
    sum_bits = bits_of(sizes, SUM_ORDER)
    launch(len(UNIT_ORDERS) + 3, reduce_whole(steps, r.vec_land, sems, take("send", 1), take("receive", len(sum_bits)), sum_bits))
    poll()

    def finish_input():
        for seq in range(seqs):
            yield
            dx_near[seq][0].wait_recv()
            dx_far[seq].wait_recv()
            summed = grad_b[seq * rows : (seq + 1) * rows, :] + dx_part[seq, place(me), :].astype(WIDE)
            summed = summed + r.dx_near[seq, 0].astype(WIDE) + r.dx_far[seq].astype(WIDE)
            r.dx[seq] = summed.astype(LOW)
        stores.append(fetch(r.dx, dx_out))

    launch(len(UNIT_ORDERS) + 4, finish_input())
    for name in sum(POLLS[place_of["poll"] :], ()):
        advance(name)
    while running:
        for name in list(running):
            advance(name)
    stores.append(fetch(steps.at[len(sum_bits)], vec_out))
    for copy in sum(last, pending):
        copy.wait_send()
    for copy in stores + whole_stores:
        copy.wait()
    assert (used["send"], used["receive"]) == semaphore_counts(sizes, seqs, width) and used["local"] == local.shape[0]


def widen_kernel(blocks, hid, dx, sums, shared, vec, *refs):
    hid_out, dx_out, wq, wk, wv, wo, wu, wd = refs[:8]
    rows_out, bu = refs[8:16], refs[16]
    low, shared_low, wide, shared_wide, hid_low, dx_low, vec_in, flat_vec, sems = refs[17:]
    width = wq.shape[0]
    own = width // blocks
    units = sums.shape[0] // width
    tiles = (units - 1) // 2
    used = [0]

    def copy(src, dst):
        made = pltpu.make_async_copy(src, dst, sems.at[used[0]])
        used[0] += 1
        made.start()
        return made

    unit = lambda ref, at: ref.at[pl.ds(at * width, width)]
    load_vec = copy(vec, vec_in)
    shared_loads = [copy(shared.at[kind], shared_low.at[kind]) for kind in range(3)]
    loads = [copy(unit(sums, at), unit(low, at)) for at in range(units)]
    token_loads = [copy(hid, hid_low), copy(dx, dx_low)]
    stores = []
    for kind, target in enumerate((wv, wq, wk)):
        shared_loads[kind].wait()
        for block in range(blocks):
            shared_wide[kind, :, block * own : (block + 1) * own] = shared_low[kind, block].astype(WIDE)
        stores.append(copy(shared_wide.at[kind], target))
    targets = (
        [unit(wd, at) for at in range(tiles)] + [wu.at[:, pl.ds(at * width, width)] for at in range(tiles)] + [wo]
    )
    for at in range(units):
        loads[at].wait()
        part = slice(at * width, (at + 1) * width)
        wide[part, :] = low[part, :].astype(WIDE)
        stores.append(copy(unit(wide, at), targets[at]))
        if at == 0:
            load_vec.wait()
            count = len(rows_out)
            for index in range(count + tiles):
                flat_vec[index * width : (index + 1) * width] = vec_in[index, :]
            for index, row in enumerate(rows_out):
                stores.append(copy(flat_vec.at[pl.ds(index * width, width)], row))
            stores.append(copy(flat_vec.at[pl.ds(count * width, tiles * width)], bu))
        if at == units // 2:
            for load in token_loads:
                load.wait()
            stores += [copy(hid_low, hid_out), copy(dx_low, dx_out)]
    for made in stores:
        made.wait()


def on_device(
    sizes,
    hidden_input,
    lengths,
    key_mask,
    query_weight,
    query_offset,
    key_weight,
    value_weight,
    value_offset,
    output_weight,
    output_offset,
    mixer_gain,
    mixer_shift,
    up_weight,
    up_offset,
    down_weight,
    down_offset,
    final_gain,
    final_shift,
    cotangent,
):
    seqs, rows, width = hidden_input.shape
    hidden = up_weight.shape[1]
    blocks = sizes["blk"]
    own = width // blocks
    scratch = layout_of(sizes, seqs, rows, width, hidden)
    anywhere = pl.BlockSpec(memory_space=pl.ANY)
    scratch_shape = types.SimpleNamespace(**{name: shape for name, (shape, _) in scratch.items()})
    units = scratch_shape.work
    shared = (3, blocks, width, own)
    hid, dx, sums, own_sums, vec_sums = pl.pallas_call(
        functools.partial(layer_kernel, sizes, tuple(scratch)),
        out_shape=(
            jax.ShapeDtypeStruct(hidden_input.shape, LOW),
            jax.ShapeDtypeStruct(hidden_input.shape, LOW),
            jax.ShapeDtypeStruct(units, LOW),
            jax.ShapeDtypeStruct(shared, LOW),
            jax.ShapeDtypeStruct((VECTORS, width), WIDE),
        ),
        in_specs=[anywhere, anywhere] + [anywhere] * 17,
        out_specs=(anywhere,) * 5,
        scratch_shapes=[pltpu.VMEM(shape, kind) for shape, kind in scratch.values()]
        + [
            pltpu.SMEM((seqs,), jnp.int32),
            *(pltpu.SemaphoreType.DMA((count,)) for count in semaphore_counts(sizes, seqs, width)),
            pltpu.SemaphoreType.DMA((25,)),
        ],
        compiler_params=pltpu.CompilerParams(
            collective_id=0, has_side_effects=True, vmem_limit_bytes=60 * 1024 * 1024
        ),
    )(
        hidden_input,
        lengths,
        key_mask,
        query_weight,
        key_weight,
        value_weight,
        output_weight,
        up_weight,
        down_weight,
        cotangent,
        query_offset,
        value_offset,
        output_offset,
        mixer_gain,
        mixer_shift,
        down_offset,
        final_gain,
        final_shift,
        up_offset,
    )
    full = jax.ShapeDtypeStruct((width, width), WIDE)
    row = jax.ShapeDtypeStruct((width,), WIDE)
    flat = jax.ShapeDtypeStruct(hidden_input.shape, LOW)
    final = pl.pallas_call(
        functools.partial(widen_kernel, blocks),
        out_shape=(
            flat,
            flat,
            full,
            full,
            full,
            full,
            jax.ShapeDtypeStruct((width, hidden), WIDE),
            jax.ShapeDtypeStruct((hidden, width), WIDE),
        )
        + (row,) * 8
        + (jax.ShapeDtypeStruct((hidden,), WIDE),),
        in_specs=[anywhere] * 5,
        out_specs=(anywhere,) * 17,
        scratch_shapes=[
            pltpu.VMEM(units, LOW),
            pltpu.VMEM(shared, LOW),
            pltpu.VMEM(units, WIDE),
            pltpu.VMEM((3, width, width), WIDE),
            pltpu.VMEM(hidden_input.shape, LOW),
            pltpu.VMEM(hidden_input.shape, LOW),
            pltpu.VMEM((VECTORS, width), WIDE),
            pltpu.VMEM((VECTORS * width,), WIDE),
            pltpu.SemaphoreType.DMA((2 * units[0] // width + 20,)),
        ],
        compiler_params=pltpu.CompilerParams(vmem_limit_bytes=60 * 1024 * 1024),
    )(hid, dx, sums, own_sums, vec_sums)
    hid, dx, wq, wk, wv, wo, wu, wd, bq, bv, bo, g1, s1, bd, g2, s2, bu = final
    return hid, dx, wq, bq, wk, wv, bv, wo, bo, g1, s1, wu, bu, wd, bd, g2, s2


def solution(mesh):
    split = P("dp", "blk", None)
    in_specs = (split, P("dp"), P("dp", "blk")) + (P(),) * 15 + (split,)
    out_specs = (split, split) + (P(),) * 15
    return jax.shard_map(
        functools.partial(on_device, dict(mesh.shape)),
        mesh=mesh,
        in_specs=in_specs,
        out_specs=out_specs,
        check_vma=False,
    )
```
